128 devices in a mesh: fsdp: 4 (over z), seq: 8 (over x_hi, y), mp: 4 (over x_lo, core).
Axes of the slice: x: 4 (x_hi: 2, x_lo: 2; x = x_hi * 2 + x_lo), y: 4, z: 4, core: 2. Of those that a mesh axis runs over, the one named last changes fastest.
Arguments:
- inputs: float32 [16384, 2048], P(('fsdp', 'seq', 'mp')), may hold values from -6 to 6
- cotangent: float32 [16384, 2048], P(('fsdp', 'seq', 'mp')), may hold values from -24 to 24
- attn_weight: float32 [1, 128, 64, 2048], P(None, ('fsdp', 'seq', 'mp')), may hold values from -1 to 1
- expand_weight: float32 [1, 8192, 2048], P(None, ('fsdp', 'seq', 'mp')), may hold values from -0.125 to 0.125
- contract_weight: float32 [1, 8192, 2048], P(None, ('fsdp', 'seq', 'mp')), may hold values from -0.0625 to 0.0625
- norm_params: float32 [1, 2, 2048], P(None, None, ('fsdp', 'seq', 'mp')), may hold values from -0.3 to 1.3
- attn_moment: float32 [1, 128, 64, 2048], P(None, ('fsdp', 'seq', 'mp')), may hold values from -224 to 224
- expand_moment: float32 [1, 8192, 2048], P(None, ('fsdp', 'seq', 'mp')), may hold values from -224 to 224
- contract_moment: float32 [1, 8192, 2048], P(None, ('fsdp', 'seq', 'mp')), may hold values from -224 to 224
- norm_first: float32 [1, 2, 2048], P(None, None, ('fsdp', 'seq', 'mp')), may hold values from -80 to 80
- norm_second: float32 [1, 2, 2048], P(None, None, ('fsdp', 'seq', 'mp')), may hold values from 819.2 to 3276.8
Outputs:
- block_output: float32 [16384, 2048], P(('fsdp', 'seq', 'mp'))
- input_grad: float32 [16384, 2048], P(('fsdp', 'seq', 'mp'))
- attn_grad: float32 [1, 128, 64, 2048], P(None, ('fsdp', 'seq', 'mp'))
- attn_moment_next: float32 [1, 128, 64, 2048], P(None, ('fsdp', 'seq', 'mp'))
- attn_next: float32 [1, 128, 64, 2048], P(None, ('fsdp', 'seq', 'mp'))
- expand_grad: float32 [1, 8192, 2048], P(None, ('fsdp', 'seq', 'mp'))
- expand_moment_next: float32 [1, 8192, 2048], P(None, ('fsdp', 'seq', 'mp'))
- expand_next: float32 [1, 8192, 2048], P(None, ('fsdp', 'seq', 'mp'))
- contract_grad: float32 [1, 8192, 2048], P(None, ('fsdp', 'seq', 'mp'))
- contract_moment_next: float32 [1, 8192, 2048], P(None, ('fsdp', 'seq', 'mp'))
- contract_next: float32 [1, 8192, 2048], P(None, ('fsdp', 'seq', 'mp'))
- norm_grad: float32 [1, 2, 2048], P(None, None, ('fsdp', 'seq', 'mp'))
- norm_first_next: float32 [1, 2, 2048], P(None, None, ('fsdp', 'seq', 'mp'))
- norm_second_next: float32 [1, 2, 2048], P(None, None, ('fsdp', 'seq', 'mp'))
- norm_next: float32 [1, 2, 2048], P(None, None, ('fsdp', 'seq', 'mp'))
The draws below stay inside these ranges and needn't reach their ends.
All inputs are finite; a program needn't handle non-finite values.
Results may differ from the reference program's by a relative error of at most 0.023.
Values may be sent and summed in bfloat16 or wider, within the bound.
A program may use at most 192 MiB of HBM per device.

```python
import math
import jax
import jax.numpy as jnp
from jax import lax

D = 2048
H = 32
HD = 64
FF = 8192
ROT = 32
LENGTH = 2048
TOKENS = 16384
QB = 512
LAYERS = 1
NS_STEPS = 5
STEP = 10


def draw_attn_weight(key, part):
    key = jax.random.fold_in(key, 11)
    base = jnp.clip(jax.random.normal(key, (LAYERS, 4, H, HD, D), jnp.float32), -4.0, 4.0)
    kind_scale = jnp.array([1.0, 1.0, 1.0, LENGTH ** 0.5 / 4.0], jnp.float32)
    scaled = base * kind_scale[None, :, None, None, None] * D ** (-0.5)
    return scaled.reshape(LAYERS, 4 * H, HD, D)


def draw_norm_params(key, part):
    key = jax.random.fold_in(key, 23)
    first_key, second_key = jax.random.split(key)
    gains = jax.random.uniform(first_key, (LAYERS, 1, D), jnp.float32, 0.7, 1.3)
    biases = jax.random.uniform(second_key, (LAYERS, 1, D), jnp.float32, -0.3, 0.3)
    return jnp.concatenate([gains, biases], axis=1)


def spiked(drawn, key, source, target, parts, factor):
    def block_of(position):
        return (jnp.arange(drawn.shape[position]) // (drawn.shape[position] // parts)).reshape((-1,) + (1,) * (drawn.ndim - 1 - position))

    one_side = jax.random.permutation(key, parts)[block_of(target)]
    other_side = (block_of(target) + parts // 2) % parts
    return jnp.where((block_of(source) == one_side) | (block_of(source) == other_side), factor * drawn, drawn)


def levels(rng, dims, cuts, smallest, high):
    def one(dim, parts):
        steps = jax.random.uniform(jax.random.fold_in(jax.random.fold_in(rng, 6), dim), (parts,), jnp.float32, smallest / len(cuts), high / len(cuts))
        return jnp.repeat(jnp.exp(steps), dims[dim] // parts).reshape((-1,) + (1,) * (len(dims) - dim - 1))

    level = one(*cuts[0])
    for cut in cuts[1:]:
        level = level * one(*cut)
    return level


def centred(key, shape, deviation, most, shards=(), held_as=jnp.bfloat16):
    values = deviation * jax.random.normal(key, shape, jnp.float32)
    if shards:
        values = values * levels(key, shape, shards, -0.22, 0.18)
    return jnp.clip(values, -most, most).astype(held_as)


def bell_draw_with(key, dims, scale, reach, cuts, heavy, kind=jnp.bfloat16):
    drawn = scale * jax.random.normal(key, dims, jnp.float32)
    if cuts:
        drawn = drawn * levels(key, dims, cuts, -0.22, 0.18)
    return jnp.clip(spiked(drawn, jax.random.fold_in(key, 3), *heavy), -reach, reach).astype(kind)


def setup_inputs(seed: int = 0) -> dict:
    key_of = jax.random.split(jax.random.key(seed), 12)
    inputs = centred(key_of[0], (TOKENS, D), 1.0, 6.0, ((0, 128),), jnp.float32)
    cotangent = bell_draw_with(key_of[1], (TOKENS, D), 1.0, 24.0, ((0, 128),), (0, 1, 128, 5.5), jnp.float32)
    attn_weight = draw_attn_weight(jax.random.fold_in(key_of[11], 71), 0)
    expand_weight = centred(key_of[3], (LAYERS, FF, D), D ** -0.5, 0.125, ((1, 128),), jnp.float32)
    contract_weight = centred(key_of[4], (LAYERS, FF, D), FF ** -0.5, 0.0625, ((1, 128),), jnp.float32)
    norm_params = draw_norm_params(jax.random.fold_in(key_of[11], 71), 0)
    attn_moment = centred(key_of[6], (LAYERS, 4 * H, HD, D), (0.3 * TOKENS ** 0.5), 224.0, ((1, 128),), jnp.float32)
    expand_moment = centred(key_of[7], (LAYERS, FF, D), (0.3 * TOKENS ** 0.5), 224.0, ((1, 128),), jnp.float32)
    contract_moment = centred(key_of[8], (LAYERS, FF, D), (0.3 * TOKENS ** 0.5), 224.0, ((1, 128),), jnp.float32)
    norm_first = centred(key_of[9], (LAYERS, 2, D), (0.11 * TOKENS ** 0.5), 80.0, ((2, 128),), jnp.float32)
    norm_second = jnp.clip(jnp.exp(math.log(3276.8) - 1.3862944 * jax.random.uniform(key_of[10], (LAYERS, 2, D), jnp.float32) ** levels(key_of[10], (LAYERS, 2, D), ((2, 128),), -0.2, 0.2)), 819.2, 3276.8)
    return {"inputs": inputs, "cotangent": cotangent, "attn_weight": attn_weight, "expand_weight": expand_weight, "contract_weight": contract_weight, "norm_params": norm_params, "attn_moment": attn_moment, "expand_moment": expand_moment, "contract_moment": contract_moment, "norm_first": norm_first, "norm_second": norm_second}


eps_norm = 1e-05
rope_base = 10000.0
muon_beta = 0.95
muon_rate = 0.15
muon_decay = 0.01
polish_a = 3.4445
polish_b = -4.775
polish_c = 2.0315
adam_first = 0.9
adam_second = 0.95
adam_rate = 0.5
adam_eps = 1e-08
masked_score = -1e+30
highest = lax.Precision.HIGHEST

@jax.custom_vjp
def low(v):
    return lax.optimization_barrier(v.astype(jnp.bfloat16)).astype(jnp.float32)

@jax.custom_vjp
def low_back(v):
    return v

def low_keep(v):
    return (low(v), None)

def low_pass(kept, grad):
    return (grad,)

def back_keep(v):
    return (v, None)

def back_low(kept, grad):
    return (low(grad),)
low.defvjp(low_keep, low_pass)
low_back.defvjp(back_keep, back_low)

def angles(positions, half):
    freq = rope_base ** (-2.0 * jnp.arange(half, dtype=jnp.float32) / (2 * half))
    turned = positions[:, None] * freq[None, :]
    return (jnp.cos(turned)[:, None, :], jnp.sin(turned)[:, None, :])

def rotate(values, cosine, sine):
    half = cosine.shape[-1]
    first = values[..., :half]
    second = values[..., half:2 * half]
    return jnp.concatenate([first * cosine - second * sine, second * cosine + first * sine, values[..., 2 * half:]], axis=-1)

def layer_forward(state, attn_weight, expand_weight, contract_weight, norm_params):
    feature_mean = lax.optimization_barrier(jnp.mean(state, axis=-1, keepdims=True))
    centered_input = state - feature_mean
    inverse_deviation = lax.rsqrt(lax.optimization_barrier(jnp.mean(centered_input * centered_input, axis=-1, keepdims=True)) + eps_norm)
    normed = low(centered_input * inverse_deviation * norm_params[0] + norm_params[1])
    weights = low(attn_weight).reshape(4, H, HD, D)
    lin = jnp.einsum('td,khed->kthe', normed, weights[:3], precision=highest)
    positions = jnp.arange(LENGTH, dtype=jnp.float32)
    cosine, sine = angles(positions, ROT // 2)
    query = low_back(low(rotate(low_back(lin[0]), cosine, sine)))
    keys = low_back(low(rotate(low_back(lin[1]), cosine, sine)))
    value = low_back(low(lin[2]))
    scale = HD ** (-0.5)

    def attend(index):
        start = index * QB
        q_block = lax.dynamic_slice_in_dim(query, start, QB, 0)
        scores = low_back(jnp.einsum('qhe,khe->hqk', q_block, keys, precision=highest) * scale)
        rows_at = start + jnp.arange(QB, dtype=jnp.int32)
        cols_at = jnp.arange(LENGTH, dtype=jnp.int32)
        scores = jnp.where((cols_at[None, :] <= rows_at[:, None])[None], scores, masked_score)
        top = lax.optimization_barrier(jnp.max(scores, axis=-1, keepdims=True))
        expo = jnp.exp(scores - top)
        probs = low(expo / lax.optimization_barrier(jnp.sum(expo, axis=-1, keepdims=True)))
        return jnp.einsum('hqk,khe->qhe', probs, value, precision=highest)
    blocks = lax.map(jax.checkpoint(attend), jnp.arange(LENGTH // QB, dtype=jnp.int32))
    attended = low_back(low(blocks.reshape(LENGTH, H, HD)))
    attn_part = jnp.einsum('the,hed->td', attended, weights[3], precision=highest)
    upward = low_back(jnp.dot(normed, low(expand_weight).T, precision=highest, preferred_element_type=jnp.float32))
    active = low(jax.nn.gelu(upward, approximate=True))
    mlp_part = jnp.dot(active, low(contract_weight), precision=highest, preferred_element_type=jnp.float32)
    return state + low_back(attn_part + mlp_part)

def forward(sequence, params):
    attn_weight, expand_weight, contract_weight, norm_params = params
    state = sequence
    for layer_module in range(LAYERS):
        state = layer_forward(state, attn_weight[layer_module], expand_weight[layer_module], contract_weight[layer_module], norm_params[layer_module])
    return state

def polish(moment):
    size = jnp.sqrt(lax.optimization_barrier(jnp.sum(moment * moment, axis=(1, 2), keepdims=True))) + 1e-07
    current = moment / size
    for turn in range(NS_STEPS):
        gram = jnp.einsum('bij,bkj->bik', current, current, precision=highest)
        mixed = polish_b * gram + polish_c * jnp.einsum('bij,bjk->bik', gram, gram, precision=highest)
        current = polish_a * current + jnp.einsum('bij,bjk->bik', mixed, current, precision=highest)
    return current

def muon_step(weight, grad, moment):
    moment_next = muon_beta * moment + grad
    ortho = polish(moment_next.reshape(-1, HD, D)).reshape(moment.shape)
    return (moment_next, weight - muon_rate * (muon_decay * weight + 0.2 * math.sqrt(D) * ortho))

def reference(inputs, cotangent, attn_weight, expand_weight, contract_weight, norm_params, attn_moment, expand_moment, contract_moment, norm_first, norm_second):
    params = (attn_weight, expand_weight, contract_weight, norm_params)
    count = TOKENS // LENGTH
    sequences = inputs.reshape(count, LENGTH, D)
    cotangents = cotangent.reshape(count, LENGTH, D)
    zeros = jax.tree.map(jnp.zeros_like, params)

    def one_sequence(total, pair):
        sequence, grad_out = pair
        result, pull = jax.vjp(forward, sequence, params)
        grad_in, grad_params = pull(grad_out)
        return (jax.tree.map(jnp.add, total, grad_params), (result, grad_in))
    grads, (results, grad_inputs) = lax.scan(one_sequence, zeros, (sequences, cotangents))
    attn_grad, expand_grad, contract_grad, norm_grad = grads
    attn_moment_next, attn_next = muon_step(attn_weight, attn_grad, attn_moment)
    expand_moment_next, expand_next = muon_step(expand_weight, expand_grad, expand_moment)
    contract_moment_next, contract_next = muon_step(contract_weight, contract_grad, contract_moment)
    first_next = adam_first * norm_first + (1.0 - adam_first) * norm_grad
    second_next = adam_second * norm_second + (1.0 - adam_second) * norm_grad * norm_grad
    first_fix = 1.0 - adam_first ** STEP
    second_fix = 1.0 - adam_second ** STEP
    norm_next = norm_params - adam_rate * (first_next / first_fix) / (jnp.sqrt(second_next / second_fix) + adam_eps)
    return (results.reshape(TOKENS, D), grad_inputs.reshape(TOKENS, D), attn_grad, attn_moment_next, attn_next, expand_grad, expand_moment_next, expand_next, contract_grad, contract_moment_next, contract_next, norm_grad, first_next, second_next, norm_next)
```

```python
import functools
import math

import jax
import jax.numpy as jnp
from jax import lax
from jax.experimental import pallas as pl
from jax.experimental.pallas import tpu as pltpu
from jax.sharding import PartitionSpec as P

D = 2048
H = 32
HD = 64
ROT = 32
LENGTH = 2048
NS_STEPS = 5
STEP = 10
ROWS = 128
WROWS = 64
KINDS = 3
QKV = 384
HIDDEN = 512
FIRST = QKV + HIDDEN
SECOND = 128 + HIDDEN
WALL = FIRST + SECOND

eps_norm = 1e-05
rope_base = 10000.0
muon_beta = 0.95
muon_rate = 0.15
muon_decay = 0.01
polish_a = 3.4445
polish_b = -4.775
polish_c = 2.0315
adam_first = 0.9
adam_second = 0.95
adam_rate = 0.5
adam_eps = 1e-08
masked_score = -1e30
highest = lax.Precision.HIGHEST
across = (((1,), (1,)), ((), ()))
downward = (((0,), (0,)), ((), ()))
MESH = pl.DeviceIdType.MESH
f32 = jnp.float32
bf16 = jnp.bfloat16


def place():
    z = lax.axis_index("fsdp")
    s = lax.axis_index("seq")
    m = lax.axis_index("mp")
    return z, s // 4, lax.rem(s, 4), m // 2, lax.rem(m, 2)


def device(z, xh, y, xl, c):
    return (lax.rem(z + 4, 4), xh * 4 + lax.rem(y + 4, 4), xl * 2 + c)


def token_rows(y, xl, c, start=0, size=ROWS):
    block = lax.rem(y + 4, 4) * 4 + xl * 2 + c
    return pl.ds(pl.multiple_of(block * ROWS + start, 64), size)


def weight_rows(kind, z, xh, start=0, size=WROWS):
    z = lax.rem(z + 4, 4)
    if kind == 0:
        base = z * 128 + (z // 3) * HIDDEN + xh * 64
    elif kind == 1:
        base = QKV + z * 128 + xh * 64
    else:
        base = FIRST + 128 + z * 128 + xh * 64
    return pl.ds(pl.multiple_of(base + start, 32), size)


class Net:
    def __init__(self, send, recv):
        self.send, self.recv, self.used, self.sent = send, recv, 0, []

    def go(self, src, dst, peer):
        slot = self.used
        self.used += 1
        copy = pltpu.make_async_remote_copy(
            src_ref=src,
            dst_ref=dst,
            send_sem=self.send.at[slot],
            recv_sem=self.recv.at[slot],
            device_id=peer,
            device_id_type=MESH,
        )
        copy.start()
        self.sent.append(copy)
        return copy

    def drain(self):
        for copy in self.sent:
            copy.wait_send()
        self.sent = []


class Local:
    def __init__(self, sems):
        self.sems, self.used = sems, 0

    def go(self, src, dst):
        copy = pltpu.make_async_copy(src, dst, self.sems.at[self.used])
        self.used += 1
        copy.start()
        return copy


def greet(peers):
    barrier = pltpu.get_barrier_semaphore()
    for peer in peers:
        pl.semaphore_signal(barrier, inc=1, device_id=peer, device_id_type=MESH)
    pl.semaphore_wait(barrier, len(peers))


def stage_peers(at):
    z, xh, y, xl, c = at
    return [
        [device(z + k, xh, y, xl, c) for k in (1, 2, 3)],
        [device(z, xh, y + k, xl, c) for k in (1, 2, 3)],
        [
            device(z, xh, y, 1 - xl, c),
            device(z, 1 - xh, y, xl, c),
            device(z, 1 - xh, y, 1 - xl, c),
        ],
        [device(z, xh, y, xl, 1 - c)],
    ]


def staged_sum(net, stages, sums, landed, between=None):
    slot = 0
    for stage, peers in enumerate(stages):
        copies = [
            net.go(sums.at[stage], landed.at[slot + k], peer) for k, peer in enumerate(peers)
        ]
        if between is not None:
            between(stage)
        total = sums[stage]
        for k, copy in enumerate(copies):
            copy.wait_recv()
            total = total + landed[slot + k]
        sums[stage + 1] = total
        slot += len(peers)


def spread(flat):
    gain = jnp.concatenate([flat[k : k + 1] for k in range(4)], axis=1)
    bias = jnp.concatenate([flat[k : k + 1] for k in range(4, 8)], axis=1)
    return gain, bias


class TokenGather:
    def __init__(self, net, at, full):
        self.net, self.at, self.full = net, at, full
        z, xh, y, xl, c = at
        self.xpart = device(z, xh, y, 1 - xl, c)
        self.yp = device(z, xh, y + 1, xl, c)
        self.ym = device(z, xh, y - 1, xl, c)
        self.sib = device(z, xh, y, xl, 1 - c)
        self.sibs = []

    def rows(self, dy, dx, start=0, size=ROWS):
        z, xh, y, xl, c = self.at
        return self.full.at[token_rows(y + dy, xl if dx == 0 else 1 - xl, c, start, size)]

    def own(self, block):
        go, here = self.net.go, self.rows(0, 0)
        self.l = go(block, here, self.yp)
        self.r = go(block, here, self.ym)
        self.p = go(block, here, self.xpart)
        self.sibs.append(go(block, here, self.sib))

    def share(self, dy, dx):
        self.sibs.append(self.net.go(self.rows(dy, dx), self.rows(dy, dx), self.sib))

    def near(self):
        go = self.net.go
        self.l.wait_recv()
        half = self.rows(-1, 0, 0, 64)
        self.a = go(half, half, self.yp)
        self.r.wait_recv()
        half = self.rows(1, 0, 64, 64)
        self.b = go(half, half, self.ym)
        self.p.wait_recv()
        other = self.rows(0, 1)
        self.lp = go(other, other, self.yp)
        self.rp = go(other, other, self.ym)
        self.share(-1, 0)
        self.share(1, 0)
        self.share(0, 1)

    def far(self):
        self.a.wait_recv()
        self.b.wait_recv()
        opposite = self.rows(2, 0)
        self.xo = self.net.go(opposite, opposite, self.xpart)
        self.share(2, 0)

    def rest(self):
        self.lp.wait_recv()
        self.share(-1, 1)
        self.rp.wait_recv()
        self.share(1, 1)
        self.xo.wait_recv()
        self.share(2, 1)

    def end(self):
        for copy in self.sibs:
            copy.wait_recv()


class WeightGather:
    def __init__(self, net, at, full, kind):
        self.net, self.at, self.full, self.kind = net, at, full, kind
        z, xh, y, xl, c = at
        self.hpart = device(z, 1 - xh, y, xl, c)
        self.zp = device(z + 1, xh, y, xl, c)
        self.zm = device(z - 1, xh, y, xl, c)

    def rows(self, dz, dh, start=0, size=WROWS):
        z, xh = self.at[:2]
        return self.full.at[
            weight_rows(self.kind, z + dz, xh if dh == 0 else 1 - xh, start, size)
        ]

    def own(self, block):
        go, here = self.net.go, self.rows(0, 0)
        self.l = go(block, here, self.zp)
        self.r = go(block, here, self.zm)
        self.p = go(block, here, self.hpart)

    def near(self):
        go = self.net.go
        self.l.wait_recv()
        half = self.rows(-1, 0, 0, 32)
        self.a = go(half, half, self.zp)
        self.r.wait_recv()
        half = self.rows(1, 0, 32, 32)
        self.b = go(half, half, self.zm)
        self.p.wait_recv()
        other = self.rows(0, 1)
        self.lp = go(other, other, self.zp)
        self.rp = go(other, other, self.zm)

    def far(self):
        go = self.net.go
        self.lp.wait_recv()
        half = self.rows(-1, 1, 0, 32)
        self.ha = go(half, half, self.zp)
        self.rp.wait_recv()
        half = self.rows(1, 1, 32, 32)
        self.hb = go(half, half, self.zm)

    def end(self):
        for copy in (self.a, self.b, self.ha, self.hb):
            copy.wait_recv()


def gather_kernel(
    x_ref, ct_ref, aw_ref, ew_ref, cw_ref, norm_ref,
    normed_ref, gb_ref, w_ref, norm_out,
    own_n, own_g, own_w, sums, landed, send, recv, local,
):
    at = place()
    z, xh, y, xl, c = at
    stages = stage_peers(at)
    net, near = Net(send, recv), Local(local)
    greet([peer for stage in stages for peer in stage])
    weights = [WeightGather(net, at, w_ref, kind) for kind in range(KINDS)]
    blocks = (aw_ref, ew_ref, cw_ref)
    kept = []

    def cast_own(kind):
        own_w[kind] = blocks[kind][...].astype(bf16)
        weights[kind].own(own_w.at[kind])
        kept.append(near.go(own_w.at[kind], weights[kind].rows(0, 0)))

    sums[0] = norm_ref[...]

    def between(stage):
        if stage == 1:
            cast_own(0)
            cast_own(1)

            @pl.loop(0, ROWS // 16)
            def _(i):
                part = pl.ds(i * 16, 16)
                own_g[part] = ct_ref[part].astype(bf16)

    staged_sum(net, stages, sums, landed, between)
    norm_out[...] = sums[4]
    gain, bias = spread(sums[4])

    @pl.loop(0, ROWS // 16)
    def _(i):
        part = pl.ds(i * 16, 16)
        x = x_ref[part]
        centred = x - jnp.mean(x, axis=1, keepdims=True)
        inverse = lax.rsqrt(jnp.mean(centred * centred, axis=1, keepdims=True) + eps_norm)
        own_n[part] = (centred * inverse * gain + bias).astype(bf16)

    normed = TokenGather(net, at, normed_ref)
    grads = TokenGather(net, at, gb_ref)
    normed.own(own_n)
    kept.append(near.go(own_n, normed.rows(0, 0)))
    weights[0].near()
    normed.near()
    grads.own(own_g)
    kept.append(near.go(own_g, grads.rows(0, 0)))
    weights[1].near()
    cast_own(2)
    weights[0].far()
    normed.far()
    weights[1].far()
    weights[2].near()
    normed.rest()
    grads.near()
    weights[2].far()
    grads.far()
    grads.rest()
    for item in weights + [normed, grads]:
        item.end()
    net.drain()
    for copy in kept:
        copy.wait()


def gather(x, ct, aw, ew, cw, norm_rows):
    any_ref = pl.BlockSpec(memory_space=pl.ANY)
    vmem = pl.BlockSpec(memory_space=pltpu.VMEM)
    return pl.pallas_call(
        gather_kernel,
        name="gather",
        out_shape=(
            jax.ShapeDtypeStruct((LENGTH, D), bf16),
            jax.ShapeDtypeStruct((LENGTH, D), bf16),
            jax.ShapeDtypeStruct((WALL, D), bf16),
            jax.ShapeDtypeStruct((8, 512), f32),
        ),
        in_specs=[vmem] * 6,
        out_specs=(any_ref, any_ref, any_ref, vmem),
        scratch_shapes=[
            pltpu.VMEM((ROWS, D), bf16),
            pltpu.VMEM((ROWS, D), bf16),
            pltpu.VMEM((KINDS, WROWS, D), bf16),
            pltpu.VMEM((5, 8, 512), f32),
            pltpu.VMEM((10, 8, 512), f32),
            pltpu.SemaphoreType.DMA((80,)),
            pltpu.SemaphoreType.DMA((80,)),
            pltpu.SemaphoreType.DMA((8,)),
        ],
        compiler_params=pltpu.CompilerParams(
            collective_id=1, has_side_effects=True, vmem_limit_bytes=48 << 20
        ),
    )(x, ct, aw, ew, cw, norm_rows)


def add_rows(count, put, *refs):
    @pl.loop(0, count // 16)
    def _(i):
        part = pl.ds(pl.multiple_of(i * 16, 16), 16)
        total = refs[0][part].astype(f32)
        for ref in refs[1:]:
            total = total + ref[part].astype(f32)
        put(part, total)


def add_into(count, out, *refs):
    def put(part, total):
        out[part] = total.astype(out.dtype)

    add_rows(count, put, *refs)


PLACES = [(0, 0), (-1, 0), (1, 0), (2, 0), (0, 1), (-1, 1), (1, 1), (2, 1)]


class TokenScatter:
    def __init__(self, net, near, at, part, mine, sibs, landed, out):
        self.net, self.near, self.at, self.part = net, near, at, part
        self.mine, self.sibs, self.landed, self.out = mine, sibs, landed, out
        z, xh, y, xl, c = at
        self.xpart = device(z, xh, y, 1 - xl, c)
        self.yp = device(z, xh, y + 1, xl, c)
        self.ym = device(z, xh, y - 1, xl, c)
        self.sib = device(z, xh, y, xl, 1 - c)
        self.loads, self.swaps = {}, {}

    def slot(self, dy, dx):
        return PLACES.index((dy, dx))

    def swap(self, dy, dx):
        z, xh, y, xl, c = self.at
        x, slot = (xl if dx == 0 else 1 - xl), self.slot(dy, dx)
        self.swaps[slot] = self.net.go(
            self.part.at[token_rows(y + dy, x, 1 - c)], self.sibs.at[slot], self.sib
        )
        self.loads[slot] = self.near.go(
            self.part.at[token_rows(y + dy, x, c)], self.mine.at[slot]
        )

    def swap_all(self):
        for dy, dx in ((2, 1), (-1, 1), (1, 1), (2, 0), (-1, 0), (1, 0), (0, 1), (0, 0)):
            self.swap(dy, dx)

    def ready(self, dy, dx, *more):
        slot = self.slot(dy, dx)
        self.loads[slot].wait()
        self.swaps[slot].wait_recv()
        add_into(ROWS, self.mine.at[slot], self.mine.at[slot], self.sibs.at[slot], *more)
        return self.mine.at[slot]

    def send(self, src, slot, peer, start=0, size=ROWS):
        return self.net.go(src, self.landed.at[slot, pl.ds(start, size)], peer)

    def far(self):
        self.xo = self.send(self.ready(2, 1), 0, self.xpart)
        self.lp = self.send(self.ready(-1, 1), 1, self.ym)
        self.rp = self.send(self.ready(1, 1), 2, self.yp)

    def opposite(self):
        self.xo.wait_recv()
        block = self.ready(2, 0, self.landed.at[0])
        self.a = self.send(block.at[pl.ds(0, 64)], 3, self.ym, 0, 64)
        self.b = self.send(block.at[pl.ds(64, 64)], 3, self.yp, 64, 64)

    def near_left(self):
        block = self.ready(-1, 0)
        self.a.wait_recv()
        top = pl.ds(0, 64)
        add_into(64, block.at[top], block.at[top], self.landed.at[3, top])
        self.l = self.send(block, 4, self.ym)

    def near_right(self):
        block = self.ready(1, 0)
        self.b.wait_recv()
        low = pl.ds(64, 64)
        add_into(64, block.at[low], block.at[low], self.landed.at[3, low])
        self.r = self.send(block, 5, self.yp)

    def partner(self):
        self.lp.wait_recv()
        self.rp.wait_recv()
        block = self.ready(0, 1, self.landed.at[1], self.landed.at[2])
        self.p = self.send(block, 6, self.xpart)

    def final(self):
        self.l.wait_recv()
        self.r.wait_recv()
        self.p.wait_recv()
        slot = self.slot(0, 0)
        self.loads[slot].wait()
        self.swaps[slot].wait_recv()
        add_into(
            ROWS, self.out, self.mine.at[slot], self.sibs.at[slot],
            self.landed.at[4], self.landed.at[5], self.landed.at[6],
        )


class WeightScatter:
    def __init__(self, net, at, part, kind, landed, out):
        self.net, self.at, self.part, self.kind = net, at, part, kind
        self.landed, self.out = landed, out
        z, xh, y, xl, c = at
        self.hpart = device(z, 1 - xh, y, xl, c)
        self.zp = device(z + 1, xh, y, xl, c)
        self.zm = device(z - 1, xh, y, xl, c)

    def rows(self, dz, dh, start=0, size=WROWS):
        z, xh = self.at[:2]
        return self.part.at[
            weight_rows(self.kind, z + dz, xh if dh == 0 else 1 - xh, start, size)
        ]

    def send(self, src, slot, peer, start=0, size=WROWS):
        return self.net.go(src, self.landed.at[slot, pl.ds(start, size)], peer)

    def opposite(self):
        self.a, self.b = [], []
        for dh in (0, 1):
            self.a.append(self.send(self.rows(2, dh, 0, 32), dh, self.zm, 0, 32))
            self.b.append(self.send(self.rows(2, dh, 32, 32), dh, self.zp, 32, 32))

    def near(self):
        self.l, self.r = [], []
        for dh in (1, 0):
            self.a[dh].wait_recv()
            half = self.rows(-1, dh, 0, 32)
            add_into(32, half, half, self.landed.at[dh, pl.ds(0, 32)])
            self.l.append(self.send(self.rows(-1, dh), 2 + dh, self.zm))
            self.b[dh].wait_recv()
            half = self.rows(1, dh, 32, 32)
            add_into(32, half, half, self.landed.at[dh, pl.ds(32, 32)])
            self.r.append(self.send(self.rows(1, dh), 4 + dh, self.zp))

    def partner(self):
        self.l[0].wait_recv()
        self.r[0].wait_recv()
        other = self.rows(0, 1)
        add_into(WROWS, other, other, self.landed.at[3], self.landed.at[5])
        self.p = self.send(other, 6, self.hpart)

    def final(self):
        self.l[1].wait_recv()
        self.r[1].wait_recv()
        self.p.wait_recv()
        add_into(
            WROWS, self.out, self.rows(0, 0),
            self.landed.at[2], self.landed.at[4], self.landed.at[6],
        )


def scatter_kernel(
    branch_ref, dnormed_ref, wgrad_ref,
    branch_out, dnormed_out, wgrad_out,
    mine, sibs, landed, wpart, wlanded, send, recv, local,
):
    at = place()
    z, xh, y, xl, c = at
    net, near = Net(send, recv), Local(local)
    greet(
        [
            device(z, xh, y, 1 - xl, c),
            device(z, xh, y, xl, 1 - c),
            device(z, xh, y + 1, xl, c),
            device(z, xh, y - 1, xl, c),
            device(z + 1, xh, y, xl, c),
            device(z - 1, xh, y, xl, c),
            device(z, 1 - xh, y, xl, c),
        ]
    )
    loads = {}
    for kind, (start, size) in ((2, (FIRST + 128, HIDDEN)), (1, (QKV, HIDDEN)), (0, (0, QKV))):
        loads[kind] = [near.go(wgrad_ref.at[pl.ds(start, size)], wpart.at[pl.ds(start, size)])]
    loads[0].append(near.go(wgrad_ref.at[pl.ds(FIRST, 128)], wpart.at[pl.ds(FIRST, 128)]))
    tokens = [
        TokenScatter(net, near, at, part, mine.at[k], sibs.at[k], landed.at[k], out)
        for k, (part, out) in enumerate(((branch_ref, branch_out), (dnormed_ref, dnormed_out)))
    ]
    weights = [
        WeightScatter(net, at, wpart, kind, wlanded.at[kind], wgrad_out.at[kind])
        for kind in range(KINDS)
    ]
    branch, dnormed = tokens
    branch.swap_all()
    for kind in (2, 1, 0):
        for load in loads[kind]:
            load.wait()
        weights[kind].opposite()
    dnormed.swap_all()
    branch.far()
    weights[2].near()
    branch.opposite()
    branch.near_left()
    branch.near_right()
    weights[1].near()
    dnormed.far()
    dnormed.opposite()
    weights[0].near()
    branch.partner()
    dnormed.near_left()
    dnormed.near_right()
    for kind in (2, 1, 0):
        weights[kind].partner()
    branch.final()
    dnormed.partner()
    for kind in (2, 1, 0):
        weights[kind].final()
    dnormed.final()
    net.drain()


def scatter(branch, dnormed, wgrad):
    any_ref = pl.BlockSpec(memory_space=pl.ANY)
    vmem = pl.BlockSpec(memory_space=pltpu.VMEM)
    return pl.pallas_call(
        scatter_kernel,
        name="scatter",
        out_shape=(
            jax.ShapeDtypeStruct((ROWS, D), f32),
            jax.ShapeDtypeStruct((ROWS, D), f32),
            jax.ShapeDtypeStruct((KINDS, WROWS, D), f32),
        ),
        in_specs=[any_ref] * 3,
        out_specs=(vmem,) * 3,
        scratch_shapes=[
            pltpu.VMEM((2, 8, ROWS, D), bf16),
            pltpu.VMEM((2, 8, ROWS, D), bf16),
            pltpu.VMEM((2, 7, ROWS, D), bf16),
            pltpu.VMEM((WALL, D), bf16),
            pltpu.VMEM((KINDS, 7, WROWS, D), bf16),
            pltpu.SemaphoreType.DMA((80,)),
            pltpu.SemaphoreType.DMA((80,)),
            pltpu.SemaphoreType.DMA((24,)),
        ],
        compiler_params=pltpu.CompilerParams(
            collective_id=2, has_side_effects=True, vmem_limit_bytes=58 << 20
        ),
    )(branch, dnormed, wgrad)


def norm_sum_kernel(part_ref, out_ref, sums, landed, send, recv):
    stages = stage_peers(place())
    net = Net(send, recv)
    greet([peer for stage in stages for peer in stage])
    sums[0] = part_ref[...]
    staged_sum(net, stages, sums, landed)
    out_ref[...] = sums[4]
    net.drain()


def norm_sum(part):
    vmem = pl.BlockSpec(memory_space=pltpu.VMEM)
    return pl.pallas_call(
        norm_sum_kernel,
        name="norm_sum",
        out_shape=jax.ShapeDtypeStruct((8, 512), f32),
        in_specs=[vmem],
        out_specs=vmem,
        scratch_shapes=[
            pltpu.VMEM((5, 8, 512), f32),
            pltpu.VMEM((10, 8, 512), f32),
            pltpu.SemaphoreType.DMA((10,)),
            pltpu.SemaphoreType.DMA((10,)),
        ],
        compiler_params=pltpu.CompilerParams(collective_id=3, has_side_effects=True),
    )(part)


def angles(positions, half):
    freq = rope_base ** (-2.0 * jnp.arange(half, dtype=jnp.float32) / (2 * half))
    turned = positions[:, None] * freq[None, :]
    return (jnp.cos(turned)[:, None, :], jnp.sin(turned)[:, None, :])


def rotate(values, cosine, sine):
    half = cosine.shape[-1]
    first = values[..., :half]
    second = values[..., half : 2 * half]
    return jnp.concatenate(
        [first * cosine - second * sine, second * cosine + first * sine, values[..., 2 * half :]],
        axis=-1,
    )


def gelu(values):
    return jax.nn.gelu(values, approximate=True)


def causal(offset, block, width):
    rows_at = offset + lax.broadcasted_iota(jnp.int32, (block, width), 0)
    cols_at = lax.broadcasted_iota(jnp.int32, (block, width), 1)
    return (cols_at <= rows_at)[None]


def block_scores(query, keys, start, block, first):
    stop = start + block
    scores = jnp.einsum(
        "qhe,khe->hqk", query[start:stop], keys[first:stop], preferred_element_type=jnp.float32
    ) * HD ** (-0.5)
    return jnp.where(causal(start - first, block, stop - first), scores, masked_score)


def attend_forward(whole, heads, block, seq_len):
    length = whole.shape[0]
    query = whole[:, 0].reshape(length, heads, HD)
    keys = whole[:, 1].reshape(length, heads, HD)
    value = whole[:, 2].reshape(length, heads, HD)
    outputs = []
    totals = []
    for index in range(length // block):
        start = index * block
        stop = start + block
        first = start // seq_len * seq_len
        scores = block_scores(query, keys, start, block, first)
        top = jnp.max(scores, axis=-1, keepdims=True)
        expo = jnp.exp(scores - top)
        total = jnp.sum(expo, axis=-1, keepdims=True)
        probs = (expo / total).astype(jnp.bfloat16)
        attended = jnp.einsum(
            "hqk,khe->qhe", probs, value[first:stop], preferred_element_type=jnp.float32
        )
        outputs.append(attended.astype(jnp.bfloat16).reshape(block, heads * HD))
        totals.append(top + jnp.log(total))
    return (jnp.concatenate(outputs, axis=0), totals)


def attend_backward(whole, totals, grad_attended, heads, block, seq_len):
    length = whole.shape[0]
    scale = HD ** (-0.5)
    query = whole[:, 0].reshape(length, heads, HD)
    keys = whole[:, 1].reshape(length, heads, HD)
    value = whole[:, 2].reshape(length, heads, HD)
    grad_out = grad_attended.reshape(length, heads, HD)
    grad_query = []
    grad_keys = jnp.zeros((length, heads, HD), jnp.float32)
    grad_value = jnp.zeros((length, heads, HD), jnp.float32)
    for index in range(length // block):
        start = index * block
        stop = start + block
        first = start // seq_len * seq_len
        scores = block_scores(query, keys, start, block, first)
        probs_full = jnp.exp(scores - totals[index])
        probs = probs_full.astype(jnp.bfloat16)
        grad_block = grad_out[start:stop]
        grad_value = grad_value.at[first:stop].add(
            jnp.einsum("hqk,qhe->khe", probs, grad_block, preferred_element_type=jnp.float32)
        )
        grad_probs = jnp.einsum(
            "qhe,khe->hqk", grad_block, value[first:stop], preferred_element_type=jnp.float32
        )
        inner = jnp.sum(probs_full * grad_probs, axis=-1, keepdims=True)
        grad_scores = (probs_full * (grad_probs - inner)).astype(jnp.bfloat16)
        grad_query.append(
            (
                jnp.einsum(
                    "hqk,khe->qhe",
                    grad_scores,
                    keys[first:stop],
                    preferred_element_type=jnp.float32,
                )
                * scale
            ).astype(jnp.bfloat16)
        )
        grad_keys = grad_keys.at[first:stop].add(
            jnp.einsum(
                "hqk,qhe->khe", grad_scores, query[start:stop], preferred_element_type=jnp.float32
            )
            * scale
        )
    stacked = [
        jnp.concatenate(grad_query, axis=0),
        grad_keys.astype(jnp.bfloat16),
        grad_value.astype(jnp.bfloat16),
    ]
    return jnp.stack([piece.reshape(length, heads * HD) for piece in stacked], axis=1)


def polish(moment):
    size = jnp.sqrt(jnp.sum(moment * moment, axis=(1, 2), keepdims=True)) + 1e-07
    current = moment / size

    def times(a, b):
        return jnp.einsum("bij,bjk->bik", a, b, precision=highest)

    gram = jnp.einsum("bij,bkj->bik", current, current, precision=highest)
    whole = jnp.eye(HD, dtype=f32)[None]
    for turn in range(NS_STEPS):
        factor = (
            polish_a * jnp.eye(HD, dtype=f32)[None] + polish_b * gram + polish_c * times(gram, gram)
        )
        whole = factor if turn == 0 else times(factor, whole)
        if turn < NS_STEPS - 1:
            gram = times(factor, times(gram, factor))
    return times(whole, current)


def body(
    inputs, cotangent, attn_weight, expand_weight, contract_weight, norm_params,
    attn_moment, expand_moment, contract_moment, norm_first, norm_second,
):
    index = (lax.axis_index("fsdp") * 8 + lax.axis_index("seq")) * 4 + lax.axis_index("mp")
    mine = (jnp.arange(D, dtype=jnp.int32) // 16) == index
    norm_rows = jnp.where(mine[None], jnp.tile(norm_params[0], (1, 128)), 0.0).reshape(8, 512)
    normed, grad_group, weights, norm_rows = gather(
        inputs,
        cotangent,
        attn_weight[0, 0],
        expand_weight[0],
        contract_weight[0],
        norm_rows,
    )
    gain = norm_rows.reshape(2, D)[0]
    first_w, second_w = weights[:FIRST], weights[FIRST:]
    cosine, sine = angles(jnp.arange(LENGTH, dtype=f32), ROT // 2)
    lin = lax.dot_general(normed, first_w[:QKV], across, preferred_element_type=f32)
    upward = lax.dot_general(normed, first_w[QKV:], across, preferred_element_type=f32)
    lin = lin.reshape(LENGTH, 3, 2, HD)
    query = rotate(lin[:, 0], cosine, sine).astype(bf16)
    keys = rotate(lin[:, 1], cosine, sine).astype(bf16)
    value = lin[:, 2].astype(bf16)
    whole = jnp.stack([query, keys, value], axis=1).reshape(LENGTH, 3, 2 * HD)
    attended, totals = attend_forward(whole, 2, 512, LENGTH)
    active = gelu(upward).astype(bf16)
    inner = jnp.concatenate([attended, active], axis=1)
    branch = jnp.dot(inner, second_w, preferred_element_type=f32).astype(bf16)
    grad_inner = lax.dot_general(grad_group, second_w, across, preferred_element_type=f32)
    grad_attended = grad_inner[:, :128].astype(bf16)
    slope = jax.vjp(gelu, upward)[1]
    grad_up = slope(grad_inner[:, 128:])[0].astype(bf16)
    second_part = lax.dot_general(inner, grad_group, downward, preferred_element_type=f32)
    grad_whole = attend_backward(whole, totals, grad_attended, 2, 512, LENGTH)
    grad_query = rotate(
        grad_whole[:, 0].reshape(LENGTH, 2, HD).astype(f32), cosine, -sine
    ).astype(bf16)
    grad_keys = rotate(
        grad_whole[:, 1].reshape(LENGTH, 2, HD).astype(f32), cosine, -sine
    ).astype(bf16)
    outer = jnp.concatenate(
        [
            grad_query.reshape(LENGTH, 128),
            grad_keys.reshape(LENGTH, 128),
            grad_whole[:, 2],
            grad_up,
        ],
        axis=1,
    )
    first_part = lax.dot_general(outer, normed, downward, preferred_element_type=f32)
    grad_normed = jnp.dot(outer, first_w, preferred_element_type=f32).astype(bf16)
    parts = jnp.concatenate([first_part, second_part], axis=0).astype(bf16)
    branch, hidden_gradient, shares = scatter(branch, grad_normed, parts)

    state = inputs + branch
    feature_mean = jnp.mean(inputs, axis=-1, keepdims=True)
    centered_input = inputs - feature_mean
    inverse_deviation = lax.rsqrt(
        jnp.mean(centered_input * centered_input, axis=-1, keepdims=True) + eps_norm
    )
    normalized_input = centered_input * inverse_deviation
    norm_part = jnp.stack(
        [jnp.sum(hidden_gradient * normalized_input, axis=0), jnp.sum(hidden_gradient, axis=0)],
        axis=0,
    )
    scaled = hidden_gradient * gain
    grad_state = cotangent + inverse_deviation * (
        scaled
        - jnp.mean(scaled, axis=-1, keepdims=True)
        - normalized_input * jnp.mean(scaled * normalized_input, axis=-1, keepdims=True)
    )
    norm_total = norm_sum(norm_part.reshape(8, 512)).reshape(2, D)
    norm_share = lax.dynamic_slice(norm_total, (0, index * 16), (2, 16))[None]

    moments = jnp.stack([attn_moment[0, 0], expand_moment[0], contract_moment[0]])
    moments = muon_beta * moments + shares
    ortho = polish(moments)
    updates = []
    for k, weight in enumerate((attn_weight, expand_weight, contract_weight)):
        shape = weight.shape
        new = weight - muon_rate * (
            muon_decay * weight + 0.2 * math.sqrt(D) * ortho[k].reshape(shape)
        )
        updates += [shares[k].reshape(shape), moments[k].reshape(shape), new]
    first_next = adam_first * norm_first + (1.0 - adam_first) * norm_share
    second_next = adam_second * norm_second + (1.0 - adam_second) * norm_share * norm_share
    first_fix = 1.0 - adam_first**STEP
    second_fix = 1.0 - adam_second**STEP
    norm_next = norm_params - adam_rate * (first_next / first_fix) / (
        jnp.sqrt(second_next / second_fix) + adam_eps
    )
    return (state, grad_state, *updates, norm_share, first_next, second_next, norm_next)


def solution(mesh):
    return jax.shard_map(
        body,
        mesh=mesh,
        in_specs=(
            P(("fsdp", "seq", "mp"), None),
            P(("fsdp", "seq", "mp"), None),
            P(None, ("fsdp", "seq", "mp"), None, None),
            P(None, ("fsdp", "seq", "mp"), None),
            P(None, ("fsdp", "seq", "mp"), None),
            P(None, None, ("fsdp", "seq", "mp")),
            P(None, ("fsdp", "seq", "mp"), None, None),
            P(None, ("fsdp", "seq", "mp"), None),
            P(None, ("fsdp", "seq", "mp"), None),
            P(None, None, ("fsdp", "seq", "mp")),
            P(None, None, ("fsdp", "seq", "mp")),
        ),
        out_specs=(
            P(("fsdp", "seq", "mp"), None),
            P(("fsdp", "seq", "mp"), None),
            P(None, ("fsdp", "seq", "mp"), None, None),
            P(None, ("fsdp", "seq", "mp"), None, None),
            P(None, ("fsdp", "seq", "mp"), None, None),
            P(None, ("fsdp", "seq", "mp"), None),
            P(None, ("fsdp", "seq", "mp"), None),
            P(None, ("fsdp", "seq", "mp"), None),
            P(None, ("fsdp", "seq", "mp"), None),
            P(None, ("fsdp", "seq", "mp"), None),
            P(None, ("fsdp", "seq", "mp"), None),
            P(None, None, ("fsdp", "seq", "mp")),
            P(None, None, ("fsdp", "seq", "mp")),
            P(None, None, ("fsdp", "seq", "mp")),
            P(None, None, ("fsdp", "seq", "mp")),
        ),
        check_vma=False,
    )
```

```python
import functools
import math

import jax
import jax.numpy as jnp
from jax import lax
from jax.experimental import pallas as pl
from jax.experimental.pallas import tpu as pltpu
from jax.sharding import PartitionSpec as P

D = 2048
H = 32
HD = 64
ROT = 32
LENGTH = 2048
NS_STEPS = 5
STEP = 10
ROWS = 128
WROWS = 64
KINDS = 3
QKV = 384
HIDDEN = 512
FIRST = QKV + HIDDEN
SECOND = 128 + HIDDEN
WALL = FIRST + SECOND

eps_norm = 1e-05
rope_base = 10000.0
muon_beta = 0.95
muon_rate = 0.15
muon_decay = 0.01
polish_a = 3.4445
polish_b = -4.775
polish_c = 2.0315
adam_first = 0.9
adam_second = 0.95
adam_rate = 0.5
adam_eps = 1e-08
masked_score = -1e30
highest = lax.Precision.HIGHEST
across = (((1,), (1,)), ((), ()))
downward = (((0,), (0,)), ((), ()))
MESH = pl.DeviceIdType.MESH
f32 = jnp.float32
bf16 = jnp.bfloat16


def place():
    z = lax.axis_index("fsdp")
    s = lax.axis_index("seq")
    m = lax.axis_index("mp")
    return z, s // 4, lax.rem(s, 4), m // 2, lax.rem(m, 2)


def device(z, xh, y, xl, c):
    return (lax.rem(z + 4, 4), xh * 4 + lax.rem(y + 4, 4), xl * 2 + c)


def token_rows(y, xl, c, start=0, size=ROWS):
    block = lax.rem(y + 4, 4) * 4 + xl * 2 + c
    return pl.ds(pl.multiple_of(block * ROWS + start, 64), size)


def weight_rows(kind, z, xh, start=0, size=WROWS):
    z = lax.rem(z + 4, 4)
    if kind == 0:
        base = z * 128 + (z // 3) * HIDDEN + xh * 64
    elif kind == 1:
        base = QKV + z * 128 + xh * 64
    else:
        base = FIRST + 128 + z * 128 + xh * 64
    return pl.ds(pl.multiple_of(base + start, 32), size)


class Net:
    def __init__(self, send, recv):
        self.send, self.recv, self.used, self.sent = send, recv, 0, []

    def go(self, src, dst, peer, sent=None):
        slot = self.used
        self.used += 1
        copy = pltpu.make_async_remote_copy(
            src_ref=src,
            dst_ref=dst,
            send_sem=self.send.at[slot],
            recv_sem=self.recv.at[slot],
            device_id=peer,
            device_id_type=MESH,
        )
        copy.start()
        (self.sent if sent is None else sent).append(copy)
        return copy

    def drain(self):
        for copy in self.sent:
            copy.wait_send()
        self.sent = []


class Local:
    def __init__(self, sems):
        self.sems, self.used = sems, 0

    def go(self, src, dst):
        copy = pltpu.make_async_copy(src, dst, self.sems.at[self.used])
        self.used += 1
        copy.start()
        return copy


def greet(peers):
    barrier = pltpu.get_barrier_semaphore()
    for peer in peers:
        pl.semaphore_signal(barrier, inc=1, device_id=peer, device_id_type=MESH)
    pl.semaphore_wait(barrier, len(peers))


def stage_peers(at):
    z, xh, y, xl, c = at
    return [
        [device(z + k, xh, y, xl, c) for k in (1, 2, 3)],
        [device(z, xh, y + k, xl, c) for k in (1, 2, 3)],
        [
            device(z, xh, y, 1 - xl, c),
            device(z, 1 - xh, y, xl, c),
            device(z, 1 - xh, y, 1 - xl, c),
        ],
        [device(z, xh, y, xl, 1 - c)],
    ]


class Staged:
    def __init__(self, net, stages, sums, landed):
        self.net, self.stages, self.sums, self.landed = net, stages, sums, landed
        self.stage = self.slot = 0

    def start(self):
        self.copies = [
            self.net.go(self.sums.at[self.stage], self.landed.at[self.slot + k], peer)
            for k, peer in enumerate(self.stages[self.stage])
        ]

    def finish(self):
        total = self.sums[self.stage]
        for copy in self.copies:
            copy.wait_recv()
            total = total + self.landed[self.slot]
            self.slot += 1
        self.stage += 1
        self.sums[self.stage] = total


def spread(flat):
    gain = jnp.concatenate([flat[k : k + 1] for k in range(4)], axis=1)
    bias = jnp.concatenate([flat[k : k + 1] for k in range(4, 8)], axis=1)
    return gain, bias


class TokenGather:
    def __init__(self, net, at, full):
        self.net, self.at, self.full, self.sent = net, at, full, []
        z, xh, y, xl, c = at
        self.xpart = device(z, xh, y, 1 - xl, c)
        self.yp = device(z, xh, y + 1, xl, c)
        self.ym = device(z, xh, y - 1, xl, c)
        self.sib = device(z, xh, y, xl, 1 - c)
        self.sibs = {}

    def rows(self, dy, dx, start=0, size=ROWS):
        z, xh, y, xl, c = self.at
        return self.full.at[token_rows(y + dy, xl if dx == 0 else 1 - xl, c, start, size)]

    def go(self, src, dst, peer):
        return self.net.go(src, dst, peer, self.sent)

    def clear(self):
        for copy in self.sent:
            copy.wait_send()

    def own(self, block):
        go, here = self.go, self.rows(0, 0)
        self.l = go(block, here, self.yp)
        self.r = go(block, here, self.ym)
        self.p = go(block, here, self.xpart)
        self.sibs[0, 0] = go(block, here, self.sib)

    def share(self, dy, dx):
        self.sibs[dy, dx] = self.go(self.rows(dy, dx), self.rows(dy, dx), self.sib)

    def near(self):
        go = self.go
        self.l.wait_recv()
        half = self.rows(-1, 0, 0, 64)
        self.a = go(half, half, self.yp)
        self.r.wait_recv()
        half = self.rows(1, 0, 64, 64)
        self.b = go(half, half, self.ym)
        self.p.wait_recv()
        other = self.rows(0, 1)
        self.lp = go(other, other, self.yp)
        self.rp = go(other, other, self.ym)
        self.share(-1, 0)
        self.share(1, 0)
        self.share(0, 1)

    def far(self):
        self.a.wait_recv()
        self.b.wait_recv()
        opposite = self.rows(2, 0)
        self.xo = self.go(opposite, opposite, self.xpart)
        self.share(2, 0)

    def rest(self):
        self.lp.wait_recv()
        self.share(-1, 1)
        self.rp.wait_recv()
        self.share(1, 1)
        self.xo.wait_recv()
        self.share(2, 1)

    def end(self, *pairs):
        for pair in pairs:
            self.sibs[pair].wait_recv()


class WeightGather:
    def __init__(self, net, at, full, kind):
        self.net, self.at, self.full, self.kind = net, at, full, kind
        z, xh, y, xl, c = at
        self.hpart = device(z, 1 - xh, y, xl, c)
        self.zp = device(z + 1, xh, y, xl, c)
        self.zm = device(z - 1, xh, y, xl, c)

    def rows(self, dz, dh, start=0, size=WROWS):
        z, xh = self.at[:2]
        return self.full.at[
            weight_rows(self.kind, z + dz, xh if dh == 0 else 1 - xh, start, size)
        ]

    def own(self, block):
        go, here = self.net.go, self.rows(0, 0)
        self.l = go(block, here, self.zp)
        self.r = go(block, here, self.zm)
        self.p = go(block, here, self.hpart)

    def near(self):
        go = self.net.go
        self.l.wait_recv()
        half = self.rows(-1, 0, 0, 32)
        self.a = go(half, half, self.zp)
        self.r.wait_recv()
        half = self.rows(1, 0, 32, 32)
        self.b = go(half, half, self.zm)
        self.p.wait_recv()
        other = self.rows(0, 1)
        self.lp = go(other, other, self.zp)
        self.rp = go(other, other, self.zm)

    def far(self):
        go = self.net.go
        self.lp.wait_recv()
        half = self.rows(-1, 1, 0, 32)
        self.ha = go(half, half, self.zp)
        self.rp.wait_recv()
        half = self.rows(1, 1, 32, 32)
        self.hb = go(half, half, self.zm)

    def end(self):
        for copy in (self.a, self.b, self.ha, self.hb):
            copy.wait_recv()


nn = (((1,), (0,)), ((), ()))
nt = (((1,), (1,)), ((), ()))
tn = (((0,), (0,)), ((), ()))
QB = 512
UNIT = 256


def dot(a, b, dims):
    return lax.dot_general(a, b, dims, preferred_element_type=f32)


def at_unit(unit, size=UNIT):
    return pl.ds(pl.multiple_of(unit * size, size), size)


def turn(part, cosine, sine):
    rows = []
    for low in (0, HD):
        first, second = part[low : low + 16], part[low + 16 : low + 32]
        rows += [first * cosine - second * sine, second * cosine + first * sine]
        rows.append(part[low + 32 : low + HD])
    return jnp.concatenate(rows, axis=0)


def of_head(h, block, axis):
    place = lax.broadcasted_iota(jnp.int32, block.shape, axis)
    return jnp.where((place < HD) == (h == 0), block, 0.0)


def gelu_pair(v):
    square = v * v
    t = jnp.tanh(math.sqrt(2 / math.pi) * (v + 0.044715 * (v * square)))
    plus = 0.5 * (1.0 + t)
    slope = plus + (0.5 * v) * (1.0 - t * t) * (
        math.sqrt(2 / math.pi) * (1.0 + 3 * 0.044715 * square)
    )
    return v * plus, slope


def affine_unit(unit, raw, normed, gain, bias):
    @pl.loop(0, UNIT // 16)
    def _(i):
        part = pl.ds(pl.multiple_of(unit * UNIT + i * 16, 16), 16)
        normed[part] = (raw[part].astype(f32) * gain + bias).astype(bf16)


def qkv_unit(unit, normed, w, table, qm, kv, q_rows, k_rows, v_rows):
    cols = at_unit(unit)
    lin = dot(w[pl.ds(0, QKV)], normed[cols], nt)
    cosine, sine = table[0:16, cols], table[16:32, cols]
    q = turn(lin[0:128], cosine, sine).astype(bf16).astype(f32) * HD**-0.5
    k = turn(lin[128:256], cosine, sine)
    v = lin[256:384]
    for h in range(2):
        qm[h, :, cols] = of_head(h, q, 0).astype(bf16)
    kv[pl.ds(0, 128), cols] = k.astype(bf16)
    kv[pl.ds(128, 128), cols] = v.astype(bf16)
    q_rows[cols] = q.T.astype(bf16)
    k_rows[cols] = k.T.astype(bf16)
    v_rows[cols] = v.T.astype(bf16)


def up_unit(unit, normed, w, inner, slope):
    cols = at_unit(unit)
    act, der = gelu_pair(dot(w[pl.ds(QKV, HIDDEN)], normed[cols], nt))
    inner[pl.ds(128, HIDDEN), cols] = act.astype(bf16)
    slope[:, cols] = der


def branch_unit(unit, inner, w, out):
    rows = at_unit(unit)
    out[rows] = dot(inner[:, rows], w[pl.ds(FIRST, SECOND)], tn).astype(bf16)


def back_unit(unit, gb, w, inner, slope, dom, do_rows, delta, dup):
    cols = at_unit(unit)
    lin = dot(w[pl.ds(FIRST, SECOND)], gb[cols], nt)
    do = lin[0:128].astype(bf16).astype(f32)
    for h in range(2):
        dom[h, :, cols] = of_head(h, do, 0).astype(bf16)
    do_rows[cols] = do.T.astype(bf16)
    both = do * inner[pl.ds(0, 128), cols].astype(f32)
    for h in range(2):
        delta[pl.ds(h, 1), cols] = jnp.sum(both[h * HD : h * HD + HD], axis=0, keepdims=True)
    dup[:, cols] = (lin[128:] * slope[:, cols]).astype(bf16)


def causal_mask(scores):
    rows = lax.broadcasted_iota(jnp.int32, scores.shape, 0)
    cols = lax.broadcasted_iota(jnp.int32, scores.shape, 1)
    return jnp.where(rows <= cols, scores, masked_score)


def attend_block(qb, qm, kv, k_rows, inner, lse):
    cols = at_unit(qb, QB)
    start = (jnp.full((1, QB), masked_score, f32), jnp.zeros((1, QB), f32), jnp.zeros((HD, QB), f32))

    def step(kb, carry, masked):
        keys = at_unit(kb, QB)
        k = k_rows[keys]
        result = []
        for h in range(2):
            top, total, out = carry[h]
            scores = dot(k, qm[h, :, cols], nn)
            if masked:
                scores = causal_mask(scores)
            high = jnp.maximum(top, jnp.max(scores, axis=0, keepdims=True))
            scale = jnp.exp(top - high)
            expo = jnp.exp(scores - high)
            total = total * scale + jnp.sum(expo, axis=0, keepdims=True)
            out = out * scale + dot(kv[pl.ds(128 + h * HD, HD), keys], expo.astype(bf16), nn)
            result.append((high, total, out))
        return tuple(result)

    carry = lax.fori_loop(0, qb, lambda kb, c: step(kb, c, False), (start, start))
    carry = step(qb, carry, True)
    for h in range(2):
        top, total, out = carry[h]
        inner[pl.ds(h * HD, HD), cols] = (out / total).astype(bf16)
        lse[pl.ds(h, 1), cols] = top + jnp.log(total)


def attend_back_block(kb, qm, kv, q_rows, k_rows, v_rows, dom, do_rows, lse, delta, dq, outer, table):
    keys = at_unit(kb, QB)

    def step(qb, carry, masked):
        cols = at_unit(qb, QB)
        k, v = k_rows[keys], v_rows[keys]
        result = []
        for h in range(2):
            dk, dv = carry[h]
            scores = dot(k, qm[h, :, cols], nn)
            if masked:
                scores = causal_mask(scores)
            probs = jnp.exp(scores - lse[pl.ds(h, 1), cols])
            dp = dot(v, dom[h, :, cols], nn)
            ds = (probs * (dp - delta[pl.ds(h, 1), cols])).astype(bf16)
            dv = dv + dot(probs.astype(bf16), do_rows[cols], nn)
            dk = dk + dot(ds, q_rows[cols], nn)
            half = pl.ds(h * HD, HD)
            part = dot(kv[half, keys], ds, nn)
            if kb == 0:
                dq[half, cols] = part
            else:
                dq[half, cols] += part
            result.append((dk, dv))
        return tuple(result)

    zero = jnp.zeros((QB, 128), f32)
    carry = step(kb, ((zero, zero), (zero, zero)), True)
    carry = lax.fori_loop(kb + 1, LENGTH // QB, lambda qb, c: step(qb, c, False), carry)
    (dk0, dv0), (dk1, dv1) = carry
    first = lax.broadcasted_iota(jnp.int32, (QB, 128), 1) < HD
    dk = jnp.where(first, dk0, dk1).astype(bf16).astype(f32).T
    dv = jnp.where(first, dv0, dv1).T
    cosine, sine = table[0:16, keys], -table[16:32, keys]
    outer[pl.ds(128, 128), keys] = turn(dk, cosine, sine).astype(bf16)
    outer[pl.ds(256, 128), keys] = dv.astype(bf16)


def query_back(dq, outer, table):
    part = (dq[...] * HD**-0.5).astype(bf16).astype(f32)
    outer[pl.ds(0, 128)] = turn(part, table[0:16], -table[16:32]).astype(bf16)


EARLY = ((0, 0), (-1, 0), (1, 0), (2, 0), (0, 1))
LATE = ((-1, 1), (1, 1), (2, 1))


def gather_kernel(
    x_ref, ct_ref, aw_ref, ew_ref, cw_ref, norm_ref, table,
    normed_out, gb_ref, w_out, gain_out, qm_out, kv_out, rows_out, inner_out, lse, branch_out,
    dom, do_rows, delta, dup,
    raw, normed, w, own_g, own_w, sums, landed, qm, kv, rows, inner, slope, send, recv, local,
):
    at = place()
    z, xh, y, xl, c = at
    stages = stage_peers(at)
    net, near = Net(send, recv), Local(local)
    greet([peer for stage in stages for peer in stage])
    weights = [WeightGather(net, at, w, kind) for kind in range(KINDS)]
    tokens = TokenGather(net, at, raw)
    grads = TokenGather(net, at, gb_ref)
    blocks = (aw_ref, ew_ref, cw_ref)
    kept, own_copies = [], []

    def unit_of(i):
        return lax.rem(y + lax.rem(i, 4), 4) * 2 + lax.rem(xl + i // 4, 2)

    def cast_own(kind):
        own_w[kind] = blocks[kind][...].astype(bf16)
        weights[kind].own(own_w.at[kind])
        own_copies.append(near.go(own_w.at[kind], weights[kind].rows(0, 0)))

    staged = Staged(net, stages, sums, landed)
    sums[0] = norm_ref[...]
    staged.start()
    cast_own(0)
    own = tokens.rows(0, 0)

    @pl.loop(0, ROWS // 16)
    def _(i):
        part = pl.ds(pl.multiple_of(i * 16, 16), 16)
        x = x_ref[part]
        centred = x - jnp.mean(x, axis=1, keepdims=True)
        inverse = lax.rsqrt(jnp.mean(centred * centred, axis=1, keepdims=True) + eps_norm)
        own[part] = (centred * inverse).astype(bf16)

    tokens.own(own)
    cast_own(1)
    staged.finish()
    staged.start()

    @pl.loop(0, ROWS // 16)
    def _(i):
        part = pl.ds(pl.multiple_of(i * 16, 16), 16)
        own_g[part] = ct_ref[part].astype(bf16)

    weights[0].near()
    staged.finish()
    staged.start()
    tokens.near()
    staged.finish()
    staged.start()
    weights[1].near()
    weights[0].far()
    tokens.far()
    grads.own(own_g)
    kept.append(near.go(own_g, grads.rows(0, 0)))
    staged.finish()
    gain_out[...] = sums[4]
    gain, bias = spread(sums[4])
    weights[0].end()
    for copy in own_copies:
        copy.wait()
    q_rows, k_rows, v_rows = rows.at[0], rows.at[1], rows.at[2]

    def tokens_in(start, stop):
        @pl.loop(start, stop)
        def _(i):
            affine_unit(unit_of(i), raw, normed, gain, bias)
            qkv_unit(unit_of(i), normed, w, table, qm, kv, q_rows, k_rows, v_rows)

    tokens.end(*EARLY)
    tokens_in(0, 5)
    weights[1].far()
    own_copies.clear()
    cast_own(2)
    tokens.rest()
    tokens.end(*LATE)
    tokens_in(5, 8)
    kept.append(near.go(normed, normed_out))
    kept += [near.go(qm, qm_out), near.go(kv, kv_out), near.go(rows, rows_out)]
    weights[1].end()
    kept.append(near.go(w.at[pl.ds(0, FIRST)], w_out))
    attend_block(0, qm, kv, k_rows, inner, lse)
    attend_block(1, qm, kv, k_rows, inner, lse)
    weights[2].near()
    attend_block(2, qm, kv, k_rows, inner, lse)
    grads.near()
    attend_block(3, qm, kv, k_rows, inner, lse)

    @pl.loop(0, 4)
    def _(i):
        up_unit(i, normed, w, inner, slope)

    grads.far()
    weights[2].far()

    @pl.loop(4, 8)
    def _(i):
        up_unit(i, normed, w, inner, slope)

    weights[2].end()
    for copy in own_copies:
        copy.wait()
    kept.append(near.go(inner, inner_out))
    tokens.clear()

    @pl.loop(0, 8)
    def _(i):
        branch_unit(i, inner, w, raw)

    kept.append(near.go(raw, branch_out))
    kept.pop(1).wait()
    kept.pop(0).wait()

    def grads_in(start, stop):
        loads = []
        for i in range(start, stop):
            part = at_unit(unit_of(i))
            loads.append(near.go(gb_ref.at[part], normed.at[part]))
        for load in loads:
            load.wait()

        @pl.loop(start, stop)
        def _(i):
            back_unit(unit_of(i), normed, w, inner, slope, dom, do_rows, delta, dup)

    grads.end(*EARLY)
    grads_in(0, 5)
    grads.rest()
    grads.end(*LATE)
    grads_in(5, 8)
    grads.clear()
    net.drain()
    for copy in kept:
        copy.wait()


def gather(x, ct, aw, ew, cw, norm_rows, table):
    any_ref = pl.BlockSpec(memory_space=pl.ANY)
    vmem = pl.BlockSpec(memory_space=pltpu.VMEM)
    shape = jax.ShapeDtypeStruct
    outs = [
        (shape((LENGTH, D), bf16), any_ref),
        (shape((LENGTH, D), bf16), any_ref),
        (shape((FIRST, D), bf16), any_ref),
        (shape((8, 512), f32), vmem),
        (shape((2, 128, LENGTH), bf16), any_ref),
        (shape((256, LENGTH), bf16), any_ref),
        (shape((3, LENGTH, 128), bf16), any_ref),
        (shape((SECOND, LENGTH), bf16), any_ref),
        (shape((8, LENGTH), f32), vmem),
        (shape((LENGTH, D), bf16), any_ref),
        (shape((2, 128, LENGTH), bf16), vmem),
        (shape((LENGTH, 128), bf16), vmem),
        (shape((8, LENGTH), f32), vmem),
        (shape((HIDDEN, LENGTH), bf16), vmem),
    ]
    return pl.pallas_call(
        gather_kernel,
        name="gather",
        out_shape=[out for out, _ in outs],
        in_specs=[vmem] * 7,
        out_specs=[spec for _, spec in outs],
        scratch_shapes=[
            pltpu.VMEM((LENGTH, D), bf16),
            pltpu.VMEM((LENGTH, D), bf16),
            pltpu.VMEM((WALL, D), bf16),
            pltpu.VMEM((ROWS, D), bf16),
            pltpu.VMEM((KINDS, WROWS, D), bf16),
            pltpu.VMEM((5, 8, 512), f32),
            pltpu.VMEM((10, 8, 512), f32),
            pltpu.VMEM((2, 128, LENGTH), bf16),
            pltpu.VMEM((256, LENGTH), bf16),
            pltpu.VMEM((3, LENGTH, 128), bf16),
            pltpu.VMEM((SECOND, LENGTH), bf16),
            pltpu.VMEM((HIDDEN, LENGTH), f32),
            pltpu.SemaphoreType.DMA((80,)),
            pltpu.SemaphoreType.DMA((80,)),
            pltpu.SemaphoreType.DMA((24,)),
        ],
        compiler_params=pltpu.CompilerParams(
            collective_id=1, has_side_effects=True, vmem_limit_bytes=60 << 20
        ),
    )(x, ct, aw, ew, cw, norm_rows, table)


def add_rows(count, put, *refs):
    @pl.loop(0, count // 16)
    def _(i):
        part = pl.ds(pl.multiple_of(i * 16, 16), 16)
        total = refs[0][part].astype(f32)
        for ref in refs[1:]:
            total = total + ref[part].astype(f32)
        put(part, total)


def add_into(count, out, *refs):
    def put(part, total):
        out[part] = total.astype(out.dtype)

    add_rows(count, put, *refs)


PLACES = [(0, 0), (-1, 0), (1, 0), (2, 0), (0, 1), (-1, 1), (1, 1), (2, 1)]


class TokenScatter:
    def __init__(self, net, near, at, part, mine, sibs, landed, out):
        self.net, self.near, self.at, self.part = net, near, at, part
        self.mine, self.sibs, self.landed, self.out = mine, sibs, landed, out
        z, xh, y, xl, c = at
        self.xpart = device(z, xh, y, 1 - xl, c)
        self.yp = device(z, xh, y + 1, xl, c)
        self.ym = device(z, xh, y - 1, xl, c)
        self.sib = device(z, xh, y, xl, 1 - c)
        self.loads, self.swaps = {}, {}

    def slot(self, dy, dx):
        return PLACES.index((dy, dx))

    def swap(self, dy, dx):
        z, xh, y, xl, c = self.at
        x, slot = (xl if dx == 0 else 1 - xl), self.slot(dy, dx)
        self.swaps[slot] = self.net.go(
            self.part.at[token_rows(y + dy, x, 1 - c)], self.sibs.at[slot], self.sib
        )
        self.loads[slot] = self.near.go(
            self.part.at[token_rows(y + dy, x, c)], self.mine.at[slot]
        )

    def swap_all(self):
        for dy, dx in ((2, 1), (-1, 1), (1, 1), (2, 0), (-1, 0), (1, 0), (0, 1), (0, 0)):
            self.swap(dy, dx)

    def ready(self, dy, dx, *more):
        slot = self.slot(dy, dx)
        self.loads[slot].wait()
        self.swaps[slot].wait_recv()
        add_into(ROWS, self.mine.at[slot], self.mine.at[slot], self.sibs.at[slot], *more)
        return self.mine.at[slot]

    def send(self, src, slot, peer, start=0, size=ROWS):
        return self.net.go(src, self.landed.at[slot, pl.ds(start, size)], peer)

    def far(self):
        self.xo = self.send(self.ready(2, 1), 0, self.xpart)
        self.lp = self.send(self.ready(-1, 1), 1, self.ym)
        self.rp = self.send(self.ready(1, 1), 2, self.yp)

    def opposite(self):
        self.xo.wait_recv()
        block = self.ready(2, 0, self.landed.at[0])
        self.a = self.send(block.at[pl.ds(0, 64)], 3, self.ym, 0, 64)
        self.b = self.send(block.at[pl.ds(64, 64)], 3, self.yp, 64, 64)

    def near_left(self):
        block = self.ready(-1, 0)
        self.a.wait_recv()
        top = pl.ds(0, 64)
        add_into(64, block.at[top], block.at[top], self.landed.at[3, top])
        self.l = self.send(block, 4, self.ym)

    def near_right(self):
        block = self.ready(1, 0)
        self.b.wait_recv()
        low = pl.ds(64, 64)
        add_into(64, block.at[low], block.at[low], self.landed.at[3, low])
        self.r = self.send(block, 5, self.yp)

    def partner(self):
        self.lp.wait_recv()
        self.rp.wait_recv()
        block = self.ready(0, 1, self.landed.at[1], self.landed.at[2])
        self.p = self.send(block, 6, self.xpart)

    def final(self):
        self.l.wait_recv()
        self.r.wait_recv()
        self.p.wait_recv()
        slot = self.slot(0, 0)
        self.loads[slot].wait()
        self.swaps[slot].wait_recv()
        add_into(
            ROWS, self.out, self.mine.at[slot], self.sibs.at[slot],
            self.landed.at[4], self.landed.at[5], self.landed.at[6],
        )


class WeightScatter:
    def __init__(self, net, at, part, kind, landed, out):
        self.net, self.at, self.part, self.kind = net, at, part, kind
        self.landed, self.out = landed, out
        z, xh, y, xl, c = at
        self.hpart = device(z, 1 - xh, y, xl, c)
        self.zp = device(z + 1, xh, y, xl, c)
        self.zm = device(z - 1, xh, y, xl, c)

    def rows(self, dz, dh, start=0, size=WROWS):
        z, xh = self.at[:2]
        return self.part.at[
            weight_rows(self.kind, z + dz, xh if dh == 0 else 1 - xh, start, size)
        ]

    def send(self, src, slot, peer, start=0, size=WROWS):
        return self.net.go(src, self.landed.at[slot, pl.ds(start, size)], peer)

    def opposite(self):
        self.a, self.b = [], []
        for dh in (0, 1):
            self.a.append(self.send(self.rows(2, dh, 0, 32), dh, self.zm, 0, 32))
            self.b.append(self.send(self.rows(2, dh, 32, 32), dh, self.zp, 32, 32))

    def near(self):
        self.l, self.r = [], []
        for dh in (1, 0):
            self.a[dh].wait_recv()
            half = self.rows(-1, dh, 0, 32)
            add_into(32, half, half, self.landed.at[dh, pl.ds(0, 32)])
            self.l.append(self.send(self.rows(-1, dh), 2 + dh, self.zm))
            self.b[dh].wait_recv()
            half = self.rows(1, dh, 32, 32)
            add_into(32, half, half, self.landed.at[dh, pl.ds(32, 32)])
            self.r.append(self.send(self.rows(1, dh), 4 + dh, self.zp))

    def partner(self):
        self.l[0].wait_recv()
        self.r[0].wait_recv()
        other = self.rows(0, 1)
        add_into(WROWS, other, other, self.landed.at[3], self.landed.at[5])
        self.p = self.send(other, 6, self.hpart)

    def final(self):
        self.l[1].wait_recv()
        self.r[1].wait_recv()
        self.p.wait_recv()
        add_into(
            WROWS, self.out, self.rows(0, 0),
            self.landed.at[2], self.landed.at[4], self.landed.at[6],
        )


def scatter_kernel(
    branch_ref, dnormed_ref, wgrad_ref,
    branch_out, dnormed_out, wgrad_out,
    mine, sibs, landed, wpart, wlanded, send, recv, local,
):
    at = place()
    z, xh, y, xl, c = at
    net, near = Net(send, recv), Local(local)
    greet(
        [
            device(z, xh, y, 1 - xl, c),
            device(z, xh, y, xl, 1 - c),
            device(z, xh, y + 1, xl, c),
            device(z, xh, y - 1, xl, c),
            device(z + 1, xh, y, xl, c),
            device(z - 1, xh, y, xl, c),
            device(z, 1 - xh, y, xl, c),
        ]
    )
    loads = {}
    for kind, (start, size) in ((2, (FIRST + 128, HIDDEN)), (1, (QKV, HIDDEN)), (0, (0, QKV))):
        loads[kind] = [near.go(wgrad_ref.at[pl.ds(start, size)], wpart.at[pl.ds(start, size)])]
    loads[0].append(near.go(wgrad_ref.at[pl.ds(FIRST, 128)], wpart.at[pl.ds(FIRST, 128)]))
    tokens = [
        TokenScatter(net, near, at, part, mine.at[k], sibs.at[k], landed.at[k], out)
        for k, (part, out) in enumerate(((branch_ref, branch_out), (dnormed_ref, dnormed_out)))
    ]
    weights = [
        WeightScatter(net, at, wpart, kind, wlanded.at[kind], wgrad_out.at[kind])
        for kind in range(KINDS)
    ]
    branch, dnormed = tokens
    branch.swap_all()
    for kind in (2, 1, 0):
        for load in loads[kind]:
            load.wait()
        weights[kind].opposite()
    dnormed.swap_all()
    branch.far()
    weights[2].near()
    branch.opposite()
    branch.near_left()
    branch.near_right()
    weights[1].near()
    dnormed.far()
    dnormed.opposite()
    weights[0].near()
    branch.partner()
    dnormed.near_left()
    dnormed.near_right()
    for kind in (2, 1, 0):
        weights[kind].partner()
    branch.final()
    dnormed.partner()
    for kind in (2, 1, 0):
        weights[kind].final()
    dnormed.final()
    net.drain()


def scatter(branch, dnormed, wgrad):
    any_ref = pl.BlockSpec(memory_space=pl.ANY)
    vmem = pl.BlockSpec(memory_space=pltpu.VMEM)
    return pl.pallas_call(
        scatter_kernel,
        name="scatter",
        out_shape=(
            jax.ShapeDtypeStruct((ROWS, D), f32),
            jax.ShapeDtypeStruct((ROWS, D), f32),
            jax.ShapeDtypeStruct((KINDS, WROWS, D), f32),
        ),
        in_specs=[any_ref] * 3,
        out_specs=(vmem,) * 3,
        scratch_shapes=[
            pltpu.VMEM((2, 8, ROWS, D), bf16),
            pltpu.VMEM((2, 8, ROWS, D), bf16),
            pltpu.VMEM((2, 7, ROWS, D), bf16),
            pltpu.VMEM((WALL, D), bf16),
            pltpu.VMEM((KINDS, 7, WROWS, D), bf16),
            pltpu.SemaphoreType.DMA((80,)),
            pltpu.SemaphoreType.DMA((80,)),
            pltpu.SemaphoreType.DMA((24,)),
        ],
        compiler_params=pltpu.CompilerParams(
            collective_id=2, has_side_effects=True, vmem_limit_bytes=58 << 20
        ),
    )(branch, dnormed, wgrad)


def norm_sum_kernel(part_ref, out_ref, sums, landed, send, recv):
    stages = stage_peers(place())
    net = Net(send, recv)
    greet([peer for stage in stages for peer in stage])
    sums[0] = part_ref[...]
    staged = Staged(net, stages, sums, landed)
    for _ in stages:
        staged.start()
        staged.finish()
    out_ref[...] = sums[4]
    net.drain()


def norm_sum(part):
    vmem = pl.BlockSpec(memory_space=pltpu.VMEM)
    return pl.pallas_call(
        norm_sum_kernel,
        name="norm_sum",
        out_shape=jax.ShapeDtypeStruct((8, 512), f32),
        in_specs=[vmem],
        out_specs=vmem,
        scratch_shapes=[
            pltpu.VMEM((5, 8, 512), f32),
            pltpu.VMEM((10, 8, 512), f32),
            pltpu.SemaphoreType.DMA((10,)),
            pltpu.SemaphoreType.DMA((10,)),
        ],
        compiler_params=pltpu.CompilerParams(collective_id=3, has_side_effects=True),
    )(part)


def attend_back_kernel(qm, kv, rows, dom, do_rows, lse, delta, table, outer, dq):
    for kb in range(LENGTH // QB):
        attend_back_block(
            kb, qm, kv, rows.at[0], rows.at[1], rows.at[2], dom, do_rows, lse, delta, dq, outer, table
        )
    query_back(dq, outer, table)


def attend_back(*args):
    vmem = pl.BlockSpec(memory_space=pltpu.VMEM)
    return pl.pallas_call(
        attend_back_kernel,
        name="attend_back",
        out_shape=jax.ShapeDtypeStruct((QKV, LENGTH), bf16),
        in_specs=[vmem] * 8,
        out_specs=vmem,
        scratch_shapes=[pltpu.VMEM((128, LENGTH), f32)],
        compiler_params=pltpu.CompilerParams(vmem_limit_bytes=48 << 20),
    )(*args)


def angles(positions, half):
    freq = rope_base ** (-2.0 * jnp.arange(half, dtype=jnp.float32) / (2 * half))
    turned = positions[:, None] * freq[None, :]
    return jnp.cos(turned), jnp.sin(turned)


def polish(moment):
    size = jnp.sqrt(jnp.sum(moment * moment, axis=(1, 2), keepdims=True)) + 1e-07
    current = moment / size

    def times(a, b):
        return jnp.einsum("bij,bjk->bik", a, b, precision=highest)

    gram = jnp.einsum("bij,bkj->bik", current, current, precision=highest)
    whole = jnp.eye(HD, dtype=f32)[None]
    for turn in range(NS_STEPS):
        factor = (
            polish_a * jnp.eye(HD, dtype=f32)[None] + polish_b * gram + polish_c * times(gram, gram)
        )
        whole = factor if turn == 0 else times(factor, whole)
        if turn < NS_STEPS - 1:
            gram = times(factor, times(gram, factor))
    return times(whole, current)


def body(
    inputs, cotangent, attn_weight, expand_weight, contract_weight, norm_params,
    attn_moment, expand_moment, contract_moment, norm_first, norm_second,
):
    index = (lax.axis_index("fsdp") * 8 + lax.axis_index("seq")) * 4 + lax.axis_index("mp")
    mine = (jnp.arange(D, dtype=jnp.int32) // 16) == index
    norm_rows = jnp.where(mine[None], jnp.tile(norm_params[0], (1, 128)), 0.0).reshape(8, 512)
    cosine, sine = angles(jnp.arange(LENGTH, dtype=f32), ROT // 2)
    table = jnp.concatenate([cosine.T, sine.T], axis=0)
    (
        normed, grad_group, first_w, norm_rows, qm, kv, rows, inner, lse, branch,
        dom, do_rows, delta, dup,
    ) = gather(
        inputs,
        cotangent,
        attn_weight[0, 0],
        expand_weight[0],
        contract_weight[0],
        norm_rows,
        table,
    )
    gain = norm_rows.reshape(2, D)[0]
    attn_back = attend_back(qm, kv, rows, dom, do_rows, lse, delta, table)
    outer = jnp.concatenate([attn_back, dup], axis=0)
    second_part = jnp.dot(inner, grad_group, preferred_element_type=f32)
    first_part = jnp.dot(outer, normed, preferred_element_type=f32)
    grad_normed = lax.dot_general(outer, first_w, tn, preferred_element_type=f32).astype(bf16)
    parts = jnp.concatenate([first_part, second_part], axis=0).astype(bf16)
    branch, hidden_gradient, shares = scatter(branch, grad_normed, parts)

    state = inputs + branch
    feature_mean = jnp.mean(inputs, axis=-1, keepdims=True)
    centered_input = inputs - feature_mean
    inverse_deviation = lax.rsqrt(
        jnp.mean(centered_input * centered_input, axis=-1, keepdims=True) + eps_norm
    )
    normalized_input = centered_input * inverse_deviation
    norm_part = jnp.stack(
        [jnp.sum(hidden_gradient * normalized_input, axis=0), jnp.sum(hidden_gradient, axis=0)],
        axis=0,
    )
    scaled = hidden_gradient * gain
    grad_state = cotangent + inverse_deviation * (
        scaled
        - jnp.mean(scaled, axis=-1, keepdims=True)
        - normalized_input * jnp.mean(scaled * normalized_input, axis=-1, keepdims=True)
    )
    norm_total = norm_sum(norm_part.reshape(8, 512)).reshape(2, D)
    norm_share = lax.dynamic_slice(norm_total, (0, index * 16), (2, 16))[None]

    moments = jnp.stack([attn_moment[0, 0], expand_moment[0], contract_moment[0]])
    moments = muon_beta * moments + shares
    ortho = polish(moments)
    updates = []
    for k, weight in enumerate((attn_weight, expand_weight, contract_weight)):
        shape = weight.shape
        new = weight - muon_rate * (
            muon_decay * weight + 0.2 * math.sqrt(D) * ortho[k].reshape(shape)
        )
        updates += [shares[k].reshape(shape), moments[k].reshape(shape), new]
    first_next = adam_first * norm_first + (1.0 - adam_first) * norm_share
    second_next = adam_second * norm_second + (1.0 - adam_second) * norm_share * norm_share
    first_fix = 1.0 - adam_first**STEP
    second_fix = 1.0 - adam_second**STEP
    norm_next = norm_params - adam_rate * (first_next / first_fix) / (
        jnp.sqrt(second_next / second_fix) + adam_eps
    )
    return (state, grad_state, *updates, norm_share, first_next, second_next, norm_next)


def solution(mesh):
    return jax.shard_map(
        body,
        mesh=mesh,
        in_specs=(
            P(("fsdp", "seq", "mp"), None),
            P(("fsdp", "seq", "mp"), None),
            P(None, ("fsdp", "seq", "mp"), None, None),
            P(None, ("fsdp", "seq", "mp"), None),
            P(None, ("fsdp", "seq", "mp"), None),
            P(None, None, ("fsdp", "seq", "mp")),
            P(None, ("fsdp", "seq", "mp"), None, None),
            P(None, ("fsdp", "seq", "mp"), None),
            P(None, ("fsdp", "seq", "mp"), None),
            P(None, None, ("fsdp", "seq", "mp")),
            P(None, None, ("fsdp", "seq", "mp")),
        ),
        out_specs=(
            P(("fsdp", "seq", "mp"), None),
            P(("fsdp", "seq", "mp"), None),
            P(None, ("fsdp", "seq", "mp"), None, None),
            P(None, ("fsdp", "seq", "mp"), None, None),
            P(None, ("fsdp", "seq", "mp"), None, None),
            P(None, ("fsdp", "seq", "mp"), None),
            P(None, ("fsdp", "seq", "mp"), None),
            P(None, ("fsdp", "seq", "mp"), None),
            P(None, ("fsdp", "seq", "mp"), None),
            P(None, ("fsdp", "seq", "mp"), None),
            P(None, ("fsdp", "seq", "mp"), None),
            P(None, None, ("fsdp", "seq", "mp")),
            P(None, None, ("fsdp", "seq", "mp")),
            P(None, None, ("fsdp", "seq", "mp")),
            P(None, None, ("fsdp", "seq", "mp")),
        ),
        check_vma=False,
    )
```

```python
import functools
import math
import types

import jax
import jax.numpy as jnp
import numpy as np
from jax import lax
from jax.experimental import pallas as pl
from jax.experimental.pallas import tpu as pltpu
from jax.sharding import PartitionSpec as P

D = 2048
H = 32
HD = 64
ROT = 32
LENGTH = 2048
NS_STEPS = 5
STEP = 10
ROWS = 128
WROWS = 64
KINDS = 3
QKV = 384
HIDDEN = 512
FIRST = QKV + HIDDEN
SECOND = 128 + HIDDEN
WALL = FIRST + SECOND

eps_norm = 1e-05
rope_base = 10000.0
muon_beta = 0.95
muon_rate = 0.15
muon_decay = 0.01
polish_a = 3.4445
polish_b = -4.775
polish_c = 2.0315
adam_first = 0.9
adam_second = 0.95
adam_rate = 0.5
adam_eps = 1e-08
masked_score = -1e30
highest = lax.Precision.HIGHEST
across = (((1,), (1,)), ((), ()))
downward = (((0,), (0,)), ((), ()))
MESH = pl.DeviceIdType.MESH
f32 = jnp.float32
bf16 = jnp.bfloat16


def place():
    z = lax.axis_index("fsdp")
    s = lax.axis_index("seq")
    m = lax.axis_index("mp")
    return z, s // 4, lax.rem(s, 4), m // 2, lax.rem(m, 2)


def device(z, xh, y, xl, c):
    return (lax.rem(z + 4, 4), xh * 4 + lax.rem(y + 4, 4), xl * 2 + c)


def token_rows(y, xl, c, start=0, size=ROWS):
    block = lax.rem(y + 4, 4) * 4 + xl * 2 + c
    return pl.ds(pl.multiple_of(block * ROWS + start, 32), size)


def weight_rows(kind, z, xh, start=0, size=WROWS):
    z = lax.rem(z + 4, 4)
    if kind == 0:
        base = z * 128 + (z // 3) * HIDDEN + xh * 64
    elif kind == 1:
        base = QKV + z * 128 + xh * 64
    else:
        base = FIRST + 128 + z * 128 + xh * 64
    return pl.ds(pl.multiple_of(base + start, 32), size)


class Net:
    def __init__(self, send, recv):
        self.send, self.recv, self.used, self.sent = send, recv, 0, []

    def go(self, src, dst, peer, sent=None):
        slot = self.used
        self.used += 1
        copy = pltpu.make_async_remote_copy(
            src_ref=src,
            dst_ref=dst,
            send_sem=self.send.at[slot],
            recv_sem=self.recv.at[slot],
            device_id=peer,
            device_id_type=MESH,
        )
        copy.start()
        (self.sent if sent is None else sent).append(copy)
        return copy

    def drain(self):
        for copy in self.sent:
            copy.wait_send()
        self.sent = []


class Local:
    def __init__(self, sems):
        self.sems, self.used = sems, 0

    def go(self, src, dst):
        copy = pltpu.make_async_copy(src, dst, self.sems.at[self.used])
        self.used += 1
        copy.start()
        return copy


def greet(peers):
    barrier = pltpu.get_barrier_semaphore()
    for peer in peers:
        pl.semaphore_signal(barrier, inc=1, device_id=peer, device_id_type=MESH)
    return lambda: pl.semaphore_wait(barrier, len(peers))


def stage_peers(at):
    z, xh, y, xl, c = at
    return [
        [device(z + k, xh, y, xl, c) for k in (1, 2, 3)],
        [device(z, xh, y + k, xl, c) for k in (1, 2, 3)],
        [
            device(z, xh, y, 1 - xl, c),
            device(z, 1 - xh, y, xl, c),
            device(z, 1 - xh, y, 1 - xl, c),
        ],
        [device(z, xh, y, xl, 1 - c)],
    ]


class Staged:
    def __init__(self, net, stages, sums, landed):
        self.net, self.stages, self.sums, self.landed = net, stages, sums, landed
        self.stage = self.slot = 0

    def start(self):
        self.copies = [
            self.net.go(self.sums.at[self.stage], self.landed.at[self.slot + k], peer)
            for k, peer in enumerate(self.stages[self.stage])
        ]

    def finish(self):
        total = self.sums[self.stage]
        for copy in self.copies:
            copy.wait_recv()
            total = total + self.landed[self.slot]
            self.slot += 1
        self.stage += 1
        self.sums[self.stage] = total


def spread(flat):
    gain = jnp.concatenate([flat[k : k + 1] for k in range(4)], axis=1)
    bias = jnp.concatenate([flat[k : k + 1] for k in range(4, 8)], axis=1)
    return gain, bias


class TokenGather:
    def __init__(self, net, at, full, around):
        self.net, self.at, self.full, self.sent, self.got = net, at, full, [], {}
        self.waited = set()
        self.around = around
        z, xh, y, xl, c = at
        self.x = device(z, xh, y, 1 - xl, c)
        self.p = device(z, xh, y + 1, xl, c)
        self.m = device(z, xh, y - 1, xl, c)
        self.s = device(z, xh, y, xl, 1 - c)

    def rows(self, dy, dx, half=None):
        z, xh, y, xl, c = self.at
        start, size = (0, ROWS) if half is None else ((0, 64), (64, 64), (64, 32), (96, 32))[half]
        return self.full.at[token_rows(y + dy, xl if dx == 0 else 1 - xl, c, start, size)]

    def go(self, name, peer, dy, dx, half=None, block=None):
        here = self.rows(dy, dx, half)
        src = here
        if block is not None:
            src = block if half is None else block.at[pl.ds(half * 64, 64)]
        self.got[name] = self.net.go(src, here, peer, self.sent)

    def wait(self, *names):
        for name in names:
            if name not in self.waited:
                self.got[name].wait_recv()
                self.waited.add(name)

    def clear(self):
        for copy in self.sent:
            copy.wait_send()

    def steps(self, tag, block):
        go, wait = self.go, self.wait

        def own1():
            go("l1", self.p, 0, 0, 0, block)
            go("r1", self.m, 0, 0, 1, block)

        def own2():
            go("l2", self.p, 0, 0, 1, block)
            go("r2", self.m, 0, 0, 0, block)
            go("s0", self.s, 0, 0, None, block)

        def ownp():
            go("p1", self.x, 0, 0, 0, block)
            go("p2", self.x, 0, 0, 1, block)

        def nl():
            wait("l1")
            go("a", self.p, -1, 0, 0)

        def nr():
            wait("r1")
            go("b", self.m, 1, 0, 1)

        def sl():
            wait("l2")
            go("s1", self.s, -1, 0)

        def sr():
            wait("r2")
            go("s2", self.s, 1, 0)

        def np1():
            wait("p1")
            go("lp1", self.p, 0, 1, 0)
            go("rp1", self.m, 0, 1, 0)

        def np2():
            wait("p2")
            go("lp2", self.p, 0, 1, 1)
            go("rp2", self.m, 0, 1, 1)
            go("s3", self.s, 0, 1)

        def fa():
            wait("a")
            go("xo1", self.x, 2, 0, 0)

        def fb():
            wait("b")
            if not self.around:
                go("xo2", self.x, 2, 0, 1)
            go("s4", self.s, 2, 0)

        def e1():
            wait("lp1", "lp2")
            if self.around:
                go("qa", self.p, -1, 1, 2)
            go("s5", self.s, -1, 1)

        def e2():
            wait("rp1", "rp2")
            if self.around:
                go("qb", self.m, 1, 1, 3)
            go("s6", self.s, 1, 1)

        def e3():
            wait("xo1", *(("qa", "qb") if self.around else ("xo2",)))
            go("s7", self.s, 2, 1)

        parts = (own1, own2, ownp, nl, nr, sl, sr, np1, np2, fa, fb, e1, e2, e3)
        return {tag + part.__name__: part for part in parts}


class WeightGather:
    def __init__(self, net, near, at, full, kind, own_w, block, load):
        self.net, self.near, self.at, self.full, self.kind, self.got = net, near, at, full, kind, {}
        self.own_w, self.block, self.load = own_w, block, load
        z, xh, y, xl, c = at
        self.h = device(z, 1 - xh, y, xl, c)
        self.p = device(z + 1, xh, y, xl, c)
        self.m = device(z - 1, xh, y, xl, c)

    def rows(self, dz, dh, half=None):
        z, xh = self.at[:2]
        start, size = (0, WROWS) if half is None else (half * 32, 32)
        return self.full.at[
            weight_rows(self.kind, z + dz, xh if dh == 0 else 1 - xh, start, size)
        ]

    def go(self, name, peer, dz, dh, half, own=False):
        here = self.rows(dz, dh, half)
        src = self.own_w.at[pl.ds(half * 32, 32)] if own else here
        self.got[name] = self.net.go(src, here, peer)

    def wait(self, *names):
        for name in names:
            self.got[name].wait_recv()

    def steps(self):
        go, wait = self.go, self.wait

        def own():
            if self.load is not None:
                self.load.wait()
            self.own_w[...] = self.block[...].astype(bf16)
            go("l1", self.p, 0, 0, 0, True)
            go("r1", self.m, 0, 0, 1, True)
            go("l2", self.p, 0, 0, 1, True)
            go("r2", self.m, 0, 0, 0, True)
            self.copy = self.near.go(self.own_w, self.rows(0, 0))

        def ownp():
            go("p1", self.h, 0, 0, 0, True)
            go("p2", self.h, 0, 0, 1, True)

        def na():
            wait("l1", "r1")
            go("a", self.p, -1, 0, 0)
            go("b", self.m, 1, 0, 1)

        def np1():
            wait("p1")
            go("lp1", self.p, 0, 1, 0)
            go("rp1", self.m, 0, 1, 0)

        def np2():
            wait("p2")
            go("rp2", self.m, 0, 1, 1)
            go("lp2", self.p, 0, 1, 1)

        def fl():
            wait("lp1")
            go("ha", self.p, -1, 1, 0)

        def fr():
            wait("rp2")
            go("hb", self.m, 1, 1, 1)

        def end():
            wait("l2", "r2", "a", "b", "lp2", "rp1", "ha", "hb")
            self.copy.wait()

        parts = (own, ownp, na, np1, np2, fl, fr, end)
        return {f"W{self.kind}" + part.__name__: part for part in parts}


nn = (((1,), (0,)), ((), ()))
nt = (((1,), (1,)), ((), ()))
tn = (((0,), (0,)), ((), ()))
QB = 512
UNIT = 256


def dot(a, b, dims):
    return lax.dot_general(a, b, dims, preferred_element_type=f32)


def at_unit(unit, size=UNIT):
    return pl.ds(pl.multiple_of(unit * size, size), size)


def turn(part, cosine, sine):
    rows = []
    for low in (0, HD):
        first, second = part[low : low + 16], part[low + 16 : low + 32]
        rows += [first * cosine - second * sine, second * cosine + first * sine]
        rows.append(part[low + 32 : low + HD])
    return jnp.concatenate(rows, axis=0)


def of_head(h, block, axis):
    place = lax.broadcasted_iota(jnp.int32, block.shape, axis)
    return jnp.where((place < HD) == (h == 0), block, 0.0)


def gelu_pair(v):
    square = v * v
    t = jnp.tanh(math.sqrt(2 / math.pi) * (v + 0.044715 * (v * square)))
    plus = 0.5 * (1.0 + t)
    slope = plus + (0.5 * v) * (1.0 - t * t) * (
        math.sqrt(2 / math.pi) * (1.0 + 3 * 0.044715 * square)
    )
    return v * plus, slope


def split(a):
    high = a.astype(bf16)
    return high, (a - high.astype(f32)).astype(bf16)


def times(a, b):
    (ah, al), (bh, bl) = split(a), split(b)
    return dot(
        jnp.concatenate([ah, ah, al, al], axis=1), jnp.concatenate([bh, bl, bh, bl], axis=0), nn
    )


def scale_weights(start, size, w, scaled, shift, affine):
    high, low = split(affine[1:2])
    pair = jnp.concatenate([high, low] * 8, axis=0)
    by_bias = dot(w[pl.ds(start, size)], pair, nt)
    shift[pl.ds(start, size)] = by_bias[:, 0:1] + by_bias[:, 1:2]

    @pl.loop(0, size // 32)
    def _(i):
        part = pl.ds(pl.multiple_of(start + i * 32, 32), 32)
        scaled[part] = (w[part].astype(f32) * affine[0:1]).astype(bf16)


def qkv_unit(unit, raw, w, shift, table, qm, kv, q_rows, k_rows, v_rows):
    cols = at_unit(unit)
    lin = dot(w[pl.ds(0, QKV)], raw[cols], nt) + shift[0:QKV]
    cosine, sine = table[0:16, cols], table[16:32, cols]
    q = turn(lin[0:128], cosine, sine).astype(bf16).astype(f32) * HD**-0.5
    k = turn(lin[128:256], cosine, sine)
    v = lin[256:384]
    for h in range(2):
        qm[h, :, cols] = of_head(h, q, 0).astype(bf16)
    kv[pl.ds(0, 128), cols] = k.astype(bf16)
    kv[pl.ds(128, 128), cols] = v.astype(bf16)
    q_rows[cols] = q.T.astype(bf16)
    k_rows[cols] = k.T.astype(bf16)
    v_rows[cols] = v.T.astype(bf16)


def up_unit(unit, raw, w, shift, inner, slope):
    cols = at_unit(unit, 2 * UNIT)
    act, der = gelu_pair(dot(w[pl.ds(QKV, HIDDEN)], raw[cols], nt) + shift[pl.ds(QKV, HIDDEN)])
    inner[pl.ds(128, HIDDEN), cols] = act.astype(bf16)
    slope[:, cols] = der


def branch_unit(unit, inner, w, out):
    rows = at_unit(unit, 2 * UNIT)
    out[rows] = dot(inner[:, rows], w[pl.ds(FIRST, SECOND)], tn).astype(bf16)


def back_unit(cols, gb, w, inner, slope, dom, do_rows, delta, dup):
    lin = dot(w[pl.ds(FIRST, SECOND)], gb[cols], nt)
    do = lin[0:128].astype(bf16).astype(f32)
    for h in range(2):
        dom[h, :, cols] = of_head(h, do, 0).astype(bf16)
    do_rows[cols] = do.T.astype(bf16)
    both = do * inner[pl.ds(0, 128), cols].astype(f32)
    for h in range(2):
        delta[pl.ds(h, 1), cols] = jnp.sum(both[h * HD : h * HD + HD], axis=0, keepdims=True)
    dup[:, cols] = (lin[128:] * slope[:, cols]).astype(bf16)


def causal_mask(scores):
    rows = lax.broadcasted_iota(jnp.int32, scores.shape, 0)
    cols = lax.broadcasted_iota(jnp.int32, scores.shape, 1)
    return jnp.where(rows <= cols, scores, masked_score)


def attend_block(qb, qm, kv, k_rows, inner, lse):
    cols = at_unit(qb, QB)
    start = (jnp.full((1, QB), masked_score, f32), jnp.zeros((1, QB), f32), jnp.zeros((HD, QB), f32))

    def step(kb, carry, masked):
        keys = at_unit(kb, QB)
        k = k_rows[keys]
        result = []
        for h in range(2):
            top, total, out = carry[h]
            scores = dot(k, qm[h, :, cols], nn)
            if masked:
                scores = causal_mask(scores)
            high = jnp.maximum(top, jnp.max(scores, axis=0, keepdims=True))
            scale = jnp.exp(top - high)
            expo = jnp.exp(scores - high)
            total = total * scale + jnp.sum(expo, axis=0, keepdims=True)
            out = out * scale + dot(kv[pl.ds(128 + h * HD, HD), keys], expo.astype(bf16), nn)
            result.append((high, total, out))
        return tuple(result)

    carry = lax.fori_loop(0, qb, lambda kb, c: step(kb, c, False), (start, start))
    carry = step(qb, carry, True)
    for h in range(2):
        top, total, out = carry[h]
        inner[pl.ds(h * HD, HD), cols] = (out / total).astype(bf16)
        lse[pl.ds(h, 1), cols] = top + jnp.log(total)


def attend_back_block(kb, qm, kv, q_rows, k_rows, v_rows, dom, do_rows, lse, delta, dq, outer, table):
    keys = pl.ds(kb * QB, QB)

    def step(keys, cols, carry, masked, fresh=False):
        k, v = k_rows[keys], v_rows[keys]
        result = []
        for h in range(2):
            dk, dv = carry[h]
            scores = dot(k, qm[pl.ds(h * 128, 128), cols], nn)
            if masked:
                scores = causal_mask(scores)
            probs = jnp.exp(scores - lse[pl.ds(h, 1), cols])
            dp = dot(v, dom[h, :, cols], nn)
            ds = (probs * (dp - delta[pl.ds(h, 1), cols])).astype(bf16)
            dv = dv + dot(probs.astype(bf16), do_rows[cols], nn)
            dk = dk + dot(ds, q_rows[cols], nn)
            half = pl.ds(h * HD, HD)
            part = dot(kv[half, keys], ds, nn)
            if fresh:
                dq[half, cols] = part
            else:
                dq[half, cols] += part
            result.append((dk, dv))
        return tuple(result)

    small = QB // 2
    low, high = pl.ds(kb * QB, small), pl.ds(kb * QB + small, small)
    zero = jnp.zeros((small, 128), f32)
    start = ((zero, zero), (zero, zero))
    first = step(low, keys, start, True, kb == 0)
    second = step(high, high, start, True)
    carry = jax.tree.map(lambda a, b: jnp.concatenate([a, b], axis=0), first, second)
    carry = lax.fori_loop(
        kb + 1, LENGTH // QB, lambda qb, c: step(keys, at_unit(qb, QB), c, False, kb == 0), carry
    )
    (dk0, dv0), (dk1, dv1) = carry
    first = lax.broadcasted_iota(jnp.int32, (QB, 128), 1) < HD
    dk = jnp.where(first, dk0, dk1).astype(bf16).astype(f32).T
    dv = jnp.where(first, dv0, dv1).T
    cosine, sine = table[0:16, keys], -table[16:32, keys]
    outer[pl.ds(128, 128), keys] = turn(dk, cosine, sine).astype(bf16)
    outer[pl.ds(256, 128), keys] = dv.astype(bf16)


def query_back(dq, outer, table):
    part = (dq[...] * HD**-0.5).astype(bf16).astype(f32)
    outer[pl.ds(0, 128)] = turn(part, table[0:16], -table[16:32]).astype(bf16)


PLACES = [(0, 0), (-1, 0), (1, 0), (0, 1), (2, 0), (-1, 1), (1, 1), (2, 1)]


def slot(dy, dx):
    return dy % 4 + 4 * dx


def add_into(count, out, *refs):
    wide = f32 if len(refs) > 2 else out.dtype

    @pl.loop(0, count // 16)
    def _(i):
        part = pl.ds(pl.multiple_of(i * 16, 16), 16)
        total = refs[0][part].astype(wide)
        for ref in refs[1:]:
            total = total + ref[part].astype(wide)
        out[part] = total.astype(out.dtype)


GROUPS = (((0, 0),), ((-1, 0), (1, 0)), ((0, 1),), ((2, 0),), ((-1, 1), (1, 1)), ((2, 1),))

GRAD_GROUPS = tuple(((dy, 0), (dy, 1)) for dy in (0, 1, 2, -1))


def gather_order(s):
    return (
        s.W0own, s.W0ownp, s.Town1, s.W0np1, s.Town2, s.st0, s.Townp, s.W0np2, s.W0na, s.W0fl, s.st1,
        s.Tnr, s.W0fr, s.W1own, s.Tnl, s.st2, s.Tsl, s.Tnp1, s.W1ownp, s.st3, s.Tnp2, s.Tsr, s.W0end,
        s.st4, s.wg0, s.W1np1, s.Tfa, s.Tfb, s.q0, s.q2, s.q3, s.W1np2, s.q1, s.W1na, s.W1fl, s.Te2,
        s.W1fr, s.W2own, s.Gown1, s.W2ownp, s.Te1, s.Gownp, s.Gown2, s.q4, s.Te3, s.W1end, s.wc, s.wg1,
        s.u0, s.Gnr, s.W2np1, s.u2, s.W2np2, s.Gnl, s.q5, s.qc, s.W2na, s.at1, s.u3, s.u1, s.W2fl,
        s.Gsr, s.clear, s.Gnp1, s.W2fr, s.Gsl, s.at2, s.Gfa, s.at3, s.Gfb, s.at0, s.ic, s.Gnp2,
        s.W2end, s.b1, s.b3, s.b0, s.k0, s.sa1, s.sa3, s.Ge1, s.Ge2, s.b2, s.sa0, s.Ge3, s.k3, s.k1,
        s.k2, s.sa2,
    )


def gather_kernel(
    x_ref, ct_ref, aw_ref, ew_ref, cw_ref, norm_ref, table,
    raw_out, gb_out, w_out, gain_out, qm_out, kv_out, rows_out, inner_out, lse, branch_out,
    dom_out, do_rows_out, delta, dup_out,
    raw, gb, w, scaled, shift, own_w, sums, landed, qm, kv, rows, inner, slope, sibs, affine, ct, late, dom, do_rows, dup, send, recv, local,
):
    at = place()
    z, xh, y, xl, c = at
    stages = stage_peers(at)
    net, near = Net(send, recv), Local(local)
    met = greet([peer for stage in stages for peer in stage])
    q_rows, k_rows, v_rows = rows.at[0], rows.at[1], rows.at[2]
    kept, raw_copy, swaps = [], [], {}
    tokens = TokenGather(net, at, raw, False)
    grads = TokenGather(net, at, gb, False)
    own, own_g = tokens.rows(0, 0), grads.rows(0, 0)
    steps = tokens.steps("T", own) | grads.steps("G", own_g)
    loads = [near.go(ct_ref, ct)] + [near.go(ref, late.at[k]) for k, ref in enumerate((ew_ref, cw_ref))]
    blocks = ((aw_ref, None), (late.at[0], loads[1]), (late.at[1], loads[2]))
    for kind, (block, load) in enumerate(blocks):
        steps |= WeightGather(net, near, at, w, kind, own_w.at[kind], block, load).steps()

    def unit_of(dy, dx):
        return lax.rem(y + dy + 4, 4) * 2 + lax.rem(xl + dx, 2)

    def step(name, work, *args):
        steps[name] = functools.partial(work, *args)

    def norm_of():
        @pl.loop(0, ROWS // 16)
        def _(i):
            part = pl.ds(pl.multiple_of(i * 16, 16), 16)
            x = x_ref[part]
            centred = x - jnp.mean(x, axis=1, keepdims=True)
            inverse = lax.rsqrt(jnp.mean(centred * centred, axis=1, keepdims=True) + eps_norm)
            own[part] = (centred * inverse).astype(bf16)

    def cast_grad():
        loads[0].wait()

        @pl.loop(0, ROWS // 16)
        def _(i):
            part = pl.ds(pl.multiple_of(i * 16, 16), 16)
            own_g[part] = ct[part].astype(bf16)

    step("LN", norm_of)
    step("castG", cast_grad)
    staged = Staged(net, stages, sums, landed)

    def stage(k):
        if k > 0:
            staged.finish()
        if k < 4:
            staged.start()
        else:
            gain_out[...] = sums[4]
            gain, bias = spread(sums[4])
            affine[0:1] = gain
            affine[1:2] = bias

    for k in range(5):
        step(f"st{k}", stage, k)

    def tokens_in(k):
        for dy, dx in GROUPS[k]:
            tokens.wait(f"s{PLACES.index((dy, dx))}")
            qkv_unit(unit_of(dy, dx), raw, scaled, shift, table, qm, kv, q_rows, k_rows, v_rows)

    def up(k):
        tokens.wait(*(f"s{PLACES.index(pair)}" for pair in GRAD_GROUPS[k]))
        up_unit(lax.rem(y + k, 4), raw, scaled, shift, inner, slope)

    def copies():
        raw_copy.append(near.go(raw, raw_out))
        kept.extend([near.go(qm, qm_out), near.go(kv, kv_out), near.go(rows, rows_out)])

    def w_copy():
        kept.append(near.go(w.at[pl.ds(0, FIRST)], w_out))

    def inner_copy():
        kept.append(near.go(inner, inner_out))

    def clear():
        tokens.clear()
        raw_copy[0].wait()

    def branch(dy):
        branch_unit(lax.rem(y + dy, 4), inner, w, raw)
        for dx in range(2):
            rows = token_rows(y + dy, xl if dx == 0 else 1 - xl, 1 - c)
            swaps[dy, dx] = net.go(raw.at[rows], sibs.at[dy + 4 * dx], tokens.s)

    def branch_sum(dy):
        for dx in range(2):
            swaps[dy, dx].wait_recv()
            mine = raw.at[token_rows(y + dy, xl if dx == 0 else 1 - xl, c)]
            add_into(ROWS, mine, mine, sibs.at[dy + 4 * dx])
            kept.append(near.go(mine, branch_out.at[dy + 4 * dx]))

    def grads_in(k):
        grads.wait(*(f"s{PLACES.index(pair)}" for pair in GRAD_GROUPS[k]))
        part = at_unit(lax.rem(y + k, 4), 2 * UNIT)
        kept.append(near.go(gb.at[part], gb_out.at[part]))
        back_unit(part, gb, w, inner, slope, dom, do_rows, delta, dup)
        kept.append(near.go(dup.at[:, part], dup_out.at[:, part]))
        kept.append(near.go(do_rows.at[part], do_rows_out.at[part]))

    for k in range(6):
        step(f"q{k}", tokens_in, k)
    for k in range(4):
        step(f"k{k}", grads_in, k)
    step("wg0", scale_weights, 0, QKV, w, scaled, shift, affine)
    step("wg1", scale_weights, QKV, HIDDEN, w, scaled, shift, affine)
    for k in range(4):
        step(f"at{k}", attend_block, k, qm, kv, k_rows, inner, lse)
        step(f"u{k}", up, k)
        step(f"b{k}", branch, k)
        step(f"sa{k}", branch_sum, k)
    step("qc", copies)
    step("wc", w_copy)
    step("ic", inner_copy)
    step("clear", clear)

    rank = (z * 8 + xh * 4 + y) * 4 + xl * 2 + c
    wide = norm_ref[...]
    for _ in range(5):
        wide = jnp.concatenate([wide, wide], axis=1)
    rows_at = lax.broadcasted_iota(jnp.int32, (8, 512), 0)
    here = (lax.broadcasted_iota(jnp.int32, (8, 512), 1) // 16) == lax.rem(rank, 32)
    one = jnp.where(here & (rows_at == rank // 32), wide[0:1], 0.0)
    sums[0] = one + jnp.where(here & (rows_at == 4 + rank // 32), wide[1:2], 0.0)
    steps.pop("LN")()
    steps.pop("castG")()
    met()
    for work in gather_order(types.SimpleNamespace(**steps)):
        work()
    kept.append(near.go(dom, dom_out))
    grads.clear()
    net.drain()
    for copy in kept:
        copy.wait()


def gather(x, ct, aw, ew, cw, norm_rows, table):
    any_ref = pl.BlockSpec(memory_space=pl.ANY)
    vmem = pl.BlockSpec(memory_space=pltpu.VMEM)
    shape = jax.ShapeDtypeStruct
    outs = [
        (shape((LENGTH, D), bf16), any_ref),
        (shape((LENGTH, D), bf16), any_ref),
        (shape((FIRST, D), bf16), any_ref),
        (shape((8, 512), f32), vmem),
        (shape((2, 128, LENGTH), bf16), any_ref),
        (shape((256, LENGTH), bf16), any_ref),
        (shape((3, LENGTH, 128), bf16), any_ref),
        (shape((SECOND, LENGTH), bf16), any_ref),
        (shape((8, LENGTH), f32), vmem),
        (shape((8, ROWS, D), bf16), any_ref),
        (shape((2, 128, LENGTH), bf16), any_ref),
        (shape((LENGTH, 128), bf16), any_ref),
        (shape((8, LENGTH), f32), vmem),
        (shape((HIDDEN, LENGTH), bf16), any_ref),
    ]
    return pl.pallas_call(
        gather_kernel,
        name="gather",
        out_shape=[out for out, _ in outs],
        in_specs=[vmem, any_ref, vmem, any_ref, any_ref, vmem, vmem],
        out_specs=[spec for _, spec in outs],
        scratch_shapes=[
            pltpu.VMEM((LENGTH, D), bf16),
            pltpu.VMEM((LENGTH, D), bf16),
            pltpu.VMEM((WALL, D), bf16),
            pltpu.VMEM((FIRST, D), bf16),
            pltpu.VMEM((FIRST, 1), f32),
            pltpu.VMEM((KINDS, WROWS, D), bf16),
            pltpu.VMEM((5, 8, 512), f32),
            pltpu.VMEM((10, 8, 512), f32),
            pltpu.VMEM((2, 128, LENGTH), bf16),
            pltpu.VMEM((256, LENGTH), bf16),
            pltpu.VMEM((3, LENGTH, 128), bf16),
            pltpu.VMEM((SECOND, LENGTH), bf16),
            pltpu.VMEM((HIDDEN, LENGTH), f32),
            pltpu.VMEM((8, ROWS, D), bf16),
            pltpu.VMEM((8, D), f32),
            pltpu.VMEM((ROWS, D), f32),
            pltpu.VMEM((2, WROWS, D), f32),
            pltpu.VMEM((2, 128, LENGTH), bf16),
            pltpu.VMEM((LENGTH, 128), bf16),
            pltpu.VMEM((HIDDEN, LENGTH), bf16),
            pltpu.SemaphoreType.DMA((112,)),
            pltpu.SemaphoreType.DMA((112,)),
            pltpu.SemaphoreType.DMA((48,)),
        ],
        compiler_params=pltpu.CompilerParams(
            collective_id=1, has_side_effects=True, vmem_limit_bytes=60 << 20
        ),
    )(x, ct, aw, ew, cw, norm_rows, table)


class TokenScatter:
    def __init__(self, net, at, block, landed, out):
        self.net, self.block, self.landed, self.out, self.got = net, block, landed, out, {}
        z, xh, y, xl, c = at
        self.x = device(z, xh, y, 1 - xl, c)
        self.p = device(z, xh, y + 1, xl, c)
        self.m = device(z, xh, y - 1, xl, c)

    def send(self, name, dy, dx, half, place, peer, *more):
        part = pl.ds(half * 64, 64)
        block, others = self.block(slot(dy, dx))
        terms = [ref.at[part] for ref in others] + [self.landed.at[k, part] for k in more]
        if terms:
            add_into(64, block.at[part], block.at[part], *terms)
        self.got[name] = self.net.go(block.at[part], self.landed.at[place, part], peer)

    def wait(self, *names):
        for name in names:
            self.got[name].wait_recv()

    def steps(self, tag):
        send, wait = self.send, self.wait

        def xo():
            send("xo1", 2, 1, 0, 0, self.x)
            send("xo2", 2, 1, 1, 0, self.x)

        def lp():
            send("lp1", -1, 1, 0, 1, self.m)
            send("lp2", -1, 1, 1, 1, self.m)

        def rp():
            send("rp1", 1, 1, 0, 2, self.p)
            send("rp2", 1, 1, 1, 2, self.p)

        def oa():
            wait("xo1")
            send("a", 2, 0, 0, 3, self.m, 0)

        def ob():
            wait("xo2")
            send("b", 2, 0, 1, 3, self.p, 0)

        def le():
            send("l2", -1, 0, 1, 4, self.m)

        def re():
            send("r1", 1, 0, 0, 5, self.p)

        def nl():
            wait("a")
            send("l1", -1, 0, 0, 4, self.m, 3)

        def nr():
            wait("b")
            send("r2", 1, 0, 1, 5, self.p, 3)

        def p1():
            wait("lp1", "rp1")
            send("p1", 0, 1, 0, 6, self.x, 1, 2)

        def p2():
            wait("lp2", "rp2")
            send("p2", 0, 1, 1, 6, self.x, 1, 2)

        def fi():
            wait("l1", "l2", "r1", "r2", "p1", "p2")
            block, others = self.block(slot(0, 0))
            add_into(ROWS, self.out, block, *others, *(self.landed.at[k] for k in (4, 5, 6)))

        parts = (xo, lp, rp, oa, ob, le, re, nl, nr, p1, p2, fi)
        return {tag + part.__name__: part for part in parts}


class WeightScatter:
    def __init__(self, net, at, part, kind, landed, out):
        self.net, self.at, self.part, self.kind = net, at, part, kind
        self.landed, self.out = landed, out
        z, xh, y, xl, c = at
        self.h = device(z, 1 - xh, y, xl, c)
        self.p = device(z + 1, xh, y, xl, c)
        self.m = device(z - 1, xh, y, xl, c)
        self.got = {}

    def rows(self, dz, dh, half=None):
        z, xh = self.at[:2]
        start, size = (0, WROWS) if half is None else (half * 32, 32)
        return self.part.at[
            weight_rows(self.kind, z + dz, xh if dh == 0 else 1 - xh, start, size)
        ]

    def send(self, src, place, peer, half=None):
        start, size = (0, WROWS) if half is None else (half * 32, 32)
        return self.net.go(src, self.landed.at[place, pl.ds(start, size)], peer)

    def steps(self):
        got = self.got

        def op():
            for dh in (1, 0):
                got["a", dh] = self.send(self.rows(2, dh, 0), dh, self.m, 0)
                got["b", dh] = self.send(self.rows(2, dh, 1), dh, self.p, 1)

        def left(dh):
            got["a", dh].wait_recv()
            half = self.rows(-1, dh, 0)
            add_into(32, half, half, self.landed.at[dh, pl.ds(0, 32)])
            got["l", dh] = self.send(self.rows(-1, dh), 2 + dh, self.m)

        def right(dh):
            got["b", dh].wait_recv()
            half = self.rows(1, dh, 1)
            add_into(32, half, half, self.landed.at[dh, pl.ds(32, 32)])
            got["r", dh] = self.send(self.rows(1, dh), 4 + dh, self.p)

        def pa():
            got["l", 1].wait_recv()
            got["r", 1].wait_recv()
            other = self.rows(0, 1)
            add_into(WROWS, other, other, self.landed.at[3], self.landed.at[5])
            got["p"] = self.send(other, 6, self.h)

        def fi():
            for name in (("l", 0), ("r", 0), "p"):
                got[name].wait_recv()
            add_into(
                WROWS, self.out, self.rows(0, 0),
                self.landed.at[2], self.landed.at[4], self.landed.at[6],
            )

        tag = f"W{self.kind}"
        return {
            tag + "op": op,
            tag + "l1": lambda: left(1),
            tag + "l0": lambda: left(0),
            tag + "r1": lambda: right(1),
            tag + "r0": lambda: right(0),
            tag + "pa": pa,
            tag + "fi": fi,
        }


TILE = 512
TILES = D // TILE


def factors_of(moments):
    eye = lax.broadcasted_iota(jnp.int32, (HD, HD), 0) == lax.broadcasted_iota(jnp.int32, (HD, HD), 1)
    one = jnp.where(eye, 1.0, 0.0)

    def each(work, *lists):
        return [work(*items) for items in zip(*lists)]

    def gram_of(moment):
        both = jnp.concatenate(split(moment), axis=0)
        gram = dot(both, both, nt)
        return gram[:HD, :HD] + gram[HD:, HD:] + (gram[:HD, HD:] + gram[HD:, :HD])

    def size_of(gram):
        size = jnp.sum(jnp.where(eye, gram, 0.0), axis=1, keepdims=True)
        return jnp.sqrt(jnp.sum(size, axis=0, keepdims=True)) + 1e-07

    grams = each(gram_of, moments)
    sizes = each(size_of, grams)
    grams = each(lambda gram, size: gram / size / size, grams, sizes)
    wholes = None
    for turn_at in range(NS_STEPS):
        squares = each(times, grams, grams)
        steps = each(lambda a, b: polish_a * one + polish_b * a + polish_c * b, grams, squares)
        wholes = steps if turn_at == 0 else each(times, steps, wholes)
        if turn_at < NS_STEPS - 1:
            grams = each(times, steps, each(times, grams, steps))
    return each(lambda whole, size: whole / size, wholes, sizes)


def scatter_order(s):
    return (
        s.Rxo, s.sec0, s.Rrp, s.Rlp, s.sec1, s.W2op, s.E0, s.E1, s.W1op, s.W2l1, s.Rp1, s.Roa, s.W2r1,
        s.Rob, s.bk0, s.W1l1, s.W1r1, s.Rp2, s.Rle, s.bk1, s.Rnl, s.W1l0, s.W2r0, s.Rnr, s.W2pa, s.bk2,
        s.bk3, s.Rre, s.qb, s.W1pa, s.g1, s.W2l0, s.W1r0, s.qk0, s.Dxo, s.Dlp, s.Drp, s.qk1, s.W0op,
        s.g3, s.st0, s.g2, s.W0r1, s.W0l1, s.W2fi, s.Dp1, s.W0r0, s.W1fi, s.st1, s.Doa, s.Dob, s.f12,
        s.W0l0, s.st2, s.Rfi, s.Dre, s.W0pa, s.Dle, s.st3, s.Dnr, s.Dp2, s.Dnl, s.st4, s.W0fi, s.f0,
        s.Dfi,
    )


def scatter_kernel(
    raw_ref, gb_ref, w_ref, branch_ref, qm_ref, kv_ref, rows_ref, inner_ref, dom_ref, do_rows_ref, dup_ref,
    am_ref, em_ref, cm_ref, lse, delta, gain_ref, table,
    branch_out, dnormed_out, wgrad_out, factor_out, norm_out,
    mine, part, sibs, landed, wpart, wlanded, w, early, outer, tiles, rows, dom, do_rows, dq, moments,
    affine, norm_part, sums, nlanded, send, recv, local, tile_sems,
):
    at = place()
    z, xh, y, xl, c = at
    net, near = Net(send, recv), Local(local)
    stages = stage_peers(at)
    sib = device(z, xh, y, xl, 1 - c)
    steps, swaps = {}, {}
    met = greet([peer for stage in stages for peer in stage])

    def step(name, work, *args):
        steps[name] = functools.partial(work, *args)

    def fetch(n):
        src = gb_ref if n < TILES else raw_ref
        cols = pl.ds(n % TILES * TILE, TILE)
        return pltpu.make_async_copy(src.at[:, cols], tiles.at[n % 2], tile_sems.at[n % 2])

    fetch(0).start()
    inner_load = near.go(inner_ref, early)
    branch_slots = {slot(dy, dx): k for k, (dy, dx) in enumerate(PLACES[:5])}
    branch_loads = {s: near.go(branch_ref.at[s], mine.at[k]) for s, k in branch_slots.items()}
    first_loads = [near.go(dup_ref, outer.at[pl.ds(QKV, HIDDEN)]), near.go(w_ref, w)]
    attn_loads = [near.go(rows_ref, rows), near.go(dom_ref, dom), near.go(do_rows_ref, do_rows)]
    moment_loads = [near.go(ref, moments.at[k]) for k, ref in enumerate((am_ref, em_ref, cm_ref))]

    def branch_block(s):
        if s not in branch_slots:
            return branch_ref.at[s], []
        load = branch_loads.pop(s, None)
        if load is not None:
            load.wait()
        return mine.at[branch_slots[s]], []

    def dnormed_block(s):
        swap = swaps.pop(s, None)
        if swap is not None:
            swap.wait_recv()
        return part.at[c, s], [sibs.at[s]]

    def factors(*kinds):
        for kind in kinds:
            moment_loads[kind].wait()
        found = factors_of([muon_beta * moments[kind] + wgrad_out[kind] for kind in kinds])
        for kind, factor in zip(kinds, found):
            factor_out[kind] = factor

    step("f12", factors, 1, 2)
    step("f0", factors, 0)
    steps |= TokenScatter(net, at, branch_block, landed.at[0], branch_out).steps("R")
    steps |= TokenScatter(net, at, dnormed_block, landed.at[1], dnormed_out).steps("D")
    for kind in range(KINDS):
        steps |= WeightScatter(
            net, at, wpart, kind, wlanded.at[kind], wgrad_out.at[kind]
        ).steps()

    def tile_in(n):
        if n + 1 < 3 * TILES:
            fetch(n + 1).start()
        fetch(n).wait()
        return pl.ds(n % TILES * TILE, TILE), tiles.at[n % 2]

    def second_pass(half):
        if half == 0:
            inner_load.wait()
        for n in range(half * TILES // 2, (half + 1) * TILES // 2):
            cols, tile = tile_in(n)
            wpart[pl.ds(FIRST, SECOND), cols] = dot(early[...], tile[...], nn).astype(bf16)
        if half == 1:
            attn_loads.extend(
                [near.go(qm_ref.at[h], early.at[pl.ds(h * 128, 128)]) for h in range(2)]
            )
            attn_loads.append(near.go(kv_ref, early.at[pl.ds(256, 256)]))

    def first_pass(start, size, base, half):
        if base == TILES and half == 0:
            for load in first_loads:
                load.wait()
        span = pl.ds(start, size)
        total = dot(outer[span], jnp.ones((LENGTH, 128), bf16), nn)[:, :1]
        for n in range(base + half * TILES // 2, base + (half + 1) * TILES // 2):
            cols, tile = tile_in(n)
            summed = dot(outer[span], tile[...], nn)
            wpart[span, cols] = (summed * affine[0:1, cols] + total * affine[1:2, cols]).astype(bf16)
            block = w[span, cols].astype(f32)
            by_gain = jnp.sum(block * summed, axis=0, keepdims=True)
            by_bias = jnp.sum(block * total, axis=0, keepdims=True)
            if base == TILES:
                norm_part[0:1, cols] = by_gain
                norm_part[1:2, cols] = by_bias
            else:
                norm_part[0:1, cols] += by_gain
                norm_part[1:2, cols] += by_bias

    for half in range(2):
        step(f"sec{half}", second_pass, half)
        step(f"E{half}", first_pass, QKV, HIDDEN, TILES, half)
        step(f"qk{half}", first_pass, 0, QKV, 2 * TILES, half)

    def back(kb):
        if kb == 0:
            for load in attn_loads:
                load.wait()
        attend_back_block(
            kb, early.at[pl.ds(0, 256)], early.at[pl.ds(256, 256)], rows.at[0], rows.at[1], rows.at[2],
            dom, do_rows, lse, delta, dq, outer, table,
        )

    for kb in range(LENGTH // QB):
        step(f"bk{kb}", back, kb)
    step("qb", query_back, dq, outer, table)

    def dnormed_unit(dy, dx):
        unit = lax.rem(y + dy, 4) * 2 + lax.rem(xl + dx, 2)
        block = dot(outer[:, at_unit(unit)], w[...], tn).astype(bf16)
        s = dy + 4 * dx
        part[0, s] = block[:ROWS]
        part[1, s] = block[ROWS:]

    def swap(dy, dx):
        s = slot(dy, dx)
        swaps[s] = net.go(part.at[1 - c, s], sibs.at[s], sib)

    def dnormed_of(dx):
        @pl.loop(0, 3)
        def _(i):
            dnormed_unit(lax.rem(i + 1, 3) + 1, dx)

        for dy in (2, -1, 1):
            swap(dy, dx)

    def dnormed_rest():
        @pl.loop(0, 2)
        def _(i):
            dnormed_unit(0, 1 - i)

        swap(0, 1)
        swap(0, 0)

    step("g1", dnormed_of, 1)
    step("g2", dnormed_of, 0)
    step("g3", dnormed_rest)
    staged = Staged(net, stages, sums, nlanded)

    def stage(k):
        if k == 0:
            for kind in range(2):
                for q in range(4):
                    sums[0, pl.ds(kind * 4 + q, 1)] = norm_part[pl.ds(kind, 1), pl.ds(q * 512, 512)]
        else:
            staged.finish()
        if k < 4:
            staged.start()
        else:
            norm_out[...] = sums[4]

    for k in range(5):
        step(f"st{k}", stage, k)

    gain, bias = spread(gain_ref[...])
    affine[0:1] = gain
    affine[1:2] = bias
    met()
    for work in scatter_order(types.SimpleNamespace(**steps)):
        work()
    net.drain()


def scatter(*args):
    any_ref = pl.BlockSpec(memory_space=pl.ANY)
    vmem = pl.BlockSpec(memory_space=pltpu.VMEM)
    return pl.pallas_call(
        scatter_kernel,
        name="scatter",
        out_shape=(
            jax.ShapeDtypeStruct((ROWS, D), f32),
            jax.ShapeDtypeStruct((ROWS, D), f32),
            jax.ShapeDtypeStruct((KINDS, WROWS, D), f32),
            jax.ShapeDtypeStruct((KINDS, HD, HD), f32),
            jax.ShapeDtypeStruct((8, 512), f32),
        ),
        in_specs=[any_ref] * 14 + [vmem] * 4,
        out_specs=(vmem,) * 5,
        scratch_shapes=[
            pltpu.VMEM((5, ROWS, D), bf16),
            pltpu.VMEM((2, 8, ROWS, D), bf16),
            pltpu.VMEM((8, ROWS, D), bf16),
            pltpu.VMEM((2, 7, ROWS, D), bf16),
            pltpu.VMEM((WALL, D), bf16),
            pltpu.VMEM((KINDS, 7, WROWS, D), bf16),
            pltpu.VMEM((FIRST, D), bf16),
            pltpu.VMEM((SECOND, LENGTH), bf16),
            pltpu.VMEM((FIRST, LENGTH), bf16),
            pltpu.VMEM((2, LENGTH, TILE), bf16),
            pltpu.VMEM((3, LENGTH, 128), bf16),
            pltpu.VMEM((2, 128, LENGTH), bf16),
            pltpu.VMEM((LENGTH, 128), bf16),
            pltpu.VMEM((128, LENGTH), f32),
            pltpu.VMEM((KINDS, WROWS, D), f32),
            pltpu.VMEM((8, D), f32),
            pltpu.VMEM((8, D), f32),
            pltpu.VMEM((5, 8, 512), f32),
            pltpu.VMEM((10, 8, 512), f32),
            pltpu.SemaphoreType.DMA((112,)),
            pltpu.SemaphoreType.DMA((112,)),
            pltpu.SemaphoreType.DMA((24,)),
            pltpu.SemaphoreType.DMA((2,)),
        ],
        compiler_params=pltpu.CompilerParams(
            collective_id=2, has_side_effects=True, vmem_limit_bytes=63 << 20
        ),
    )(*args)


def update_kernel(
    x_ref, ct_ref, branch_ref, dnormed_ref, gain_ref, share_ref, factor_ref,
    aw, ew, cw, am, em, cm,
    state_out, grad_out, ag, an, aweight, eg, en, eweight, cg, cn, cweight,
):
    x, dnormed = x_ref[...], dnormed_ref[...]
    state_out[...] = x + branch_ref[...]
    centred = x - jnp.mean(x, axis=1, keepdims=True)
    inverse = lax.rsqrt(jnp.mean(centred * centred, axis=1, keepdims=True) + eps_norm)
    xhat = centred * inverse
    scaled = dnormed * spread(gain_ref[...])[0]
    grad_out[...] = ct_ref[...] + inverse * (
        scaled
        - jnp.mean(scaled, axis=1, keepdims=True)
        - xhat * jnp.mean(scaled * xhat, axis=1, keepdims=True)
    )
    kinds = ((aw, am, ag, an, aweight), (ew, em, eg, en, eweight), (cw, cm, cg, cn, cweight))
    for k, (weight, moment, grad, moment_next, weight_next) in enumerate(kinds):
        share = share_ref[k]
        grad[...] = share
        following = muon_beta * moment[...] + share
        moment_next[...] = following
        ortho = times(factor_ref[k], following)
        old = weight[...]
        weight_next[...] = old - muon_rate * (muon_decay * old + 0.2 * math.sqrt(D) * ortho)


def update(x, ct, branch, dnormed, gain_rows, shares, factors, *blocks):
    steps = 2
    token = pl.BlockSpec((ROWS // steps, D), lambda i: (i, 0))
    block = pl.BlockSpec((WROWS, D // steps), lambda i: (0, i))
    shape = jax.ShapeDtypeStruct
    return pl.pallas_call(
        update_kernel,
        name="update",
        grid=(steps,),
        out_shape=[shape((ROWS, D), f32)] * 2 + [shape((WROWS, D), f32)] * 9,
        in_specs=[token] * 4
        + [
            pl.BlockSpec((8, 512), lambda i: (0, 0)),
            pl.BlockSpec((KINDS, WROWS, D // steps), lambda i: (0, 0, i)),
            pl.BlockSpec((KINDS, HD, HD), lambda i: (0, 0, 0)),
        ]
        + [block] * 6,
        out_specs=[token] * 2 + [block] * 9,
        compiler_params=pltpu.CompilerParams(vmem_limit_bytes=60 << 20),
    )(x, ct, branch, dnormed, gain_rows, shares, factors, *blocks)


def angles():
    half = ROT // 2
    freq = rope_base ** (-2.0 * np.arange(half) / ROT)
    turned = freq[:, None] * np.arange(LENGTH)[None, :]
    return jnp.asarray(np.concatenate([np.cos(turned), np.sin(turned)]).astype(np.float32))


def body(
    inputs, cotangent, attn_weight, expand_weight, contract_weight, norm_params,
    attn_moment, expand_moment, contract_moment, norm_first, norm_second,
):
    index = (lax.axis_index("fsdp") * 8 + lax.axis_index("seq")) * 4 + lax.axis_index("mp")
    table = angles()
    (
        raw, grad_group, first_w, norm_rows, qm, kv, rows, inner, lse, branch,
        dom, do_rows, delta, dup,
    ) = gather(
        inputs,
        cotangent,
        attn_weight[0, 0],
        expand_weight[0],
        contract_weight[0],
        norm_params[0],
        table,
    )
    blocks = (attn_weight[0, 0], expand_weight[0], contract_weight[0])
    moments = (attn_moment[0, 0], expand_moment[0], contract_moment[0])
    branch, dnormed, shares, factors, norm_total = scatter(
        raw, grad_group, first_w, branch, qm, kv, rows, inner, dom, do_rows, dup,
        *moments, lse, delta, norm_rows, table,
    )
    state, grad_state, *updates = update(
        inputs, cotangent, branch, dnormed, norm_rows, shares, factors, *blocks, *moments
    )
    updates = [
        part.reshape(attn_weight.shape if k < 3 else expand_weight.shape)
        for k, part in enumerate(updates)
    ]
    norm_share = jnp.concatenate(
        [
            lax.dynamic_slice(norm_total, (4 * kind + index // 32, index % 32 * 16), (1, 16))
            for kind in range(2)
        ]
    )[None]
    first_next = adam_first * norm_first + (1.0 - adam_first) * norm_share
    second_next = adam_second * norm_second + (1.0 - adam_second) * norm_share * norm_share
    first_fix = 1.0 - adam_first**STEP
    second_fix = 1.0 - adam_second**STEP
    norm_next = norm_params - adam_rate * (first_next / first_fix) / (
        jnp.sqrt(second_next / second_fix) + adam_eps
    )
    return (state, grad_state, *updates, norm_share, first_next, second_next, norm_next)


def solution(mesh):
    return jax.shard_map(
        body,
        mesh=mesh,
        in_specs=(
            P(("fsdp", "seq", "mp"), None),
            P(("fsdp", "seq", "mp"), None),
            P(None, ("fsdp", "seq", "mp"), None, None),
            P(None, ("fsdp", "seq", "mp"), None),
            P(None, ("fsdp", "seq", "mp"), None),
            P(None, None, ("fsdp", "seq", "mp")),
            P(None, ("fsdp", "seq", "mp"), None, None),
            P(None, ("fsdp", "seq", "mp"), None),
            P(None, ("fsdp", "seq", "mp"), None),
            P(None, None, ("fsdp", "seq", "mp")),
            P(None, None, ("fsdp", "seq", "mp")),
        ),
        out_specs=(
            P(("fsdp", "seq", "mp"), None),
            P(("fsdp", "seq", "mp"), None),
            P(None, ("fsdp", "seq", "mp"), None, None),
            P(None, ("fsdp", "seq", "mp"), None, None),
            P(None, ("fsdp", "seq", "mp"), None, None),
            P(None, ("fsdp", "seq", "mp"), None),
            P(None, ("fsdp", "seq", "mp"), None),
            P(None, ("fsdp", "seq", "mp"), None),
            P(None, ("fsdp", "seq", "mp"), None),
            P(None, ("fsdp", "seq", "mp"), None),
            P(None, ("fsdp", "seq", "mp"), None),
            P(None, None, ("fsdp", "seq", "mp")),
            P(None, None, ("fsdp", "seq", "mp")),
            P(None, None, ("fsdp", "seq", "mp")),
            P(None, None, ("fsdp", "seq", "mp")),
        ),
        check_vma=False,
    )
```

```python
import functools
import math
import types

import jax
import jax.numpy as jnp
import numpy as np
from jax import lax
from jax.experimental import pallas as pl
from jax.experimental.pallas import tpu as pltpu
from jax.sharding import PartitionSpec as P

D = 2048
H = 32
HD = 64
ROT = 32
LENGTH = 2048
NS_STEPS = 5
STEP = 10
ROWS = 128
WROWS = 64
KINDS = 3
QKV = 384
HIDDEN = 512
FIRST = QKV + HIDDEN
SECOND = 128 + HIDDEN
WALL = FIRST + SECOND

eps_norm = 1e-05
rope_base = 10000.0
muon_beta = 0.95
muon_rate = 0.15
muon_decay = 0.01
polish_a = 3.4445
polish_b = -4.775
polish_c = 2.0315
adam_first = 0.9
adam_second = 0.95
adam_rate = 0.5
adam_eps = 1e-08
masked_score = -1e30
highest = lax.Precision.HIGHEST
across = (((1,), (1,)), ((), ()))
downward = (((0,), (0,)), ((), ()))
MESH = pl.DeviceIdType.MESH
f32 = jnp.float32
bf16 = jnp.bfloat16


def place():
    z = lax.axis_index("fsdp")
    s = lax.axis_index("seq")
    m = lax.axis_index("mp")
    return z, s // 4, lax.rem(s, 4), m // 2, lax.rem(m, 2)


def device(z, xh, y, xl, c):
    return (lax.rem(z + 4, 4), xh * 4 + lax.rem(y + 4, 4), xl * 2 + c)


def token_rows(y, xl, c, start=0, size=ROWS):
    block = lax.rem(y + 4, 4) * 4 + xl * 2 + c
    return pl.ds(pl.multiple_of(block * ROWS + start, 32), size)


def weight_rows(kind, z, xh, start=0, size=WROWS):
    z = lax.rem(z + 4, 4)
    if kind == 0:
        base = z * 128 + (z // 3) * HIDDEN + xh * 64
    elif kind == 1:
        base = QKV + z * 128 + xh * 64
    else:
        base = FIRST + 128 + z * 128 + xh * 64
    return pl.ds(pl.multiple_of(base + start, 32), size)


class Net:
    def __init__(self, send, recv):
        self.send, self.recv, self.used, self.sent = send, recv, 0, []

    def go(self, src, dst, peer, sent=None):
        slot = self.used
        self.used += 1
        copy = pltpu.make_async_remote_copy(
            src_ref=src,
            dst_ref=dst,
            send_sem=self.send.at[slot],
            recv_sem=self.recv.at[slot],
            device_id=peer,
            device_id_type=MESH,
        )
        copy.start()
        (self.sent if sent is None else sent).append(copy)
        return copy

    def drain(self):
        for copy in self.sent:
            copy.wait_send()
        self.sent = []


class Local:
    def __init__(self, sems):
        self.sems, self.used = sems, 0

    def go(self, src, dst):
        copy = pltpu.make_async_copy(src, dst, self.sems.at[self.used])
        self.used += 1
        copy.start()
        return copy


def greet(peers):
    barrier = pltpu.get_barrier_semaphore()
    for peer in peers:
        pl.semaphore_signal(barrier, inc=1, device_id=peer, device_id_type=MESH)
    return lambda: pl.semaphore_wait(barrier, len(peers))


def stage_peers(at):
    z, xh, y, xl, c = at
    return [
        [device(z + k, xh, y, xl, c) for k in (1, 2, 3)],
        [device(z, xh, y + k, xl, c) for k in (1, 2, 3)],
        [
            device(z, xh, y, 1 - xl, c),
            device(z, 1 - xh, y, xl, c),
            device(z, 1 - xh, y, 1 - xl, c),
        ],
        [device(z, xh, y, xl, 1 - c)],
    ]


class Staged:
    def __init__(self, net, stages, sums, landed):
        self.net, self.stages, self.sums, self.landed = net, stages, sums, landed
        self.stage = self.slot = 0

    def start(self):
        self.copies = [
            self.net.go(self.sums.at[self.stage], self.landed.at[self.slot + k], peer)
            for k, peer in enumerate(self.stages[self.stage])
        ]

    def finish(self):
        total = self.sums[self.stage]
        for copy in self.copies:
            copy.wait_recv()
            total = total + self.landed[self.slot]
            self.slot += 1
        self.stage += 1
        self.sums[self.stage] = total


def spread(flat):
    gain = jnp.concatenate([flat[k : k + 1] for k in range(4)], axis=1)
    bias = jnp.concatenate([flat[k : k + 1] for k in range(4, 8)], axis=1)
    return gain, bias


class TokenGather:
    def __init__(self, net, at, full, around):
        self.net, self.at, self.full, self.sent, self.got = net, at, full, [], {}
        self.waited = set()
        self.around = around
        z, xh, y, xl, c = at
        self.x = device(z, xh, y, 1 - xl, c)
        self.p = device(z, xh, y + 1, xl, c)
        self.m = device(z, xh, y - 1, xl, c)
        self.s = device(z, xh, y, xl, 1 - c)

    def rows(self, dy, dx, half=None):
        z, xh, y, xl, c = self.at
        start, size = (0, ROWS) if half is None else ((0, 64), (64, 64), (64, 32), (96, 32))[half]
        return self.full.at[token_rows(y + dy, xl if dx == 0 else 1 - xl, c, start, size)]

    def go(self, name, peer, dy, dx, half=None, block=None):
        here = self.rows(dy, dx, half)
        src = here
        if block is not None:
            src = block if half is None else block.at[pl.ds(half * 64, 64)]
        self.got[name] = self.net.go(src, here, peer, self.sent)

    def wait(self, *names):
        for name in names:
            if name not in self.waited:
                self.got[name].wait_recv()
                self.waited.add(name)

    def clear(self):
        for copy in self.sent:
            copy.wait_send()

    def steps(self, tag, block):
        go, wait = self.go, self.wait

        def own1():
            go("l1", self.p, 0, 0, 0, block)
            go("r1", self.m, 0, 0, 1, block)

        def own2():
            go("l2", self.p, 0, 0, 1, block)
            go("r2", self.m, 0, 0, 0, block)
            go("s0", self.s, 0, 0, None, block)

        def ownp():
            go("p1", self.x, 0, 0, 0, block)
            go("p2", self.x, 0, 0, 1, block)

        def nl():
            wait("l1")
            go("a", self.p, -1, 0, 0)

        def nr():
            wait("r1")
            go("b", self.m, 1, 0, 1)

        def sl():
            wait("l2")
            go("s1", self.s, -1, 0)

        def sr():
            wait("r2")
            go("s2", self.s, 1, 0)

        def np1():
            wait("p1")
            go("lp1", self.p, 0, 1, 0)
            go("rp1", self.m, 0, 1, 0)

        def np2():
            wait("p2")
            go("lp2", self.p, 0, 1, 1)
            go("rp2", self.m, 0, 1, 1)
            go("s3", self.s, 0, 1)

        def fa():
            wait("a")
            go("xo1", self.x, 2, 0, 0)

        def fb():
            wait("b")
            if not self.around:
                go("xo2", self.x, 2, 0, 1)
            go("s4", self.s, 2, 0)

        def e1():
            wait("lp1", "lp2")
            if self.around:
                go("qa", self.p, -1, 1, 2)
            go("s5", self.s, -1, 1)

        def e2():
            wait("rp1", "rp2")
            if self.around:
                go("qb", self.m, 1, 1, 3)
            go("s6", self.s, 1, 1)

        def e3():
            wait("xo1", *(("qa", "qb") if self.around else ("xo2",)))
            go("s7", self.s, 2, 1)

        parts = (own1, own2, ownp, nl, nr, sl, sr, np1, np2, fa, fb, e1, e2, e3)
        return {tag + part.__name__: part for part in parts}


class WeightGather:
    def __init__(self, net, near, at, full, kind, own_w, block, load):
        self.net, self.near, self.at, self.full, self.kind, self.got = net, near, at, full, kind, {}
        self.own_w, self.block, self.load = own_w, block, load
        z, xh, y, xl, c = at
        self.h = device(z, 1 - xh, y, xl, c)
        self.p = device(z + 1, xh, y, xl, c)
        self.m = device(z - 1, xh, y, xl, c)

    def rows(self, dz, dh, half=None):
        z, xh = self.at[:2]
        start, size = (0, WROWS) if half is None else (half * 32, 32)
        return self.full.at[
            weight_rows(self.kind, z + dz, xh if dh == 0 else 1 - xh, start, size)
        ]

    def go(self, name, peer, dz, dh, half, own=False):
        here = self.rows(dz, dh, half)
        src = self.own_w.at[pl.ds(half * 32, 32)] if own else here
        self.got[name] = self.net.go(src, here, peer)

    def wait(self, *names):
        for name in names:
            self.got[name].wait_recv()

    def steps(self):
        go, wait = self.go, self.wait

        def own():
            if self.load is not None:
                self.load.wait()
            self.own_w[...] = self.block[...].astype(bf16)
            go("l1", self.p, 0, 0, 0, True)
            go("r1", self.m, 0, 0, 1, True)
            go("l2", self.p, 0, 0, 1, True)
            go("r2", self.m, 0, 0, 0, True)
            self.copy = self.near.go(self.own_w, self.rows(0, 0))

        def ownp():
            go("p1", self.h, 0, 0, 0, True)
            go("p2", self.h, 0, 0, 1, True)

        def na():
            wait("l1", "r1")
            go("a", self.p, -1, 0, 0)
            go("b", self.m, 1, 0, 1)

        def np1():
            wait("p1")
            go("lp1", self.p, 0, 1, 0)
            go("rp1", self.m, 0, 1, 0)

        def np2():
            wait("p2")
            go("rp2", self.m, 0, 1, 1)
            go("lp2", self.p, 0, 1, 1)

        def fl():
            wait("lp1")
            go("ha", self.p, -1, 1, 0)

        def fr():
            wait("rp2")
            go("hb", self.m, 1, 1, 1)

        def end():
            wait("l2", "r2", "a", "b", "lp2", "rp1", "ha", "hb")
            self.copy.wait()

        parts = (own, ownp, na, np1, np2, fl, fr, end)
        return {f"W{self.kind}" + part.__name__: part for part in parts}


nn = (((1,), (0,)), ((), ()))
nt = (((1,), (1,)), ((), ()))
tn = (((0,), (0,)), ((), ()))
QB = 512
UNIT = 256


def dot(a, b, dims):
    return lax.dot_general(a, b, dims, preferred_element_type=f32)


def at_unit(unit, size=UNIT):
    return pl.ds(pl.multiple_of(unit * size, size), size)


def turn(part, cosine, sine):
    rows = []
    for low in (0, HD):
        first, second = part[low : low + 16], part[low + 16 : low + 32]
        rows += [first * cosine - second * sine, second * cosine + first * sine]
        rows.append(part[low + 32 : low + HD])
    return jnp.concatenate(rows, axis=0)


def of_head(h, block, axis):
    place = lax.broadcasted_iota(jnp.int32, block.shape, axis)
    return jnp.where((place < HD) == (h == 0), block, 0.0)


def gelu_pair(v):
    square = v * v
    t = jnp.tanh(math.sqrt(2 / math.pi) * (v + 0.044715 * (v * square)))
    plus = 0.5 * (1.0 + t)
    slope = plus + (0.5 * v) * (1.0 - t * t) * (
        math.sqrt(2 / math.pi) * (1.0 + 3 * 0.044715 * square)
    )
    return v * plus, slope


def split(a):
    high = a.astype(bf16)
    return high, (a - high.astype(f32)).astype(bf16)


def times(a, b):
    (ah, al), (bh, bl) = split(a), split(b)
    return dot(
        jnp.concatenate([ah, ah, al, al], axis=1), jnp.concatenate([bh, bl, bh, bl], axis=0), nn
    )


def scale_weights(start, size, w, scaled, shift, affine):
    high, low = split(affine[1:2])
    pair = jnp.concatenate([high, low] * 8, axis=0)
    by_bias = dot(w[pl.ds(start, size)], pair, nt)
    shift[pl.ds(start, size)] = by_bias[:, 0:1] + by_bias[:, 1:2]

    @pl.loop(0, size // 32)
    def _(i):
        part = pl.ds(pl.multiple_of(start + i * 32, 32), 32)
        scaled[part] = (w[part].astype(f32) * affine[0:1]).astype(bf16)


def qkv_unit(unit, raw, w, shift, table, qm, kv, q_rows, k_rows, v_rows):
    cols = at_unit(unit)
    lin = dot(w[pl.ds(0, QKV)], raw[cols], nt) + shift[0:QKV]
    cosine, sine = table[0:16, cols], table[16:32, cols]
    q = turn(lin[0:128], cosine, sine).astype(bf16).astype(f32) * HD**-0.5
    k = turn(lin[128:256], cosine, sine)
    v = lin[256:384]
    for h in range(2):
        qm[h, :, cols] = of_head(h, q, 0).astype(bf16)
    kv[pl.ds(0, 128), cols] = k.astype(bf16)
    kv[pl.ds(128, 128), cols] = v.astype(bf16)
    q_rows[cols] = q.T.astype(bf16)
    k_rows[cols] = k.T.astype(bf16)
    v_rows[cols] = v.T.astype(bf16)


def up_unit(unit, raw, w, shift, inner, slope):
    cols = at_unit(unit, 2 * UNIT)
    act, der = gelu_pair(dot(w[pl.ds(QKV, HIDDEN)], raw[cols], nt) + shift[pl.ds(QKV, HIDDEN)])
    inner[pl.ds(128, HIDDEN), cols] = act.astype(bf16)
    slope[:, cols] = der


def branch_unit(unit, inner, w, out):
    rows = at_unit(unit, 2 * UNIT)
    out[rows] = dot(inner[:, rows], w[pl.ds(FIRST, SECOND)], tn).astype(bf16)


def back_unit(cols, gb, w, inner, slope, dom, do_rows, delta, dup):
    lin = dot(w[pl.ds(FIRST, SECOND)], gb[cols], nt)
    do = lin[0:128].astype(bf16).astype(f32)
    for h in range(2):
        dom[h, :, cols] = of_head(h, do, 0).astype(bf16)
    do_rows[cols] = do.T.astype(bf16)
    both = do * inner[pl.ds(0, 128), cols].astype(f32)
    for h in range(2):
        delta[pl.ds(h, 1), cols] = jnp.sum(both[h * HD : h * HD + HD], axis=0, keepdims=True)
    dup[:, cols] = (lin[128:] * slope[:, cols]).astype(bf16)


def causal_mask(scores):
    rows = lax.broadcasted_iota(jnp.int32, scores.shape, 0)
    cols = lax.broadcasted_iota(jnp.int32, scores.shape, 1)
    return jnp.where(rows <= cols, scores, masked_score)


def attend_block(qb, qm, kv, k_rows, inner, lse):
    cols = at_unit(qb, QB)
    start = (jnp.full((1, QB), masked_score, f32), jnp.zeros((1, QB), f32), jnp.zeros((HD, QB), f32))

    def step(kb, carry, masked):
        keys = at_unit(kb, QB)
        k = k_rows[keys]
        result = []
        for h in range(2):
            top, total, out = carry[h]
            scores = dot(k, qm[h, :, cols], nn)
            if masked:
                scores = causal_mask(scores)
            high = jnp.maximum(top, jnp.max(scores, axis=0, keepdims=True))
            scale = jnp.exp(top - high)
            expo = jnp.exp(scores - high)
            total = total * scale + jnp.sum(expo, axis=0, keepdims=True)
            out = out * scale + dot(kv[pl.ds(128 + h * HD, HD), keys], expo.astype(bf16), nn)
            result.append((high, total, out))
        return tuple(result)

    carry = lax.fori_loop(0, qb, lambda kb, c: step(kb, c, False), (start, start))
    carry = step(qb, carry, True)
    for h in range(2):
        top, total, out = carry[h]
        inner[pl.ds(h * HD, HD), cols] = (out / total).astype(bf16)
        lse[pl.ds(h, 1), cols] = top + jnp.log(total)


def attend_back_block(kb, qm, kv, q_rows, k_rows, v_rows, dom, do_rows, lse, delta, dq, outer, table):
    keys = pl.ds(kb * QB, QB)

    def step(keys, cols, carry, masked, fresh=False):
        k, v = k_rows[keys], v_rows[keys]
        result = []
        for h in range(2):
            dk, dv = carry[h]
            scores = dot(k, qm[pl.ds(h * 128, 128), cols], nn)
            if masked:
                scores = causal_mask(scores)
            probs = jnp.exp(scores - lse[pl.ds(h, 1), cols])
            dp = dot(v, dom[h, :, cols], nn)
            ds = (probs * (dp - delta[pl.ds(h, 1), cols])).astype(bf16)
            dv = dv + dot(probs.astype(bf16), do_rows[cols], nn)
            dk = dk + dot(ds, q_rows[cols], nn)
            half = pl.ds(h * HD, HD)
            part = dot(kv[half, keys], ds, nn)
            if fresh:
                dq[half, cols] = part
            else:
                dq[half, cols] += part
            result.append((dk, dv))
        return tuple(result)

    small = QB // 2
    low, high = pl.ds(kb * QB, small), pl.ds(kb * QB + small, small)
    zero = jnp.zeros((small, 128), f32)
    start = ((zero, zero), (zero, zero))
    first = step(low, keys, start, True, kb == 0)
    second = step(high, high, start, True)
    carry = jax.tree.map(lambda a, b: jnp.concatenate([a, b], axis=0), first, second)
    carry = lax.fori_loop(
        kb + 1, LENGTH // QB, lambda qb, c: step(keys, at_unit(qb, QB), c, False, kb == 0), carry
    )
    (dk0, dv0), (dk1, dv1) = carry
    first = lax.broadcasted_iota(jnp.int32, (QB, 128), 1) < HD
    dk = jnp.where(first, dk0, dk1).astype(bf16).astype(f32).T
    dv = jnp.where(first, dv0, dv1).T
    cosine, sine = table[0:16, keys], -table[16:32, keys]
    outer[pl.ds(128, 128), keys] = turn(dk, cosine, sine).astype(bf16)
    outer[pl.ds(256, 128), keys] = dv.astype(bf16)


def query_back(dq, outer, table):
    part = (dq[...] * HD**-0.5).astype(bf16).astype(f32)
    outer[pl.ds(0, 128)] = turn(part, table[0:16], -table[16:32]).astype(bf16)


PLACES = [(0, 0), (-1, 0), (1, 0), (0, 1), (2, 0), (-1, 1), (1, 1), (2, 1)]


def slot(dy, dx):
    return dy % 4 + 4 * dx


def add_into(count, out, *refs):
    wide = f32 if len(refs) > 2 else out.dtype

    @pl.loop(0, count // 16)
    def _(i):
        part = pl.ds(pl.multiple_of(i * 16, 16), 16)
        total = refs[0][part].astype(wide)
        for ref in refs[1:]:
            total = total + ref[part].astype(wide)
        out[part] = total.astype(out.dtype)


GROUPS = (((0, 0),), ((-1, 0), (1, 0)), ((0, 1),), ((2, 0),), ((-1, 1), (1, 1)), ((2, 1),))

GRAD_GROUPS = tuple(((dy, 0), (dy, 1)) for dy in (0, 1, 2, -1))


def gather_order(s):
    return (
        s.W0own, s.W0ownp, s.LN, s.Town1, s.W0np1, s.Town2, s.st0, s.Townp, s.W0np2, s.W0na, s.W0fl,
        s.st1, s.Tnr, s.W0fr, s.W1own, s.Tnl, s.st2, s.Tsl, s.Tnp1, s.W1ownp, s.st3, s.Tnp2, s.Tsr,
        s.W0end, s.st4, s.wg0, s.W1np1, s.Tfa, s.Tfb, s.q0, s.q2, s.q3, s.W1np2, s.q1, s.W1na, s.W1fl,
        s.Te2, s.W1fr, s.W2own, s.castG, s.Gown1, s.W2ownp, s.Te1, s.Gownp, s.Gown2, s.q4, s.Te3,
        s.W1end, s.wc, s.wg1, s.u0, s.Gnr, s.W2np1, s.u2, s.W2np2, s.Gnl, s.q5, s.qc, s.W2na, s.at1,
        s.u3, s.u1, s.W2fl, s.Gsr, s.clear, s.Gnp1, s.W2fr, s.Gsl, s.at2, s.Gfa, s.at3, s.Gfb, s.at0,
        s.ic, s.Gnp2, s.W2end, s.b1, s.b3, s.b0, s.k0, s.sa1, s.sa3, s.Ge1, s.Ge2, s.b2, s.sa0, s.Ge3,
        s.k3, s.k1, s.k2, s.sa2,
    )


def gather_kernel(
    x_ref, ct_ref, aw_ref, ew_ref, cw_ref, norm_ref, table,
    raw_out, gb_out, w_out, gain_out, qm_out, kv_out, rows_out, inner_out, lse, branch_out,
    dom_out, do_rows_out, delta, dup_out,
    raw, gb, w, scaled, shift, own_w, sums, landed, qm, kv, rows, inner, slope, sibs, affine, ct, late, dom, do_rows, dup, send, recv, local,
):
    at = place()
    z, xh, y, xl, c = at
    stages = stage_peers(at)
    net, near = Net(send, recv), Local(local)
    met = greet([peer for stage in stages for peer in stage])
    q_rows, k_rows, v_rows = rows.at[0], rows.at[1], rows.at[2]
    kept, raw_copy, swaps = [], [], {}
    tokens = TokenGather(net, at, raw, False)
    grads = TokenGather(net, at, gb, False)
    own, own_g = tokens.rows(0, 0), grads.rows(0, 0)
    steps = tokens.steps("T", own) | grads.steps("G", own_g)
    loads = [near.go(ct_ref, ct)] + [near.go(ref, late.at[k]) for k, ref in enumerate((ew_ref, cw_ref))]
    blocks = ((aw_ref, None), (late.at[0], loads[1]), (late.at[1], loads[2]))
    for kind, (block, load) in enumerate(blocks):
        steps |= WeightGather(net, near, at, w, kind, own_w.at[kind], block, load).steps()

    def unit_of(dy, dx):
        return lax.rem(y + dy + 4, 4) * 2 + lax.rem(xl + dx, 2)

    def step(name, work, *args):
        steps[name] = functools.partial(work, *args)

    def norm_of():
        @pl.loop(0, ROWS // 16)
        def _(i):
            part = pl.ds(pl.multiple_of(i * 16, 16), 16)
            x = x_ref[part]
            centred = x - jnp.mean(x, axis=1, keepdims=True)
            inverse = lax.rsqrt(jnp.mean(centred * centred, axis=1, keepdims=True) + eps_norm)
            own[part] = (centred * inverse).astype(bf16)

    def cast_grad():
        loads[0].wait()

        @pl.loop(0, ROWS // 16)
        def _(i):
            part = pl.ds(pl.multiple_of(i * 16, 16), 16)
            own_g[part] = ct[part].astype(bf16)

    step("LN", norm_of)
    step("castG", cast_grad)
    staged = Staged(net, stages, sums, landed)

    def stage(k):
        if k > 0:
            staged.finish()
        if k < 4:
            staged.start()
        else:
            gain_out[...] = sums[4]
            gain, bias = spread(sums[4])
            affine[0:1] = gain
            affine[1:2] = bias

    for k in range(5):
        step(f"st{k}", stage, k)

    def tokens_in(k):
        for dy, dx in GROUPS[k]:
            tokens.wait(f"s{PLACES.index((dy, dx))}")
            qkv_unit(unit_of(dy, dx), raw, scaled, shift, table, qm, kv, q_rows, k_rows, v_rows)

    def up(k):
        tokens.wait(*(f"s{PLACES.index(pair)}" for pair in GRAD_GROUPS[k]))
        up_unit(lax.rem(y + k, 4), raw, scaled, shift, inner, slope)

    def copies():
        raw_copy.append(near.go(raw, raw_out))
        kept.extend([near.go(qm, qm_out), near.go(kv, kv_out), near.go(rows, rows_out)])

    def w_copy():
        kept.append(near.go(w.at[pl.ds(0, FIRST)], w_out))

    def inner_copy():
        kept.append(near.go(inner, inner_out))

    def clear():
        tokens.clear()
        raw_copy[0].wait()

    def branch(dy):
        branch_unit(lax.rem(y + dy, 4), inner, w, raw)
        for dx in range(2):
            rows = token_rows(y + dy, xl if dx == 0 else 1 - xl, 1 - c)
            swaps[dy, dx] = net.go(raw.at[rows], sibs.at[dy + 4 * dx], tokens.s)

    def branch_sum(dy):
        for dx in range(2):
            swaps[dy, dx].wait_recv()
            mine = raw.at[token_rows(y + dy, xl if dx == 0 else 1 - xl, c)]
            add_into(ROWS, mine, mine, sibs.at[dy + 4 * dx])
            kept.append(near.go(mine, branch_out.at[dy + 4 * dx]))

    def grads_in(k):
        grads.wait(*(f"s{PLACES.index(pair)}" for pair in GRAD_GROUPS[k]))
        part = at_unit(lax.rem(y + k, 4), 2 * UNIT)
        kept.append(near.go(gb.at[part], gb_out.at[part]))
        back_unit(part, gb, w, inner, slope, dom, do_rows, delta, dup)
        kept.append(near.go(dup.at[:, part], dup_out.at[:, part]))
        kept.append(near.go(do_rows.at[part], do_rows_out.at[part]))

    for k in range(6):
        step(f"q{k}", tokens_in, k)
    for k in range(4):
        step(f"k{k}", grads_in, k)
    step("wg0", scale_weights, 0, QKV, w, scaled, shift, affine)
    step("wg1", scale_weights, QKV, HIDDEN, w, scaled, shift, affine)
    for k in range(4):
        step(f"at{k}", attend_block, k, qm, kv, k_rows, inner, lse)
        step(f"u{k}", up, k)
        step(f"b{k}", branch, k)
        step(f"sa{k}", branch_sum, k)
    step("qc", copies)
    step("wc", w_copy)
    step("ic", inner_copy)
    step("clear", clear)

    rank = (z * 8 + xh * 4 + y) * 4 + xl * 2 + c
    wide = norm_ref[...]
    for _ in range(5):
        wide = jnp.concatenate([wide, wide], axis=1)
    rows_at = lax.broadcasted_iota(jnp.int32, (8, 512), 0)
    here = (lax.broadcasted_iota(jnp.int32, (8, 512), 1) // 16) == lax.rem(rank, 32)
    one = jnp.where(here & (rows_at == rank // 32), wide[0:1], 0.0)
    sums[0] = one + jnp.where(here & (rows_at == 4 + rank // 32), wide[1:2], 0.0)
    met()
    for work in gather_order(types.SimpleNamespace(**steps)):
        work()
    kept.append(near.go(dom, dom_out))
    grads.clear()
    net.drain()
    for copy in kept:
        copy.wait()


def gather(x, ct, aw, ew, cw, norm_rows, table):
    any_ref = pl.BlockSpec(memory_space=pl.ANY)
    vmem = pl.BlockSpec(memory_space=pltpu.VMEM)
    shape = jax.ShapeDtypeStruct
    outs = [
        (shape((LENGTH, D), bf16), any_ref),
        (shape((LENGTH, D), bf16), any_ref),
        (shape((FIRST, D), bf16), any_ref),
        (shape((8, 512), f32), vmem),
        (shape((2, 128, LENGTH), bf16), any_ref),
        (shape((256, LENGTH), bf16), any_ref),
        (shape((3, LENGTH, 128), bf16), any_ref),
        (shape((SECOND, LENGTH), bf16), any_ref),
        (shape((8, LENGTH), f32), vmem),
        (shape((8, ROWS, D), bf16), any_ref),
        (shape((2, 128, LENGTH), bf16), any_ref),
        (shape((LENGTH, 128), bf16), any_ref),
        (shape((8, LENGTH), f32), vmem),
        (shape((HIDDEN, LENGTH), bf16), any_ref),
    ]
    return pl.pallas_call(
        gather_kernel,
        name="gather",
        out_shape=[out for out, _ in outs],
        in_specs=[vmem, any_ref, vmem, any_ref, any_ref, vmem, vmem],
        out_specs=[spec for _, spec in outs],
        scratch_shapes=[
            pltpu.VMEM((LENGTH, D), bf16),
            pltpu.VMEM((LENGTH, D), bf16),
            pltpu.VMEM((WALL, D), bf16),
            pltpu.VMEM((FIRST, D), bf16),
            pltpu.VMEM((FIRST, 1), f32),
            pltpu.VMEM((KINDS, WROWS, D), bf16),
            pltpu.VMEM((5, 8, 512), f32),
            pltpu.VMEM((10, 8, 512), f32),
            pltpu.VMEM((2, 128, LENGTH), bf16),
            pltpu.VMEM((256, LENGTH), bf16),
            pltpu.VMEM((3, LENGTH, 128), bf16),
            pltpu.VMEM((SECOND, LENGTH), bf16),
            pltpu.VMEM((HIDDEN, LENGTH), f32),
            pltpu.VMEM((8, ROWS, D), bf16),
            pltpu.VMEM((8, D), f32),
            pltpu.VMEM((ROWS, D), f32),
            pltpu.VMEM((2, WROWS, D), f32),
            pltpu.VMEM((2, 128, LENGTH), bf16),
            pltpu.VMEM((LENGTH, 128), bf16),
            pltpu.VMEM((HIDDEN, LENGTH), bf16),
            pltpu.SemaphoreType.DMA((112,)),
            pltpu.SemaphoreType.DMA((112,)),
            pltpu.SemaphoreType.DMA((48,)),
        ],
        compiler_params=pltpu.CompilerParams(
            collective_id=1, has_side_effects=True, vmem_limit_bytes=60 << 20
        ),
    )(x, ct, aw, ew, cw, norm_rows, table)


class TokenScatter:
    def __init__(self, net, at, block, landed, out, around):
        self.around = around
        self.net, self.block, self.landed, self.out, self.got = net, block, landed, out, {}
        z, xh, y, xl, c = at
        self.x = device(z, xh, y, 1 - xl, c)
        self.p = device(z, xh, y + 1, xl, c)
        self.m = device(z, xh, y - 1, xl, c)

    def send(self, name, dy, dx, half, place, peer, *more):
        part = pl.ds(*((0, 64), (64, 64), (64, 32), (96, 32))[half])
        block, others = self.block(slot(dy, dx))
        terms = [ref.at[part] for ref in others] + [self.landed.at[k, part] for k in more]
        if terms:
            add_into(part.size, block.at[part], block.at[part], *terms)
        self.got[name] = self.net.go(block.at[part], self.landed.at[place, part], peer)

    def wait(self, *names):
        for name in names:
            self.got[name].wait_recv()

    def steps(self, tag):
        send, wait = self.send, self.wait

        def xo():
            send("xo1", 2, 1, 0, 0, self.x)
            if self.around:
                send("qa", 2, 1, 2, 7, self.m)
                send("qb", 2, 1, 3, 7, self.p)
            else:
                send("xo2", 2, 1, 1, 0, self.x)

        def quarter(name, dy, rows):
            if self.around:
                wait(name)
                block, _ = self.block(slot(dy, 1))
                part = pl.ds(rows, 32)
                add_into(32, block.at[part], block.at[part], self.landed.at[7, part])

        def lp():
            send("lp1", -1, 1, 0, 1, self.m)

        def lq():
            quarter("qa", -1, 64)
            send("lp2", -1, 1, 1, 1, self.m)

        def rp():
            send("rp1", 1, 1, 0, 2, self.p)

        def rq():
            quarter("qb", 1, 96)
            send("rp2", 1, 1, 1, 2, self.p)

        def oa():
            wait("xo1")
            send("a", 2, 0, 0, 3, self.m, 0)

        def ob():
            if self.around:
                send("b", 2, 0, 1, 3, self.p)
            else:
                wait("xo2")
                send("b", 2, 0, 1, 3, self.p, 0)

        def le():
            send("l2", -1, 0, 1, 4, self.m)

        def re():
            send("r1", 1, 0, 0, 5, self.p)

        def nl():
            wait("a")
            send("l1", -1, 0, 0, 4, self.m, 3)

        def nr():
            wait("b")
            send("r2", 1, 0, 1, 5, self.p, 3)

        def p1():
            wait("lp1", "rp1")
            send("p1", 0, 1, 0, 6, self.x, 1, 2)

        def p2():
            wait("lp2", "rp2")
            send("p2", 0, 1, 1, 6, self.x, 1, 2)

        def fi():
            wait("l1", "l2", "r1", "r2", "p1", "p2")
            block, others = self.block(slot(0, 0))
            add_into(ROWS, self.out, block, *others, *(self.landed.at[k] for k in (4, 5, 6)))

        parts = (xo, lp, rp, lq, rq, oa, ob, le, re, nl, nr, p1, p2, fi)
        return {tag + part.__name__: part for part in parts}


class WeightScatter:
    def __init__(self, net, at, part, kind, landed, out):
        self.net, self.at, self.part, self.kind = net, at, part, kind
        self.landed, self.out = landed, out
        z, xh, y, xl, c = at
        self.h = device(z, 1 - xh, y, xl, c)
        self.p = device(z + 1, xh, y, xl, c)
        self.m = device(z - 1, xh, y, xl, c)
        self.got = {}

    def rows(self, dz, dh, half=None):
        z, xh = self.at[:2]
        start, size = (0, WROWS) if half is None else (half * 32, 32)
        return self.part.at[
            weight_rows(self.kind, z + dz, xh if dh == 0 else 1 - xh, start, size)
        ]

    def send(self, src, place, peer, half=None):
        start, size = (0, WROWS) if half is None else (half * 32, 32)
        return self.net.go(src, self.landed.at[place, pl.ds(start, size)], peer)

    def steps(self):
        got = self.got

        def op():
            for dh in (1, 0):
                got["a", dh] = self.send(self.rows(2, dh, 0), dh, self.m, 0)
                got["b", dh] = self.send(self.rows(2, dh, 1), dh, self.p, 1)

        def left(dh):
            got["a", dh].wait_recv()
            half = self.rows(-1, dh, 0)
            add_into(32, half, half, self.landed.at[dh, pl.ds(0, 32)])
            got["l", dh] = self.send(self.rows(-1, dh), 2 + dh, self.m)

        def right(dh):
            got["b", dh].wait_recv()
            half = self.rows(1, dh, 1)
            add_into(32, half, half, self.landed.at[dh, pl.ds(32, 32)])
            got["r", dh] = self.send(self.rows(1, dh), 4 + dh, self.p)

        def pa():
            got["l", 1].wait_recv()
            got["r", 1].wait_recv()
            other = self.rows(0, 1)
            add_into(WROWS, other, other, self.landed.at[3], self.landed.at[5])
            got["p"] = self.send(other, 6, self.h)

        def fi():
            for name in (("l", 0), ("r", 0), "p"):
                got[name].wait_recv()
            add_into(
                WROWS, self.out, self.rows(0, 0),
                self.landed.at[2], self.landed.at[4], self.landed.at[6],
            )

        tag = f"W{self.kind}"
        return {
            tag + "op": op,
            tag + "l1": lambda: left(1),
            tag + "l0": lambda: left(0),
            tag + "r1": lambda: right(1),
            tag + "r0": lambda: right(0),
            tag + "pa": pa,
            tag + "fi": fi,
        }


TILE = 512
TILES = D // TILE


def factors_of(moments):
    eye = lax.broadcasted_iota(jnp.int32, (HD, HD), 0) == lax.broadcasted_iota(jnp.int32, (HD, HD), 1)
    one = jnp.where(eye, 1.0, 0.0)

    def each(work, *lists):
        return [work(*items) for items in zip(*lists)]

    def gram_of(moment):
        both = jnp.concatenate(split(moment), axis=0)
        gram = dot(both, both, nt)
        return gram[:HD, :HD] + gram[HD:, HD:] + (gram[:HD, HD:] + gram[HD:, :HD])

    def size_of(gram):
        size = jnp.sum(jnp.where(eye, gram, 0.0), axis=1, keepdims=True)
        return jnp.sqrt(jnp.sum(size, axis=0, keepdims=True)) + 1e-07

    grams = each(gram_of, moments)
    sizes = each(size_of, grams)
    grams = each(lambda gram, size: gram / size / size, grams, sizes)
    wholes = None
    for turn_at in range(NS_STEPS):
        squares = each(times, grams, grams)
        steps = each(lambda a, b: polish_a * one + polish_b * a + polish_c * b, grams, squares)
        wholes = steps if turn_at == 0 else each(times, steps, wholes)
        if turn_at < NS_STEPS - 1:
            grams = each(times, steps, each(times, grams, steps))
    return each(lambda whole, size: whole / size, wholes, sizes)


def scatter_order(s):
    return (
        s.Rlp, s.Rrp, s.Rxo, s.sec0, s.sec1, s.Rlq, s.W2op, s.Rrq, s.Rle, s.E0, s.E1, s.W1op, s.Rp1,
        s.W2l1, s.Rre, s.Roa, s.W2r1, s.Rob, s.bk0, s.Rp2, s.W1r1, s.W1l1, s.bk1, s.bk2, s.bk3, s.W2r0,
        s.Rnl, s.Rnr, s.qb, s.W2pa, s.gB, s.gA, s.Dxo, s.W2l0, s.qk0, s.Dlp, s.Drp, s.qk1, s.st0,
        s.W1pa, s.W0op, s.gD, s.st1, s.Dlq, s.Dob, s.Drq, s.Rfi, s.W0r1, s.W0l1, s.W1l0, s.st2, s.gC,
        s.Doa, s.Dp1, s.st3, s.Dle, s.W1r0, s.st4, s.W0pa, s.Dre, s.Dnl, s.W0l0, s.Dnr, s.W0r0, s.W2fi,
        s.W1fi, s.Dp2, s.f12, s.W0fi, s.f0, s.Dfi,
    )


def scatter_kernel(
    raw_ref, gb_ref, w_ref, branch_ref, qm_ref, kv_ref, rows_ref, inner_ref, dom_ref, do_rows_ref, dup_ref,
    am_ref, em_ref, cm_ref, lse, delta, gain_ref, table,
    branch_res, dnormed_out, wgrad_res, factor_out, norm_out,
    branch_out, wgrad_out, mine, part, sibs, landed, wpart, wlanded, w, early, outer, tiles, rows, dom, do_rows, dq, moments,
    affine, norm_part, sums, nlanded, send, recv, local, tile_sems,
):
    at = place()
    z, xh, y, xl, c = at
    net, near = Net(send, recv), Local(local)
    stages = stage_peers(at)
    sib = device(z, xh, y, xl, 1 - c)
    steps, swaps = {}, {}
    met = greet([peer for stage in stages for peer in stage])

    def step(name, work, *args):
        steps[name] = functools.partial(work, *args)

    def fetch(n):
        src = gb_ref if n < TILES else raw_ref
        cols = pl.ds(n % TILES * TILE, TILE)
        return pltpu.make_async_copy(src.at[:, cols], tiles.at[n % 2], tile_sems.at[n % 2])

    fetch(0).start()
    inner_load = near.go(inner_ref, early)
    branch_slots = {slot(dy, dx): k for k, (dy, dx) in enumerate(PLACES[:5])}
    branch_loads = {s: near.go(branch_ref.at[s], mine.at[k]) for s, k in branch_slots.items()}
    first_loads = [near.go(dup_ref, outer.at[pl.ds(QKV, HIDDEN)]), near.go(w_ref, w)]
    attn_loads = [near.go(rows_ref, rows), near.go(dom_ref, dom), near.go(do_rows_ref, do_rows)]
    moment_loads = [near.go(ref, moments.at[k]) for k, ref in enumerate((am_ref, em_ref, cm_ref))]

    def branch_block(s):
        if s not in branch_slots:
            return branch_ref.at[s], []
        load = branch_loads.pop(s, None)
        if load is not None:
            load.wait()
        return mine.at[branch_slots[s]], []

    def dnormed_block(s):
        swap = swaps.pop(s, None)
        if swap is not None:
            swap.wait_recv()
        return part.at[c, s], [sibs.at[s]]

    def factors(*kinds):
        for kind in kinds:
            moment_loads[kind].wait()
        found = factors_of([muon_beta * moments[kind] + wgrad_out[kind] for kind in kinds])
        for kind, factor in zip(kinds, found):
            factor_out[kind] = factor

    step("f12", factors, 1, 2)
    step("f0", factors, 0)
    kept = []

    def keep(name, src, dst):
        work = steps[name]

        def then():
            work()
            kept.append(near.go(src, dst))

        steps[name] = then

    steps |= TokenScatter(net, at, branch_block, landed.at[0], branch_out, False).steps("R")
    steps |= TokenScatter(net, at, dnormed_block, landed.at[1], dnormed_out, True).steps("D")
    for kind in range(KINDS):
        steps |= WeightScatter(
            net, at, wpart, kind, wlanded.at[kind], wgrad_out.at[kind]
        ).steps()

        keep(f"W{kind}fi", wgrad_out.at[kind], wgrad_res.at[kind])
    keep("Rfi", branch_out, branch_res)

    def tile_in(n):
        if n + 1 < 3 * TILES:
            fetch(n + 1).start()
        fetch(n).wait()
        return pl.ds(n % TILES * TILE, TILE), tiles.at[n % 2]

    def second_pass(half):
        if half == 0:
            inner_load.wait()
        for n in range(half * TILES // 2, (half + 1) * TILES // 2):
            cols, tile = tile_in(n)
            wpart[pl.ds(FIRST, SECOND), cols] = dot(early[...], tile[...], nn).astype(bf16)
        if half == 1:
            attn_loads.extend(
                [near.go(qm_ref.at[h], early.at[pl.ds(h * 128, 128)]) for h in range(2)]
            )
            attn_loads.append(near.go(kv_ref, early.at[pl.ds(256, 256)]))

    def first_pass(start, size, base, half):
        if base == TILES and half == 0:
            for load in first_loads:
                load.wait()
        span = pl.ds(start, size)
        total = dot(outer[span], jnp.ones((LENGTH, 128), bf16), nn)[:, :1]
        for n in range(base + half * TILES // 2, base + (half + 1) * TILES // 2):
            cols, tile = tile_in(n)
            summed = dot(outer[span], tile[...], nn)
            wpart[span, cols] = (summed * affine[0:1, cols] + total * affine[1:2, cols]).astype(bf16)
            block = w[span, cols].astype(f32)
            by_gain = jnp.sum(block * summed, axis=0, keepdims=True)
            by_bias = jnp.sum(block * total, axis=0, keepdims=True)
            if base == TILES:
                norm_part[0:1, cols] = by_gain
                norm_part[1:2, cols] = by_bias
            else:
                norm_part[0:1, cols] += by_gain
                norm_part[1:2, cols] += by_bias

    for half in range(2):
        step(f"sec{half}", second_pass, half)
        step(f"E{half}", first_pass, QKV, HIDDEN, TILES, half)
        step(f"qk{half}", first_pass, 0, QKV, 2 * TILES, half)

    def back(kb):
        if kb == 0:
            for load in attn_loads:
                load.wait()
        attend_back_block(
            kb, early.at[pl.ds(0, 256)], early.at[pl.ds(256, 256)], rows.at[0], rows.at[1], rows.at[2],
            dom, do_rows, lse, delta, dq, outer, table,
        )

    for kb in range(LENGTH // QB):
        step(f"bk{kb}", back, kb)
    step("qb", query_back, dq, outer, table)

    def dnormed_unit(dy, dx):
        unit = lax.rem(y + dy, 4) * 2 + lax.rem(xl + dx, 2)
        block = dot(outer[:, at_unit(unit)], w[...], tn).astype(bf16)
        s = dy + 4 * dx
        part[0, s] = block[:ROWS]
        part[1, s] = block[ROWS:]

    def swap(dy, dx):
        s = slot(dy, dx)
        swaps[s] = net.go(part.at[1 - c, s], sibs.at[s], sib)

    def dnormed_of(*pairs):
        (dy, dx), (sy, sx) = pairs

        @pl.loop(0, 2)
        def _(i):
            dnormed_unit(dy % 4 + (sy % 4 - dy % 4) * i, dx + (sx - dx) * i)

        for pair in pairs:
            swap(*pair)

    step("gA", dnormed_of, (1, 1), (-1, 1))
    step("gB", dnormed_of, (2, 1), (2, 0))
    step("gC", dnormed_of, (1, 0), (-1, 0))
    step("gD", dnormed_of, (0, 1), (0, 0))
    staged = Staged(net, stages, sums, nlanded)

    def stage(k):
        if k == 0:
            for kind in range(2):
                for q in range(4):
                    sums[0, pl.ds(kind * 4 + q, 1)] = norm_part[pl.ds(kind, 1), pl.ds(q * 512, 512)]
        else:
            staged.finish()
        if k < 4:
            staged.start()
        else:
            norm_out[...] = sums[4]

    for k in range(5):
        step(f"st{k}", stage, k)

    gain, bias = spread(gain_ref[...])
    affine[0:1] = gain
    affine[1:2] = bias
    met()
    for work in scatter_order(types.SimpleNamespace(**steps)):
        work()
    net.drain()
    for copy in kept:
        copy.wait()


def scatter(*args):
    any_ref = pl.BlockSpec(memory_space=pl.ANY)
    vmem = pl.BlockSpec(memory_space=pltpu.VMEM)
    return pl.pallas_call(
        scatter_kernel,
        name="scatter",
        out_shape=(
            jax.ShapeDtypeStruct((ROWS, D), f32),
            jax.ShapeDtypeStruct((ROWS, D), f32),
            jax.ShapeDtypeStruct((KINDS, WROWS, D), f32),
            jax.ShapeDtypeStruct((KINDS, HD, HD), f32),
            jax.ShapeDtypeStruct((8, 512), f32),
        ),
        in_specs=[any_ref] * 14 + [vmem] * 4,
        out_specs=(any_ref, vmem, any_ref, vmem, vmem),
        scratch_shapes=[
            pltpu.VMEM((ROWS, D), f32),
            pltpu.VMEM((KINDS, WROWS, D), f32),
            pltpu.VMEM((5, ROWS, D), bf16),
            pltpu.VMEM((2, 8, ROWS, D), bf16),
            pltpu.VMEM((8, ROWS, D), bf16),
            pltpu.VMEM((2, 8, ROWS, D), bf16),
            pltpu.VMEM((WALL, D), bf16),
            pltpu.VMEM((KINDS, 7, WROWS, D), bf16),
            pltpu.VMEM((FIRST, D), bf16),
            pltpu.VMEM((SECOND, LENGTH), bf16),
            pltpu.VMEM((FIRST, LENGTH), bf16),
            pltpu.VMEM((2, LENGTH, TILE), bf16),
            pltpu.VMEM((3, LENGTH, 128), bf16),
            pltpu.VMEM((2, 128, LENGTH), bf16),
            pltpu.VMEM((LENGTH, 128), bf16),
            pltpu.VMEM((128, LENGTH), f32),
            pltpu.VMEM((KINDS, WROWS, D), f32),
            pltpu.VMEM((8, D), f32),
            pltpu.VMEM((8, D), f32),
            pltpu.VMEM((5, 8, 512), f32),
            pltpu.VMEM((10, 8, 512), f32),
            pltpu.SemaphoreType.DMA((112,)),
            pltpu.SemaphoreType.DMA((112,)),
            pltpu.SemaphoreType.DMA((32,)),
            pltpu.SemaphoreType.DMA((2,)),
        ],
        compiler_params=pltpu.CompilerParams(
            collective_id=2, has_side_effects=True, vmem_limit_bytes=63 << 20
        ),
    )(*args)


def update_kernel(
    x_ref, ct_ref, branch_ref, dnormed_ref, gain_ref, share_ref, factor_ref,
    aw, ew, cw, am, em, cm, norm_ref, params, first, second,
    state_out, grad_out, ag, an, aweight, eg, en, eweight, cg, cn, cweight,
    norm_out, first_out, second_out, params_out,
):
    @pl.when(pl.program_id(0) == 0)
    def _():
        z, xh, y, xl, c = place()
        rank = (z * 8 + xh * 4 + y) * 4 + xl * 2 + c
        for kind in range(2):
            row = norm_ref[pl.ds(kind * 4 + rank // 32, 1)]
            row = pltpu.roll(row, lax.rem(512 - 16 * lax.rem(rank, 32), 512), 1)
            norm_out[pl.ds(kind, 1)] = row[:, :16]
        share = norm_out[...]
        first_next = adam_first * first[...] + (1.0 - adam_first) * share
        second_next = adam_second * second[...] + (1.0 - adam_second) * share * share
        first_out[...] = first_next
        second_out[...] = second_next
        first_fix = 1.0 - adam_first**STEP
        second_fix = 1.0 - adam_second**STEP
        params_out[...] = params[...] - adam_rate * (first_next / first_fix) / (
            jnp.sqrt(second_next / second_fix) + adam_eps
        )

    x, dnormed = x_ref[...], dnormed_ref[...]
    state_out[...] = x + branch_ref[...]
    centred = x - jnp.mean(x, axis=1, keepdims=True)
    inverse = lax.rsqrt(jnp.mean(centred * centred, axis=1, keepdims=True) + eps_norm)
    xhat = centred * inverse
    scaled = dnormed * spread(gain_ref[...])[0]
    grad_out[...] = ct_ref[...] + inverse * (
        scaled
        - jnp.mean(scaled, axis=1, keepdims=True)
        - xhat * jnp.mean(scaled * xhat, axis=1, keepdims=True)
    )
    kinds = ((aw, am, ag, an, aweight), (ew, em, eg, en, eweight), (cw, cm, cg, cn, cweight))
    for k, (weight, moment, grad, moment_next, weight_next) in enumerate(kinds):
        share = share_ref[k]
        grad[...] = share
        following = muon_beta * moment[...] + share
        moment_next[...] = following
        ortho = times(factor_ref[k], following)
        old = weight[...]
        weight_next[...] = old - muon_rate * (muon_decay * old + 0.2 * math.sqrt(D) * ortho)


def update(x, ct, branch, dnormed, gain_rows, shares, factors, *others):
    steps = 2
    token = pl.BlockSpec((ROWS // steps, D), lambda i: (i, 0))
    block = pl.BlockSpec((WROWS, D // steps), lambda i: (0, i))
    norm = pl.BlockSpec((2, 16), lambda i: (0, 0))
    shape = jax.ShapeDtypeStruct
    return pl.pallas_call(
        update_kernel,
        name="update",
        grid=(steps,),
        out_shape=[shape((ROWS, D), f32)] * 2 + [shape((WROWS, D), f32)] * 9 + [shape((2, 16), f32)] * 4,
        in_specs=[token] * 4
        + [
            pl.BlockSpec((8, 512), lambda i: (0, 0)),
            pl.BlockSpec((KINDS, WROWS, D // steps), lambda i: (0, 0, i)),
            pl.BlockSpec((KINDS, HD, HD), lambda i: (0, 0, 0)),
        ]
        + [block] * 6
        + [pl.BlockSpec((8, 512), lambda i: (0, 0))]
        + [norm] * 3,
        out_specs=[token] * 2 + [block] * 9 + [norm] * 4,
        compiler_params=pltpu.CompilerParams(vmem_limit_bytes=60 << 20),
    )(x, ct, branch, dnormed, gain_rows, shares, factors, *others)


def angles():
    half = ROT // 2
    freq = rope_base ** (-2.0 * np.arange(half) / ROT)
    turned = freq[:, None] * np.arange(LENGTH)[None, :]
    return jnp.asarray(np.concatenate([np.cos(turned), np.sin(turned)]).astype(np.float32))


def body(
    inputs, cotangent, attn_weight, expand_weight, contract_weight, norm_params,
    attn_moment, expand_moment, contract_moment, norm_first, norm_second,
):
    table = angles()
    (
        raw, grad_group, first_w, norm_rows, qm, kv, rows, inner, lse, branch,
        dom, do_rows, delta, dup,
    ) = gather(
        inputs,
        cotangent,
        attn_weight[0, 0],
        expand_weight[0],
        contract_weight[0],
        norm_params[0],
        table,
    )
    blocks = (attn_weight[0, 0], expand_weight[0], contract_weight[0])
    moments = (attn_moment[0, 0], expand_moment[0], contract_moment[0])
    branch, dnormed, shares, factors, norm_total = scatter(
        raw, grad_group, first_w, branch, qm, kv, rows, inner, dom, do_rows, dup,
        *moments, lse, delta, norm_rows, table,
    )
    state, grad_state, *updates = update(
        inputs, cotangent, branch, dnormed, norm_rows, shares, factors, *blocks, *moments,
        norm_total, norm_params[0], norm_first[0], norm_second[0],
    )
    shapes = [attn_weight.shape] * 3 + [expand_weight.shape] * 6 + [norm_params.shape] * 4
    return state, grad_state, *(part.reshape(shape) for part, shape in zip(updates, shapes))


def solution(mesh):
    return jax.shard_map(
        body,
        mesh=mesh,
        in_specs=(
            P(("fsdp", "seq", "mp"), None),
            P(("fsdp", "seq", "mp"), None),
            P(None, ("fsdp", "seq", "mp"), None, None),
            P(None, ("fsdp", "seq", "mp"), None),
            P(None, ("fsdp", "seq", "mp"), None),
            P(None, None, ("fsdp", "seq", "mp")),
            P(None, ("fsdp", "seq", "mp"), None, None),
            P(None, ("fsdp", "seq", "mp"), None),
            P(None, ("fsdp", "seq", "mp"), None),
            P(None, None, ("fsdp", "seq", "mp")),
            P(None, None, ("fsdp", "seq", "mp")),
        ),
        out_specs=(
            P(("fsdp", "seq", "mp"), None),
            P(("fsdp", "seq", "mp"), None),
            P(None, ("fsdp", "seq", "mp"), None, None),
            P(None, ("fsdp", "seq", "mp"), None, None),
            P(None, ("fsdp", "seq", "mp"), None, None),
            P(None, ("fsdp", "seq", "mp"), None),
            P(None, ("fsdp", "seq", "mp"), None),
            P(None, ("fsdp", "seq", "mp"), None),
            P(None, ("fsdp", "seq", "mp"), None),
            P(None, ("fsdp", "seq", "mp"), None),
            P(None, ("fsdp", "seq", "mp"), None),
            P(None, None, ("fsdp", "seq", "mp")),
            P(None, None, ("fsdp", "seq", "mp")),
            P(None, None, ("fsdp", "seq", "mp")),
            P(None, None, ("fsdp", "seq", "mp")),
        ),
        check_vma=False,
    )
```

```python
import functools
import math
import types

import jax
import jax.numpy as jnp
import numpy as np
from jax import lax
from jax.experimental import pallas as pl
from jax.experimental.pallas import tpu as pltpu
from jax.sharding import PartitionSpec as P

D = 2048
H = 32
HD = 64
ROT = 32
LENGTH = 2048
NS_STEPS = 5
STEP = 10
ROWS = 128
WROWS = 64
KINDS = 3
QKV = 384
HIDDEN = 512
FIRST = QKV + HIDDEN
SECOND = 128 + HIDDEN
WALL = FIRST + SECOND

eps_norm = 1e-05
rope_base = 10000.0
muon_beta = 0.95
muon_rate = 0.15
muon_decay = 0.01
polish_a = 3.4445
polish_b = -4.775
polish_c = 2.0315
adam_first = 0.9
adam_second = 0.95
adam_rate = 0.5
adam_eps = 1e-08
masked_score = -1e30
highest = lax.Precision.HIGHEST
across = (((1,), (1,)), ((), ()))
downward = (((0,), (0,)), ((), ()))
MESH = pl.DeviceIdType.MESH
f32 = jnp.float32
bf16 = jnp.bfloat16


def place():
    z = lax.axis_index("fsdp")
    s = lax.axis_index("seq")
    m = lax.axis_index("mp")
    return z, s // 4, lax.rem(s, 4), m // 2, lax.rem(m, 2)


def device(z, xh, y, xl, c):
    return (lax.rem(z + 4, 4), xh * 4 + lax.rem(y + 4, 4), xl * 2 + c)


def token_rows(y, xl, c, start=0, size=ROWS):
    block = lax.rem(y + 4, 4) * 4 + xl * 2 + c
    return pl.ds(pl.multiple_of(block * ROWS + start, 32), size)


def weight_rows(kind, z, xh, start=0, size=WROWS):
    z = lax.rem(z + 4, 4)
    if kind == 0:
        base = z * 128 + (z // 3) * HIDDEN + xh * 64
    elif kind == 1:
        base = QKV + z * 128 + xh * 64
    else:
        base = FIRST + 128 + z * 128 + xh * 64
    return pl.ds(pl.multiple_of(base + start, 32), size)


class Net:
    def __init__(self, send, recv):
        self.send, self.recv, self.used, self.sent = send, recv, 0, []

    def go(self, src, dst, peer, sent=None):
        slot = self.used
        self.used += 1
        copy = pltpu.make_async_remote_copy(
            src_ref=src,
            dst_ref=dst,
            send_sem=self.send.at[slot],
            recv_sem=self.recv.at[slot],
            device_id=peer,
            device_id_type=MESH,
        )
        copy.start()
        (self.sent if sent is None else sent).append(copy)
        return copy

    def drain(self):
        for copy in self.sent:
            copy.wait_send()
        self.sent = []


class Local:
    def __init__(self, sems):
        self.sems, self.used = sems, 0

    def go(self, src, dst):
        copy = pltpu.make_async_copy(src, dst, self.sems.at[self.used])
        self.used += 1
        copy.start()
        return copy


def greet(peers):
    barrier = pltpu.get_barrier_semaphore()
    for peer in peers:
        pl.semaphore_signal(barrier, inc=1, device_id=peer, device_id_type=MESH)
    return lambda: pl.semaphore_wait(barrier, len(peers))


def stage_peers(at):
    z, xh, y, xl, c = at
    return [
        [device(z + k, xh, y, xl, c) for k in (1, 2, 3)],
        [device(z, xh, y + k, xl, c) for k in (1, 2, 3)],
        [
            device(z, xh, y, 1 - xl, c),
            device(z, 1 - xh, y, xl, c),
            device(z, 1 - xh, y, 1 - xl, c),
        ],
        [device(z, xh, y, xl, 1 - c)],
    ]


class Staged:
    def __init__(self, net, stages, sums, landed):
        self.net, self.stages, self.sums, self.landed = net, stages, sums, landed
        self.stage = self.slot = 0

    def start(self):
        self.copies = [
            self.net.go(self.sums.at[self.stage], self.landed.at[self.slot + k], peer)
            for k, peer in enumerate(self.stages[self.stage])
        ]

    def finish(self):
        total = self.sums[self.stage]
        for copy in self.copies:
            copy.wait_recv()
            total = total + self.landed[self.slot]
            self.slot += 1
        self.stage += 1
        self.sums[self.stage] = total


def spread(flat):
    gain = jnp.concatenate([flat[k : k + 1] for k in range(4)], axis=1)
    bias = jnp.concatenate([flat[k : k + 1] for k in range(4, 8)], axis=1)
    return gain, bias


class TokenGather:
    def __init__(self, net, at, full, around):
        self.net, self.at, self.full, self.sent, self.got = net, at, full, [], {}
        self.waited = set()
        self.around = around
        z, xh, y, xl, c = at
        self.x = device(z, xh, y, 1 - xl, c)
        self.p = device(z, xh, y + 1, xl, c)
        self.m = device(z, xh, y - 1, xl, c)
        self.s = device(z, xh, y, xl, 1 - c)

    def rows(self, dy, dx, half=None):
        z, xh, y, xl, c = self.at
        start, size = (0, ROWS) if half is None else ((0, 64), (64, 64), (64, 32), (96, 32))[half]
        return self.full.at[token_rows(y + dy, xl if dx == 0 else 1 - xl, c, start, size)]

    def go(self, name, peer, dy, dx, half=None, block=None):
        here = self.rows(dy, dx, half)
        src = here
        if block is not None:
            src = block if half is None else block.at[pl.ds(half * 64, 64)]
        self.got[name] = self.net.go(src, here, peer, self.sent)

    def wait(self, *names):
        for name in names:
            if name not in self.waited:
                self.got[name].wait_recv()
                self.waited.add(name)

    def clear(self):
        for copy in self.sent:
            copy.wait_send()

    def steps(self, tag, block):
        go, wait = self.go, self.wait

        def own1():
            go("l1", self.p, 0, 0, 0, block)
            go("r1", self.m, 0, 0, 1, block)

        def own2():
            go("l2", self.p, 0, 0, 1, block)
            go("r2", self.m, 0, 0, 0, block)
            go("s0", self.s, 0, 0, None, block)

        def ownp():
            go("p1", self.x, 0, 0, 0, block)
            go("p2", self.x, 0, 0, 1, block)

        def nl():
            wait("l1")
            go("a", self.p, -1, 0, 0)

        def nr():
            wait("r1")
            go("b", self.m, 1, 0, 1)

        def sl():
            wait("l2")
            go("s1", self.s, -1, 0)

        def sr():
            wait("r2")
            go("s2", self.s, 1, 0)

        def np1():
            wait("p1")
            go("lp1", self.p, 0, 1, 0)
            go("rp1", self.m, 0, 1, 0)

        def np2():
            wait("p2")
            go("lp2", self.p, 0, 1, 1)
            go("rp2", self.m, 0, 1, 1)
            go("s3", self.s, 0, 1)

        def fa():
            wait("a")
            go("xo1", self.x, 2, 0, 0)

        def fb():
            wait("b")
            if not self.around:
                go("xo2", self.x, 2, 0, 1)
            go("s4", self.s, 2, 0)

        def e1():
            wait("lp1", "lp2")
            if self.around:
                go("qa", self.p, -1, 1, 2)
            go("s5", self.s, -1, 1)

        def e2():
            wait("rp1", "rp2")
            if self.around:
                go("qb", self.m, 1, 1, 3)
            go("s6", self.s, 1, 1)

        def e3():
            wait("xo1", *(("qa", "qb") if self.around else ("xo2",)))
            go("s7", self.s, 2, 1)

        parts = (own1, own2, ownp, nl, nr, sl, sr, np1, np2, fa, fb, e1, e2, e3)
        return {tag + part.__name__: part for part in parts}


class WeightGather:
    def __init__(self, net, near, at, full, kind, own_w, block, load):
        self.net, self.near, self.at, self.full, self.kind, self.got = net, near, at, full, kind, {}
        self.own_w, self.block, self.load = own_w, block, load
        z, xh, y, xl, c = at
        self.h = device(z, 1 - xh, y, xl, c)
        self.p = device(z + 1, xh, y, xl, c)
        self.m = device(z - 1, xh, y, xl, c)

    def rows(self, dz, dh, half=None):
        z, xh = self.at[:2]
        start, size = (0, WROWS) if half is None else (half * 32, 32)
        return self.full.at[
            weight_rows(self.kind, z + dz, xh if dh == 0 else 1 - xh, start, size)
        ]

    def go(self, name, peer, dz, dh, half, own=False):
        here = self.rows(dz, dh, half)
        src = self.own_w.at[pl.ds(half * 32, 32)] if own else here
        self.got[name] = self.net.go(src, here, peer)

    def wait(self, *names):
        for name in names:
            self.got[name].wait_recv()

    def steps(self):
        go, wait = self.go, self.wait

        def own():
            if self.load is not None:
                self.load.wait()
            self.own_w[...] = self.block[...].astype(bf16)
            go("l1", self.p, 0, 0, 0, True)
            go("r1", self.m, 0, 0, 1, True)
            go("l2", self.p, 0, 0, 1, True)
            go("r2", self.m, 0, 0, 0, True)
            self.copy = self.near.go(self.own_w, self.rows(0, 0))

        def ownp():
            go("p1", self.h, 0, 0, 0, True)
            go("p2", self.h, 0, 0, 1, True)

        def na():
            wait("l1", "r1")
            go("a", self.p, -1, 0, 0)
            go("b", self.m, 1, 0, 1)

        def np1():
            wait("p1")
            go("lp1", self.p, 0, 1, 0)
            go("rp1", self.m, 0, 1, 0)

        def np2():
            wait("p2")
            go("rp2", self.m, 0, 1, 1)
            go("lp2", self.p, 0, 1, 1)

        def fl():
            wait("lp1")
            go("ha", self.p, -1, 1, 0)

        def fr():
            wait("rp2")
            go("hb", self.m, 1, 1, 1)

        def end():
            wait("l2", "r2", "a", "b", "lp2", "rp1", "ha", "hb")
            self.copy.wait()

        parts = (own, ownp, na, np1, np2, fl, fr, end)
        return {f"W{self.kind}" + part.__name__: part for part in parts}


nn = (((1,), (0,)), ((), ()))
nt = (((1,), (1,)), ((), ()))
tn = (((0,), (0,)), ((), ()))
QB = 512
UNIT = 256


def dot(a, b, dims):
    return lax.dot_general(a, b, dims, preferred_element_type=f32)


def at_unit(unit, size=UNIT):
    return pl.ds(pl.multiple_of(unit * size, size), size)


def turn(part, cosine, sine):
    rows = []
    for low in (0, HD):
        first, second = part[low : low + 16], part[low + 16 : low + 32]
        rows += [first * cosine - second * sine, second * cosine + first * sine]
        rows.append(part[low + 32 : low + HD])
    return jnp.concatenate(rows, axis=0)


def of_head(h, block, axis):
    place = lax.broadcasted_iota(jnp.int32, block.shape, axis)
    return jnp.where((place < HD) == (h == 0), block, 0.0)


def gelu_pair(v):
    square = v * v
    t = jnp.tanh(math.sqrt(2 / math.pi) * (v + 0.044715 * (v * square)))
    plus = 0.5 * (1.0 + t)
    slope = plus + (0.5 * v) * (1.0 - t * t) * (
        math.sqrt(2 / math.pi) * (1.0 + 3 * 0.044715 * square)
    )
    return v * plus, slope


def split(a):
    high = a.astype(bf16)
    return high, (a - high.astype(f32)).astype(bf16)


def times(a, b):
    (ah, al), (bh, bl) = split(a), split(b)
    return dot(
        jnp.concatenate([ah, ah, al, al], axis=1), jnp.concatenate([bh, bl, bh, bl], axis=0), nn
    )


def scale_weights(start, size, w, scaled, shift, affine):
    high, low = split(affine[1:2])
    pair = jnp.concatenate([high, low] * 8, axis=0)
    by_bias = dot(w[pl.ds(start, size)], pair, nt)
    shift[pl.ds(start, size)] = by_bias[:, 0:1] + by_bias[:, 1:2]

    @pl.loop(0, size // 32)
    def _(i):
        part = pl.ds(pl.multiple_of(start + i * 32, 32), 32)
        scaled[part] = (w[part].astype(f32) * affine[0:1]).astype(bf16)


def qkv_unit(unit, raw, w, shift, table, qm, kv, q_rows, k_rows, v_rows):
    cols = at_unit(unit)
    lin = dot(w[pl.ds(0, QKV)], raw[cols], nt) + shift[0:QKV]
    cosine, sine = table[0:16, cols], table[16:32, cols]
    q = turn(lin[0:128], cosine, sine).astype(bf16).astype(f32) * HD**-0.5
    k = turn(lin[128:256], cosine, sine)
    v = lin[256:384]
    for h in range(2):
        qm[h, :, cols] = of_head(h, q, 0).astype(bf16)
    kv[pl.ds(0, 128), cols] = k.astype(bf16)
    kv[pl.ds(128, 128), cols] = v.astype(bf16)
    q_rows[cols] = q.T.astype(bf16)
    k_rows[cols] = k.T.astype(bf16)
    v_rows[cols] = v.T.astype(bf16)


def up_unit(unit, raw, w, shift, inner, slope):
    cols = at_unit(unit, 2 * UNIT)
    act, der = gelu_pair(dot(w[pl.ds(QKV, HIDDEN)], raw[cols], nt) + shift[pl.ds(QKV, HIDDEN)])
    inner[pl.ds(128, HIDDEN), cols] = act.astype(bf16)
    slope[:, cols] = der


def branch_unit(unit, inner, w, out):
    rows = at_unit(unit, 2 * UNIT)
    out[rows] = dot(inner[:, rows], w[pl.ds(FIRST, SECOND)], tn).astype(bf16)


def back_unit(cols, gb, w, inner, slope, dom, do_rows, delta, dup):
    lin = dot(w[pl.ds(FIRST, SECOND)], gb[cols], nt)
    do = lin[0:128].astype(bf16).astype(f32)
    for h in range(2):
        dom[h, :, cols] = of_head(h, do, 0).astype(bf16)
    do_rows[cols] = do.T.astype(bf16)
    both = do * inner[pl.ds(0, 128), cols].astype(f32)
    for h in range(2):
        delta[pl.ds(h, 1), cols] = jnp.sum(both[h * HD : h * HD + HD], axis=0, keepdims=True)
    dup[:, cols] = (lin[128:] * slope[:, cols]).astype(bf16)


def causal_mask(scores):
    rows = lax.broadcasted_iota(jnp.int32, scores.shape, 0)
    cols = lax.broadcasted_iota(jnp.int32, scores.shape, 1)
    return jnp.where(rows <= cols, scores, masked_score)


def attend_block(qb, qm, kv, k_rows, inner, lse):
    cols = at_unit(qb, QB)
    start = (jnp.full((1, QB), masked_score, f32), jnp.zeros((1, QB), f32), jnp.zeros((HD, QB), f32))

    def step(kb, carry, masked):
        keys = at_unit(kb, QB)
        k = k_rows[keys]
        result = []
        for h in range(2):
            top, total, out = carry[h]
            scores = dot(k, qm[h, :, cols], nn)
            if masked:
                scores = causal_mask(scores)
            high = jnp.maximum(top, jnp.max(scores, axis=0, keepdims=True))
            scale = jnp.exp(top - high)
            expo = jnp.exp(scores - high)
            total = total * scale + jnp.sum(expo, axis=0, keepdims=True)
            out = out * scale + dot(kv[pl.ds(128 + h * HD, HD), keys], expo.astype(bf16), nn)
            result.append((high, total, out))
        return tuple(result)

    carry = lax.fori_loop(0, qb, lambda kb, c: step(kb, c, False), (start, start))
    carry = step(qb, carry, True)
    for h in range(2):
        top, total, out = carry[h]
        inner[pl.ds(h * HD, HD), cols] = (out / total).astype(bf16)
        lse[pl.ds(h, 1), cols] = top + jnp.log(total)


def attend_back_block(kb, qm, kv, q_rows, k_rows, v_rows, dom, do_rows, lse, delta, dq, outer, table):
    keys = pl.ds(kb * QB, QB)

    def step(keys, cols, carry, masked, fresh=False):
        k, v = k_rows[keys], v_rows[keys]
        result = []
        for h in range(2):
            dk, dv = carry[h]
            scores = dot(k, qm[pl.ds(h * 128, 128), cols], nn)
            if masked:
                scores = causal_mask(scores)
            probs = jnp.exp(scores - lse[pl.ds(h, 1), cols])
            dp = dot(v, dom[h, :, cols], nn)
            ds = (probs * (dp - delta[pl.ds(h, 1), cols])).astype(bf16)
            dv = dv + dot(probs.astype(bf16), do_rows[cols], nn)
            dk = dk + dot(ds, q_rows[cols], nn)
            half = pl.ds(h * HD, HD)
            part = dot(kv[half, keys], ds, nn)
            if fresh:
                dq[half, cols] = part
            else:
                dq[half, cols] += part
            result.append((dk, dv))
        return tuple(result)

    small = QB // 2
    low, high = pl.ds(kb * QB, small), pl.ds(kb * QB + small, small)
    zero = jnp.zeros((small, 128), f32)
    start = ((zero, zero), (zero, zero))
    first = step(low, keys, start, True, kb == 0)
    second = step(high, high, start, True)
    carry = jax.tree.map(lambda a, b: jnp.concatenate([a, b], axis=0), first, second)
    carry = lax.fori_loop(
        kb + 1, LENGTH // QB, lambda qb, c: step(keys, at_unit(qb, QB), c, False, kb == 0), carry
    )
    (dk0, dv0), (dk1, dv1) = carry
    first = lax.broadcasted_iota(jnp.int32, (QB, 128), 1) < HD
    dk = jnp.where(first, dk0, dk1).astype(bf16).astype(f32).T
    dv = jnp.where(first, dv0, dv1).T
    cosine, sine = table[0:16, keys], -table[16:32, keys]
    outer[pl.ds(128, 128), keys] = turn(dk, cosine, sine).astype(bf16)
    outer[pl.ds(256, 128), keys] = dv.astype(bf16)


def query_back(dq, outer, table):
    part = (dq[...] * HD**-0.5).astype(bf16).astype(f32)
    outer[pl.ds(0, 128)] = turn(part, table[0:16], -table[16:32]).astype(bf16)


PLACES = [(0, 0), (-1, 0), (1, 0), (0, 1), (2, 0), (-1, 1), (1, 1), (2, 1)]


def slot(dy, dx):
    return dy % 4 + 4 * dx


def add_into(count, out, *refs):
    wide = f32 if len(refs) > 2 else out.dtype

    @pl.loop(0, count // 16)
    def _(i):
        part = pl.ds(pl.multiple_of(i * 16, 16), 16)
        total = refs[0][part].astype(wide)
        for ref in refs[1:]:
            total = total + ref[part].astype(wide)
        out[part] = total.astype(out.dtype)


GROUPS = (((0, 0),), ((-1, 0), (1, 0)), ((0, 1),), ((2, 0),), ((-1, 1), (1, 1)), ((2, 1),))

GRAD_GROUPS = tuple(((dy, 0), (dy, 1)) for dy in (0, 1, 2, -1))


def gather_order(s):
    return (
        s.st0, s.W0own, s.W0ownp, s.LN, s.Town1, s.W0np1, s.Townp, s.Town2, s.st1, s.W0np2, s.Tnl,
        s.W0fl, s.W0na, s.Tnr, s.Tnp1, s.Tsl, s.W0fr, s.st2, s.W1own, s.W1ownp, s.st3, s.Tfa, s.Tfb,
        s.Tnp2, s.W0end, s.st4, s.wg0, s.W1np1, s.q3, s.Tsr, s.q2, s.castG, s.Gown1, s.W1np2, s.q0,
        s.W1na, s.q1, s.Gown2, s.Te2, s.W1fl, s.W1fr, s.W2own, s.W2ownp, s.Te1, s.q4, s.Gownp, s.Gnr,
        s.W1end, s.wc, s.wg1, s.u3, s.Te3, s.Gnl, s.W2np1, s.u1, s.u0, s.W2np2, s.u2, s.W2na, s.q5,
        s.qc, s.at2, s.W2fr, s.Gnp1, s.Gfa, s.W2fl, s.clear, s.at1, s.Gsr, s.Gfb, s.at3, s.Gsl, s.at0,
        s.ic, s.W2end, s.Gnp2, s.b2, s.b0, s.b1, s.k0, s.sa0, s.Ge2, s.Ge1, s.b3, s.sa2, s.sa1, s.k1,
        s.Ge3, s.k3, s.sa3, s.k2,
    )


def gather_kernel(
    x_ref, ct_ref, aw_ref, ew_ref, cw_ref, norm_ref, table,
    raw_out, gb_out, w_out, gain_out, qm_out, kv_out, rows_out, inner_out, lse, branch_out,
    dom_out, do_rows_out, delta, dup_out,
    raw, gb, w, scaled, shift, own_w, sums, landed, qm, kv, rows, inner, slope, sibs, affine, ct, late, dom, do_rows, dup, send, recv, local,
):
    at = place()
    z, xh, y, xl, c = at
    stages = stage_peers(at)
    net, near = Net(send, recv), Local(local)
    met = greet([peer for stage in stages for peer in stage])
    q_rows, k_rows, v_rows = rows.at[0], rows.at[1], rows.at[2]
    kept, raw_copy, swaps = [], [], {}
    tokens = TokenGather(net, at, raw, False)
    grads = TokenGather(net, at, gb, False)
    own, own_g = tokens.rows(0, 0), grads.rows(0, 0)
    steps = tokens.steps("T", own) | grads.steps("G", own_g)
    loads = [near.go(ct_ref, ct)] + [near.go(ref, late.at[k]) for k, ref in enumerate((ew_ref, cw_ref))]
    blocks = ((aw_ref, None), (late.at[0], loads[1]), (late.at[1], loads[2]))
    for kind, (block, load) in enumerate(blocks):
        steps |= WeightGather(net, near, at, w, kind, own_w.at[kind], block, load).steps()

    def unit_of(dy, dx):
        return lax.rem(y + dy + 4, 4) * 2 + lax.rem(xl + dx, 2)

    def step(name, work, *args):
        steps[name] = functools.partial(work, *args)

    def norm_of():
        @pl.loop(0, ROWS // 16)
        def _(i):
            part = pl.ds(pl.multiple_of(i * 16, 16), 16)
            x = x_ref[part]
            centred = x - jnp.mean(x, axis=1, keepdims=True)
            inverse = lax.rsqrt(jnp.mean(centred * centred, axis=1, keepdims=True) + eps_norm)
            own[part] = (centred * inverse).astype(bf16)

    def cast_grad():
        loads[0].wait()

        @pl.loop(0, ROWS // 16)
        def _(i):
            part = pl.ds(pl.multiple_of(i * 16, 16), 16)
            own_g[part] = ct[part].astype(bf16)

    step("LN", norm_of)
    step("castG", cast_grad)
    staged = Staged(net, stages, sums, landed)

    def stage(k):
        if k > 0:
            staged.finish()
        if k < 4:
            staged.start()
        else:
            gain_out[...] = sums[4]
            gain, bias = spread(sums[4])
            affine[0:1] = gain
            affine[1:2] = bias

    for k in range(5):
        step(f"st{k}", stage, k)

    def tokens_in(k):
        for dy, dx in GROUPS[k]:
            tokens.wait(f"s{PLACES.index((dy, dx))}")
            qkv_unit(unit_of(dy, dx), raw, scaled, shift, table, qm, kv, q_rows, k_rows, v_rows)

    def up(k):
        tokens.wait(*(f"s{PLACES.index(pair)}" for pair in GRAD_GROUPS[k]))
        up_unit(lax.rem(y + k, 4), raw, scaled, shift, inner, slope)

    def copies():
        raw_copy.append(near.go(raw, raw_out))
        kept.extend([near.go(qm, qm_out), near.go(kv, kv_out), near.go(rows, rows_out)])

    def w_copy():
        kept.append(near.go(w.at[pl.ds(0, FIRST)], w_out))

    def inner_copy():
        kept.append(near.go(inner, inner_out))

    def clear():
        tokens.clear()
        raw_copy[0].wait()

    def branch(dy):
        branch_unit(lax.rem(y + dy, 4), inner, w, raw)
        for dx in range(2):
            rows = token_rows(y + dy, xl if dx == 0 else 1 - xl, 1 - c)
            swaps[dy, dx] = net.go(raw.at[rows], sibs.at[dy + 4 * dx], tokens.s)

    def branch_sum(dy):
        for dx in range(2):
            swaps[dy, dx].wait_recv()
            mine = raw.at[token_rows(y + dy, xl if dx == 0 else 1 - xl, c)]
            add_into(ROWS, mine, mine, sibs.at[dy + 4 * dx])
            kept.append(near.go(mine, branch_out.at[dy + 4 * dx]))

    def grads_in(k):
        grads.wait(*(f"s{PLACES.index(pair)}" for pair in GRAD_GROUPS[k]))
        part = at_unit(lax.rem(y + k, 4), 2 * UNIT)
        kept.append(near.go(gb.at[part], gb_out.at[part]))
        back_unit(part, gb, w, inner, slope, dom, do_rows, delta, dup)
        kept.append(near.go(dup.at[:, part], dup_out.at[:, part]))
        kept.append(near.go(do_rows.at[part], do_rows_out.at[part]))

    for k in range(6):
        step(f"q{k}", tokens_in, k)
    for k in range(4):
        step(f"k{k}", grads_in, k)
    step("wg0", scale_weights, 0, QKV, w, scaled, shift, affine)
    step("wg1", scale_weights, QKV, HIDDEN, w, scaled, shift, affine)
    for k in range(4):
        step(f"at{k}", attend_block, k, qm, kv, k_rows, inner, lse)
        step(f"u{k}", up, k)
        step(f"b{k}", branch, k)
        step(f"sa{k}", branch_sum, k)
    step("qc", copies)
    step("wc", w_copy)
    step("ic", inner_copy)
    step("clear", clear)

    rank = (z * 8 + xh * 4 + y) * 4 + xl * 2 + c
    wide = norm_ref[...]
    for _ in range(5):
        wide = jnp.concatenate([wide, wide], axis=1)
    rows_at = lax.broadcasted_iota(jnp.int32, (8, 512), 0)
    here = (lax.broadcasted_iota(jnp.int32, (8, 512), 1) // 16) == lax.rem(rank, 32)
    one = jnp.where(here & (rows_at == rank // 32), wide[0:1], 0.0)
    sums[0] = one + jnp.where(here & (rows_at == 4 + rank // 32), wide[1:2], 0.0)
    met()
    for work in gather_order(types.SimpleNamespace(**steps)):
        work()
    kept.append(near.go(dom, dom_out))
    grads.clear()
    net.drain()
    for copy in kept:
        copy.wait()


def gather(x, ct, aw, ew, cw, norm_rows, table):
    any_ref = pl.BlockSpec(memory_space=pl.ANY)
    vmem = pl.BlockSpec(memory_space=pltpu.VMEM)
    shape = jax.ShapeDtypeStruct
    outs = [
        (shape((LENGTH, D), bf16), any_ref),
        (shape((LENGTH, D), bf16), any_ref),
        (shape((FIRST, D), bf16), any_ref),
        (shape((8, 512), f32), vmem),
        (shape((2, 128, LENGTH), bf16), any_ref),
        (shape((256, LENGTH), bf16), any_ref),
        (shape((3, LENGTH, 128), bf16), any_ref),
        (shape((SECOND, LENGTH), bf16), any_ref),
        (shape((8, LENGTH), f32), vmem),
        (shape((8, ROWS, D), bf16), any_ref),
        (shape((2, 128, LENGTH), bf16), any_ref),
        (shape((LENGTH, 128), bf16), any_ref),
        (shape((8, LENGTH), f32), vmem),
        (shape((HIDDEN, LENGTH), bf16), any_ref),
    ]
    return pl.pallas_call(
        gather_kernel,
        name="gather",
        out_shape=[out for out, _ in outs],
        in_specs=[vmem, any_ref, vmem, any_ref, any_ref, vmem, vmem],
        out_specs=[spec for _, spec in outs],
        scratch_shapes=[
            pltpu.VMEM((LENGTH, D), bf16),
            pltpu.VMEM((LENGTH, D), bf16),
            pltpu.VMEM((WALL, D), bf16),
            pltpu.VMEM((FIRST, D), bf16),
            pltpu.VMEM((FIRST, 1), f32),
            pltpu.VMEM((KINDS, WROWS, D), bf16),
            pltpu.VMEM((5, 8, 512), f32),
            pltpu.VMEM((10, 8, 512), f32),
            pltpu.VMEM((2, 128, LENGTH), bf16),
            pltpu.VMEM((256, LENGTH), bf16),
            pltpu.VMEM((3, LENGTH, 128), bf16),
            pltpu.VMEM((SECOND, LENGTH), bf16),
            pltpu.VMEM((HIDDEN, LENGTH), f32),
            pltpu.VMEM((8, ROWS, D), bf16),
            pltpu.VMEM((8, D), f32),
            pltpu.VMEM((ROWS, D), f32),
            pltpu.VMEM((2, WROWS, D), f32),
            pltpu.VMEM((2, 128, LENGTH), bf16),
            pltpu.VMEM((LENGTH, 128), bf16),
            pltpu.VMEM((HIDDEN, LENGTH), bf16),
            pltpu.SemaphoreType.DMA((112,)),
            pltpu.SemaphoreType.DMA((112,)),
            pltpu.SemaphoreType.DMA((48,)),
        ],
        compiler_params=pltpu.CompilerParams(
            collective_id=1, has_side_effects=True, vmem_limit_bytes=60 << 20
        ),
    )(x, ct, aw, ew, cw, norm_rows, table)


class TokenScatter:
    def __init__(self, net, at, block, landed, out, around):
        self.around = around
        self.net, self.block, self.landed, self.out, self.got = net, block, landed, out, {}
        z, xh, y, xl, c = at
        self.x = device(z, xh, y, 1 - xl, c)
        self.p = device(z, xh, y + 1, xl, c)
        self.m = device(z, xh, y - 1, xl, c)

    def send(self, name, dy, dx, half, place, peer, *more):
        part = pl.ds(*((0, 64), (64, 64), (64, 32), (96, 32))[half])
        block, others = self.block(slot(dy, dx))
        terms = [ref.at[part] for ref in others] + [self.landed.at[k, part] for k in more]
        if terms:
            add_into(part.size, block.at[part], block.at[part], *terms)
        self.got[name] = self.net.go(block.at[part], self.landed.at[place, part], peer)

    def wait(self, *names):
        for name in names:
            self.got[name].wait_recv()

    def steps(self, tag):
        send, wait = self.send, self.wait

        def xo():
            send("xo1", 2, 1, 0, 0, self.x)
            if self.around:
                send("qa", 2, 1, 2, 7, self.m)
                send("qb", 2, 1, 3, 7, self.p)
            else:
                send("xo2", 2, 1, 1, 0, self.x)

        def quarter(name, dy, rows):
            if self.around:
                wait(name)
                block, _ = self.block(slot(dy, 1))
                part = pl.ds(rows, 32)
                add_into(32, block.at[part], block.at[part], self.landed.at[7, part])

        def lp():
            send("lp1", -1, 1, 0, 1, self.m)

        def lq():
            quarter("qa", -1, 64)
            send("lp2", -1, 1, 1, 1, self.m)

        def rp():
            send("rp1", 1, 1, 0, 2, self.p)

        def rq():
            quarter("qb", 1, 96)
            send("rp2", 1, 1, 1, 2, self.p)

        def oa():
            wait("xo1")
            send("a", 2, 0, 0, 3, self.m, 0)

        def ob():
            if self.around:
                send("b", 2, 0, 1, 3, self.p)
            else:
                wait("xo2")
                send("b", 2, 0, 1, 3, self.p, 0)

        def le():
            send("l2", -1, 0, 1, 4, self.m)

        def re():
            send("r1", 1, 0, 0, 5, self.p)

        def nl():
            wait("a")
            send("l1", -1, 0, 0, 4, self.m, 3)

        def nr():
            wait("b")
            send("r2", 1, 0, 1, 5, self.p, 3)

        def p1():
            wait("lp1", "rp1")
            send("p1", 0, 1, 0, 6, self.x, 1, 2)

        def p2():
            wait("lp2", "rp2")
            send("p2", 0, 1, 1, 6, self.x, 1, 2)

        def fi():
            wait("l1", "l2", "r1", "r2", "p1", "p2")
            block, others = self.block(slot(0, 0))
            add_into(ROWS, self.out, block, *others, *(self.landed.at[k] for k in (4, 5, 6)))

        parts = (xo, lp, rp, lq, rq, oa, ob, le, re, nl, nr, p1, p2, fi)
        return {tag + part.__name__: part for part in parts}


class WeightScatter:
    def __init__(self, net, at, part, kind, landed, out, tag, cols):
        self.net, self.at, self.part, self.kind = net, at, part, kind
        self.tag, self.cols = tag, cols
        self.landed, self.out = landed.at[:, :, cols], out.at[:, cols]
        z, xh, y, xl, c = at
        self.h = device(z, 1 - xh, y, xl, c)
        self.p = device(z + 1, xh, y, xl, c)
        self.m = device(z - 1, xh, y, xl, c)
        self.got = {}

    def rows(self, dz, dh, half=None):
        z, xh = self.at[:2]
        start, size = (0, WROWS) if half is None else (half * 32, 32)
        return self.part.at[
            weight_rows(self.kind, z + dz, xh if dh == 0 else 1 - xh, start, size), self.cols
        ]

    def send(self, src, place, peer, half=None):
        start, size = (0, WROWS) if half is None else (half * 32, 32)
        return self.net.go(src, self.landed.at[place, pl.ds(start, size)], peer)

    def steps(self):
        got = self.got

        def op():
            for dh in (1, 0):
                got["a", dh] = self.send(self.rows(2, dh, 0), dh, self.m, 0)
                got["b", dh] = self.send(self.rows(2, dh, 1), dh, self.p, 1)

        def left(dh):
            got["a", dh].wait_recv()
            half = self.rows(-1, dh, 0)
            add_into(32, half, half, self.landed.at[dh, pl.ds(0, 32)])
            got["l", dh] = self.send(self.rows(-1, dh), 2 + dh, self.m)

        def right(dh):
            got["b", dh].wait_recv()
            half = self.rows(1, dh, 1)
            add_into(32, half, half, self.landed.at[dh, pl.ds(32, 32)])
            got["r", dh] = self.send(self.rows(1, dh), 4 + dh, self.p)

        def pa():
            got["l", 1].wait_recv()
            got["r", 1].wait_recv()
            other = self.rows(0, 1)
            add_into(WROWS, other, other, self.landed.at[3], self.landed.at[5])
            got["p"] = self.send(other, 6, self.h)

        def fi():
            for name in (("l", 0), ("r", 0), "p"):
                got[name].wait_recv()
            add_into(
                WROWS, self.out, self.rows(0, 0),
                self.landed.at[2], self.landed.at[4], self.landed.at[6],
            )

        tag = self.tag
        return {
            tag + "op": op,
            tag + "l1": lambda: left(1),
            tag + "l0": lambda: left(0),
            tag + "r1": lambda: right(1),
            tag + "r0": lambda: right(0),
            tag + "pa": pa,
            tag + "fi": fi,
        }


TILE = 512
TILES = D // TILE


def factors_of(moments):
    eye = lax.broadcasted_iota(jnp.int32, (HD, HD), 0) == lax.broadcasted_iota(jnp.int32, (HD, HD), 1)
    one = jnp.where(eye, 1.0, 0.0)

    def each(work, *lists):
        return [work(*items) for items in zip(*lists)]

    def gram_of(moment):
        both = jnp.concatenate(split(moment), axis=0)
        gram = dot(both, both, nt)
        return gram[:HD, :HD] + gram[HD:, HD:] + (gram[:HD, HD:] + gram[HD:, :HD])

    def size_of(gram):
        size = jnp.sum(jnp.where(eye, gram, 0.0), axis=1, keepdims=True)
        return jnp.sqrt(jnp.sum(size, axis=0, keepdims=True)) + 1e-07

    grams = each(gram_of, moments)
    sizes = each(size_of, grams)
    grams = each(lambda gram, size: gram / size / size, grams, sizes)
    wholes = None
    for turn_at in range(NS_STEPS):
        squares = each(times, grams, grams)
        steps = each(lambda a, b: polish_a * one + polish_b * a + polish_c * b, grams, squares)
        wholes = steps if turn_at == 0 else each(times, steps, wholes)
        if turn_at < NS_STEPS - 1:
            grams = each(times, steps, each(times, grams, steps))
    return each(lambda whole, size: whole / size, wholes, sizes)


def scatter_order(s):
    return (
        s.Rxo, s.Rre, s.Rle, s.sec0, s.Rlp, s.sec1, s.W2op, s.Rlq, s.Rrp, s.E0, s.Rrq, s.V1op, s.bk0,
        s.Rp1, s.Roa, s.W2r1, s.V1l1, s.Rob, s.W2l1, s.bk1, s.V1r0, s.bk2, s.V1r1, s.bk3, s.Rnl, s.qb,
        s.Rnr, s.W2l0, s.W2r0, s.Rp2, s.gB, s.gA, s.Dxo, s.E1, s.U1op, s.W2pa, s.Drp, s.Dlp, s.qk0,
        s.U1l1, s.U1r1, s.qk1, s.st0, s.W0op, s.Dob, s.Dlq, s.V1pa, s.gD, s.W0l1, s.U1pa, s.V1l0,
        s.st1, s.Doa, s.Drq, s.U1l0, s.Dp1, s.W0r1, s.gC, s.Dre, s.Dle, s.st2, s.U1r0, s.W0l0, s.Dnl,
        s.W0pa, s.st3, s.W0r0, s.V1fi, s.Dp2, s.Dnr, s.W2fi, s.U1fi, s.Rfi, s.f12, s.st4, s.W0fi, s.f0,
        s.Dfi,
    )


def scatter_kernel(
    raw_ref, gb_ref, w_ref, branch_ref, qm_ref, kv_ref, rows_ref, inner_ref, dom_ref, do_rows_ref, dup_ref,
    am_ref, em_ref, cm_ref, lse, delta, gain_ref, table,
    branch_res, dnormed_out, wgrad_res, factor_out, norm_out,
    branch_out, wgrad_out, mine, part, sibs, landed, wpart, wlanded, w, early, outer, tiles, rows, dom, do_rows, dq, moments,
    affine, norm_part, sums, nlanded, send, recv, local, tile_sems,
):
    at = place()
    z, xh, y, xl, c = at
    net, near = Net(send, recv), Local(local)
    stages = stage_peers(at)
    sib = device(z, xh, y, xl, 1 - c)
    steps, swaps = {}, {}
    met = greet([peer for stage in stages for peer in stage])

    def step(name, work, *args):
        steps[name] = functools.partial(work, *args)

    def fetch(n):
        src = gb_ref if n < TILES else raw_ref
        cols = pl.ds(n % TILES * TILE, TILE)
        return pltpu.make_async_copy(src.at[:, cols], tiles.at[n % 2], tile_sems.at[n % 2])

    fetch(0).start()
    inner_load = near.go(inner_ref, early)
    branch_slots = {slot(dy, dx): k for k, (dy, dx) in enumerate(PLACES[:5])}
    branch_loads = {s: near.go(branch_ref.at[s], mine.at[k]) for s, k in branch_slots.items()}
    first_loads = [near.go(dup_ref, outer.at[pl.ds(QKV, HIDDEN)]), near.go(w_ref, w)]
    attn_loads = [near.go(rows_ref, rows), near.go(dom_ref, dom), near.go(do_rows_ref, do_rows)]
    moment_loads = [near.go(ref, moments.at[k]) for k, ref in enumerate((am_ref, em_ref, cm_ref))]

    def branch_block(s):
        if s not in branch_slots:
            return branch_ref.at[s], []
        load = branch_loads.pop(s, None)
        if load is not None:
            load.wait()
        return mine.at[branch_slots[s]], []

    def dnormed_block(s):
        swap = swaps.pop(s, None)
        if swap is not None:
            swap.wait_recv()
        return part.at[c, s], [sibs.at[s]]

    def factors(*kinds):
        for kind in kinds:
            moment_loads[kind].wait()
        found = factors_of([muon_beta * moments[kind] + wgrad_out[kind] for kind in kinds])
        for kind, factor in zip(kinds, found):
            factor_out[kind] = factor

    step("f12", factors, 1, 2)
    step("f0", factors, 0)
    kept = []

    def keep(name, src, dst):
        work = steps[name]

        def then():
            work()
            kept.append(near.go(src, dst))

        steps[name] = then

    steps |= TokenScatter(net, at, branch_block, landed.at[0], branch_out, False).steps("R")
    steps |= TokenScatter(net, at, dnormed_block, landed.at[1], dnormed_out, True).steps("D")
    half = D // 2
    for tag, kind, start, size in (("W0", 0, 0, D), ("V1", 1, 0, half), ("U1", 1, half, half), ("W2", 2, 0, D)):
        cols = pl.ds(start, size)
        steps |= WeightScatter(
            net, at, wpart, kind, wlanded.at[kind], wgrad_out.at[kind], tag, cols
        ).steps()
        keep(tag + "fi", wgrad_out.at[kind, :, cols], wgrad_res.at[kind, :, cols])
    keep("Rfi", branch_out, branch_res)

    def tile_in(n):
        if n + 1 < 3 * TILES:
            fetch(n + 1).start()
        fetch(n).wait()
        return pl.ds(n % TILES * TILE, TILE), tiles.at[n % 2]

    def second_pass(half):
        if half == 0:
            inner_load.wait()
        for n in range(half * TILES // 2, (half + 1) * TILES // 2):
            cols, tile = tile_in(n)
            wpart[pl.ds(FIRST, SECOND), cols] = dot(early[...], tile[...], nn).astype(bf16)
        if half == 1:
            attn_loads.extend(
                [near.go(qm_ref.at[h], early.at[pl.ds(h * 128, 128)]) for h in range(2)]
            )
            attn_loads.append(near.go(kv_ref, early.at[pl.ds(256, 256)]))

    def first_pass(start, size, base, half):
        if base == TILES and half == 0:
            for load in first_loads:
                load.wait()
        span = pl.ds(start, size)
        total = dot(outer[span], jnp.ones((LENGTH, 128), bf16), nn)[:, :1]
        for n in range(base + half * TILES // 2, base + (half + 1) * TILES // 2):
            cols, tile = tile_in(n)
            summed = dot(outer[span], tile[...], nn)
            wpart[span, cols] = (summed * affine[0:1, cols] + total * affine[1:2, cols]).astype(bf16)
            block = w[span, cols].astype(f32)
            by_gain = jnp.sum(block * summed, axis=0, keepdims=True)
            by_bias = jnp.sum(block * total, axis=0, keepdims=True)
            if base == TILES:
                norm_part[0:1, cols] = by_gain
                norm_part[1:2, cols] = by_bias
            else:
                norm_part[0:1, cols] += by_gain
                norm_part[1:2, cols] += by_bias

    for half in range(2):
        step(f"sec{half}", second_pass, half)
        step(f"E{half}", first_pass, QKV, HIDDEN, TILES, half)
        step(f"qk{half}", first_pass, 0, QKV, 2 * TILES, half)

    def back(kb):
        if kb == 0:
            for load in attn_loads:
                load.wait()
        attend_back_block(
            kb, early.at[pl.ds(0, 256)], early.at[pl.ds(256, 256)], rows.at[0], rows.at[1], rows.at[2],
            dom, do_rows, lse, delta, dq, outer, table,
        )

    for kb in range(LENGTH // QB):
        step(f"bk{kb}", back, kb)
    step("qb", query_back, dq, outer, table)

    def dnormed_unit(dy, dx):
        unit = lax.rem(y + dy, 4) * 2 + lax.rem(xl + dx, 2)
        block = dot(outer[:, at_unit(unit)], w[...], tn).astype(bf16)
        s = dy + 4 * dx
        part[0, s] = block[:ROWS]
        part[1, s] = block[ROWS:]

    def swap(dy, dx):
        s = slot(dy, dx)
        swaps[s] = net.go(part.at[1 - c, s], sibs.at[s], sib)

    def dnormed_of(*pairs):
        (dy, dx), (sy, sx) = pairs

        @pl.loop(0, 2)
        def _(i):
            dnormed_unit(dy % 4 + (sy % 4 - dy % 4) * i, dx + (sx - dx) * i)

        for pair in pairs:
            swap(*pair)

    step("gA", dnormed_of, (1, 1), (-1, 1))
    step("gB", dnormed_of, (2, 1), (2, 0))
    step("gC", dnormed_of, (1, 0), (-1, 0))
    step("gD", dnormed_of, (0, 1), (0, 0))
    staged = Staged(net, stages, sums, nlanded)

    def stage(k):
        if k == 0:
            for kind in range(2):
                for q in range(4):
                    sums[0, pl.ds(kind * 4 + q, 1)] = norm_part[pl.ds(kind, 1), pl.ds(q * 512, 512)]
        else:
            staged.finish()
        if k < 4:
            staged.start()
        else:
            norm_out[...] = sums[4]

    for k in range(5):
        step(f"st{k}", stage, k)

    gain, bias = spread(gain_ref[...])
    affine[0:1] = gain
    affine[1:2] = bias
    met()
    for work in scatter_order(types.SimpleNamespace(**steps)):
        work()
    net.drain()
    for copy in kept:
        copy.wait()


def scatter(*args):
    any_ref = pl.BlockSpec(memory_space=pl.ANY)
    vmem = pl.BlockSpec(memory_space=pltpu.VMEM)
    return pl.pallas_call(
        scatter_kernel,
        name="scatter",
        out_shape=(
            jax.ShapeDtypeStruct((ROWS, D), f32),
            jax.ShapeDtypeStruct((ROWS, D), f32),
            jax.ShapeDtypeStruct((KINDS, WROWS, D), f32),
            jax.ShapeDtypeStruct((KINDS, HD, HD), f32),
            jax.ShapeDtypeStruct((8, 512), f32),
        ),
        in_specs=[any_ref] * 14 + [vmem] * 4,
        out_specs=(any_ref, vmem, any_ref, vmem, vmem),
        scratch_shapes=[
            pltpu.VMEM((ROWS, D), f32),
            pltpu.VMEM((KINDS, WROWS, D), f32),
            pltpu.VMEM((5, ROWS, D), bf16),
            pltpu.VMEM((2, 8, ROWS, D), bf16),
            pltpu.VMEM((8, ROWS, D), bf16),
            pltpu.VMEM((2, 8, ROWS, D), bf16),
            pltpu.VMEM((WALL, D), bf16),
            pltpu.VMEM((KINDS, 7, WROWS, D), bf16),
            pltpu.VMEM((FIRST, D), bf16),
            pltpu.VMEM((SECOND, LENGTH), bf16),
            pltpu.VMEM((FIRST, LENGTH), bf16),
            pltpu.VMEM((2, LENGTH, TILE), bf16),
            pltpu.VMEM((3, LENGTH, 128), bf16),
            pltpu.VMEM((2, 128, LENGTH), bf16),
            pltpu.VMEM((LENGTH, 128), bf16),
            pltpu.VMEM((128, LENGTH), f32),
            pltpu.VMEM((KINDS, WROWS, D), f32),
            pltpu.VMEM((8, D), f32),
            pltpu.VMEM((8, D), f32),
            pltpu.VMEM((5, 8, 512), f32),
            pltpu.VMEM((10, 8, 512), f32),
            pltpu.SemaphoreType.DMA((112,)),
            pltpu.SemaphoreType.DMA((112,)),
            pltpu.SemaphoreType.DMA((32,)),
            pltpu.SemaphoreType.DMA((2,)),
        ],
        compiler_params=pltpu.CompilerParams(
            collective_id=2, has_side_effects=True, vmem_limit_bytes=63 << 20
        ),
    )(*args)


def update_kernel(
    x_ref, ct_ref, branch_ref, dnormed_ref, gain_ref, share_ref, factor_ref,
    aw, ew, cw, am, em, cm, norm_ref, params, first, second,
    state_out, grad_out, ag, an, aweight, eg, en, eweight, cg, cn, cweight,
    norm_out, first_out, second_out, params_out,
):
    @pl.when(pl.program_id(0) == 0)
    def _():
        z, xh, y, xl, c = place()
        rank = (z * 8 + xh * 4 + y) * 4 + xl * 2 + c
        for kind in range(2):
            row = norm_ref[pl.ds(kind * 4 + rank // 32, 1)]
            row = pltpu.roll(row, lax.rem(512 - 16 * lax.rem(rank, 32), 512), 1)
            norm_out[pl.ds(kind, 1)] = row[:, :16]
        share = norm_out[...]
        first_next = adam_first * first[...] + (1.0 - adam_first) * share
        second_next = adam_second * second[...] + (1.0 - adam_second) * share * share
        first_out[...] = first_next
        second_out[...] = second_next
        first_fix = 1.0 - adam_first**STEP
        second_fix = 1.0 - adam_second**STEP
        params_out[...] = params[...] - adam_rate * (first_next / first_fix) / (
            jnp.sqrt(second_next / second_fix) + adam_eps
        )

    x, dnormed = x_ref[...], dnormed_ref[...]
    state_out[...] = x + branch_ref[...]
    centred = x - jnp.mean(x, axis=1, keepdims=True)
    inverse = lax.rsqrt(jnp.mean(centred * centred, axis=1, keepdims=True) + eps_norm)
    xhat = centred * inverse
    scaled = dnormed * spread(gain_ref[...])[0]
    grad_out[...] = ct_ref[...] + inverse * (
        scaled
        - jnp.mean(scaled, axis=1, keepdims=True)
        - xhat * jnp.mean(scaled * xhat, axis=1, keepdims=True)
    )
    kinds = ((aw, am, ag, an, aweight), (ew, em, eg, en, eweight), (cw, cm, cg, cn, cweight))
    for k, (weight, moment, grad, moment_next, weight_next) in enumerate(kinds):
        share = share_ref[k]
        grad[...] = share
        following = muon_beta * moment[...] + share
        moment_next[...] = following
        ortho = times(factor_ref[k], following)
        old = weight[...]
        weight_next[...] = old - muon_rate * (muon_decay * old + 0.2 * math.sqrt(D) * ortho)


def update(x, ct, branch, dnormed, gain_rows, shares, factors, *others):
    steps = 2
    token = pl.BlockSpec((ROWS // steps, D), lambda i: (i, 0))
    block = pl.BlockSpec((WROWS, D // steps), lambda i: (0, i))
    norm = pl.BlockSpec((2, 16), lambda i: (0, 0))
    shape = jax.ShapeDtypeStruct
    return pl.pallas_call(
        update_kernel,
        name="update",
        grid=(steps,),
        out_shape=[shape((ROWS, D), f32)] * 2 + [shape((WROWS, D), f32)] * 9 + [shape((2, 16), f32)] * 4,
        in_specs=[token] * 4
        + [
            pl.BlockSpec((8, 512), lambda i: (0, 0)),
            pl.BlockSpec((KINDS, WROWS, D // steps), lambda i: (0, 0, i)),
            pl.BlockSpec((KINDS, HD, HD), lambda i: (0, 0, 0)),
        ]
        + [block] * 6
        + [pl.BlockSpec((8, 512), lambda i: (0, 0))]
        + [norm] * 3,
        out_specs=[token] * 2 + [block] * 9 + [norm] * 4,
        compiler_params=pltpu.CompilerParams(vmem_limit_bytes=60 << 20),
    )(x, ct, branch, dnormed, gain_rows, shares, factors, *others)


def angles():
    half = ROT // 2
    freq = rope_base ** (-2.0 * np.arange(half) / ROT)
    turned = freq[:, None] * np.arange(LENGTH)[None, :]
    return jnp.asarray(np.concatenate([np.cos(turned), np.sin(turned)]).astype(np.float32))


def body(
    inputs, cotangent, attn_weight, expand_weight, contract_weight, norm_params,
    attn_moment, expand_moment, contract_moment, norm_first, norm_second,
):
    table = angles()
    (
        raw, grad_group, first_w, norm_rows, qm, kv, rows, inner, lse, branch,
        dom, do_rows, delta, dup,
    ) = gather(
        inputs,
        cotangent,
        attn_weight[0, 0],
        expand_weight[0],
        contract_weight[0],
        norm_params[0],
        table,
    )
    blocks = (attn_weight[0, 0], expand_weight[0], contract_weight[0])
    moments = (attn_moment[0, 0], expand_moment[0], contract_moment[0])
    branch, dnormed, shares, factors, norm_total = scatter(
        raw, grad_group, first_w, branch, qm, kv, rows, inner, dom, do_rows, dup,
        *moments, lse, delta, norm_rows, table,
    )
    state, grad_state, *updates = update(
        inputs, cotangent, branch, dnormed, norm_rows, shares, factors, *blocks, *moments,
        norm_total, norm_params[0], norm_first[0], norm_second[0],
    )
    shapes = [attn_weight.shape] * 3 + [expand_weight.shape] * 6 + [norm_params.shape] * 4
    return state, grad_state, *(part.reshape(shape) for part, shape in zip(updates, shapes))


def solution(mesh):
    return jax.shard_map(
        body,
        mesh=mesh,
        in_specs=(
            P(("fsdp", "seq", "mp"), None),
            P(("fsdp", "seq", "mp"), None),
            P(None, ("fsdp", "seq", "mp"), None, None),
            P(None, ("fsdp", "seq", "mp"), None),
            P(None, ("fsdp", "seq", "mp"), None),
            P(None, None, ("fsdp", "seq", "mp")),
            P(None, ("fsdp", "seq", "mp"), None, None),
            P(None, ("fsdp", "seq", "mp"), None),
            P(None, ("fsdp", "seq", "mp"), None),
            P(None, None, ("fsdp", "seq", "mp")),
            P(None, None, ("fsdp", "seq", "mp")),
        ),
        out_specs=(
            P(("fsdp", "seq", "mp"), None),
            P(("fsdp", "seq", "mp"), None),
            P(None, ("fsdp", "seq", "mp"), None, None),
            P(None, ("fsdp", "seq", "mp"), None, None),
            P(None, ("fsdp", "seq", "mp"), None, None),
            P(None, ("fsdp", "seq", "mp"), None),
            P(None, ("fsdp", "seq", "mp"), None),
            P(None, ("fsdp", "seq", "mp"), None),
            P(None, ("fsdp", "seq", "mp"), None),
            P(None, ("fsdp", "seq", "mp"), None),
            P(None, ("fsdp", "seq", "mp"), None),
            P(None, None, ("fsdp", "seq", "mp")),
            P(None, None, ("fsdp", "seq", "mp")),
            P(None, None, ("fsdp", "seq", "mp")),
            P(None, None, ("fsdp", "seq", "mp")),
        ),
        check_vma=False,
    )
```
